128 devices in a mesh: aux: 16 (over y, z_hi, core), row: 8 (over x, z_lo).
Axes of the slice: x: 4, y: 4, z: 4 (z_hi: 2, z_lo: 2; z = z_hi * 2 + z_lo), core: 2. Of those that a mesh axis runs over, the one named last changes fastest.
Arguments:
- factors: bfloat16 [16, 768, 128, 128], P('aux', 'row'), may hold values from -0.15625 to 0.15625
- block_rows: int32 [16, 768], P('aux', 'row'), may hold values from 0 to 47, as said below
- block_cols: int32 [16, 768], P('aux', 'row'), may hold values from 0 to 47
- block_count: int32 [16, 8], P('aux', 'row'), may hold values from 24 to 96, as said below
- orbitals: bfloat16 [6144, 800], P(('aux', 'row')), may hold values from -6 to 6
- response: bfloat16 [6144, 800], P(('aux', 'row')), may hold values from -6 to 6
Outputs:
- response_fock: float32 [6144, 800], P('row')
The draws below stay inside these ranges and needn't reach their ends.
Inputs may be any that keep to these rules, and one draw needn't show every extreme that they name: `block_rows`: slot s names a row shell block of its row group, from (s // 96) * 6 up to the next group's first; no (row block, column block) pair repeats within the 96 slots of one auxiliary function and row group. `block_count`: some auxiliary function and row group has all 96 slots live.
All inputs are finite; a program needn't handle non-finite values.
Results may differ from the reference program's by a relative error of at most 0.004.
Values may be sent and summed in bfloat16 or wider, within the bound.
No kernel may reach another device: no remote copies, remote signals or barrier semaphores. Data moves between devices by JAX's collectives and lax.ppermute only.
A program may use at most 128 MiB of HBM per device.

```python
import jax
import jax.numpy as jnp
from jax import lax

NB = 6144
NOCC = 800
BLK = 128
SLOTS = 96
AUX = 16
ROW_GROUPS = 8
ROW_SLOTS = 768


def screening_lists(key):
    key = jax.random.fold_in(key, 11)
    group_blocks = NB // (BLK * ROW_GROUPS)
    column_blocks = NB // BLK
    keys = jax.random.split(key, AUX * ROW_GROUPS)

    def pick_slots(subkey):
        return jax.random.permutation(subkey, group_blocks * column_blocks)[:SLOTS]
    chosen = jax.vmap(pick_slots)(keys).astype(jnp.int32).reshape(AUX, ROW_GROUPS, SLOTS)
    group_ids = jnp.arange(ROW_GROUPS, dtype=jnp.int32)[None, :, None]
    row_ids = group_ids * group_blocks + chosen // column_blocks
    column_ids = chosen % column_blocks
    return (row_ids.reshape(AUX, ROW_GROUPS * SLOTS), column_ids.reshape(AUX, ROW_GROUPS * SLOTS))


def draw_block_rows(key, part):
    row_ids, column_ids = screening_lists(key)
    return row_ids.astype(jnp.int32)


def draw_block_cols(key, part):
    row_ids, column_ids = screening_lists(key)
    return column_ids.astype(jnp.int32)


def draw_block_count(key, part):
    key = jax.random.fold_in(key, 3)
    first, second = jax.random.split(key)
    counts = jax.random.randint(first, (AUX * ROW_GROUPS,), SLOTS // 4, SLOTS + 1)
    fullest = jax.random.randint(second, (), 0, AUX * ROW_GROUPS)
    counts = jnp.where(jnp.arange(AUX * ROW_GROUPS) == fullest, SLOTS, counts)
    return counts.reshape(AUX, ROW_GROUPS).astype(jnp.int32)


def block_levels(rng, dims, cuts, least, top_value):
    def one(axis_at, parts):
        draws = jax.random.uniform(jax.random.fold_in(jax.random.fold_in(rng, 6), axis_at), (parts,), jnp.float32, least / len(cuts), top_value / len(cuts))
        return jnp.repeat(jnp.exp(draws), dims[axis_at] // parts).reshape((-1,) + (1,) * (len(dims) - axis_at - 1))

    loudness = one(*cuts[0])
    for cut in cuts[1:]:
        loudness = loudness * one(*cut)
    return loudness


def gaussian(own_key, shape, scale, most, cuts=(), kind=jnp.bfloat16):
    level = block_levels(own_key, shape, cuts, -0.22, 0.18) if cuts else 1.0
    values = jax.random.normal(own_key, shape, jnp.float32) * scale * level
    return jnp.minimum(jnp.maximum(values, -most), most).astype(kind)


def setup_inputs(seed: int = 0) -> dict:
    splits = jax.random.split(jax.random.key(seed), 7)
    return {
        "factors": gaussian(splits[0], (AUX, ROW_SLOTS, BLK, BLK), (NB // 4) ** -0.5, 0.15625, ((0, 16), (1, 8))),
        "block_rows": draw_block_rows(jax.random.fold_in(splits[6], 71), 0),
        "block_cols": draw_block_cols(jax.random.fold_in(splits[6], 71), 0),
        "block_count": draw_block_count(jax.random.fold_in(splits[6], 71), 0),
        "orbitals": gaussian(splits[4], (NB, NOCC), 1.0, 6.0, ((0, 128),)),
        "response": gaussian(splits[5], (NB, NOCC), 1.0, 6.0, ((0, 128),)),
    }


def reference(factors, block_rows, block_cols, block_count, orbitals, response):
    combined = jnp.concatenate([orbitals, response], axis=1)
    panels = combined.reshape(NB // BLK, BLK, 2 * NOCC)

    def one_group(accumulated, group):
        blocks, row_ids, column_ids, live_count = group
        pieces = panels[column_ids]
        products = jnp.einsum("smn,snk->smk", blocks.astype(jnp.float32), pieces.astype(jnp.float32))
        live = (jnp.arange(SLOTS, dtype=jnp.int32) < live_count).astype(jnp.float32)
        products = products * live[:, None, None]
        summed = jax.ops.segment_sum(products, row_ids, num_segments=NB // BLK)
        return accumulated + summed, None

    def one_aux(total, inputs):
        blocks, row_ids, column_ids, counts = inputs
        start = jnp.zeros((NB // BLK, BLK, 2 * NOCC), jnp.float32)
        accumulated, _ = lax.scan(
            one_group,
            start,
            (
                blocks.reshape(ROW_GROUPS, SLOTS, BLK, BLK),
                row_ids.reshape(ROW_GROUPS, SLOTS),
                column_ids.reshape(ROW_GROUPS, SLOTS),
                counts,
            ),
        )
        half = accumulated.reshape(NB, 2 * NOCC).astype(jnp.bfloat16)
        half_orbital = half[:, :NOCC]
        half_response = half[:, NOCC:]
        cross_x = (jnp.dot(half_orbital.T, orbitals, preferred_element_type=jnp.float32) / NB).astype(jnp.bfloat16)
        cross_y = (jnp.dot(half_response.T, orbitals, preferred_element_type=jnp.float32) / NB).astype(jnp.bfloat16)
        coulomb = jnp.sum(
            half_orbital.astype(jnp.float32) * response.astype(jnp.float32)
            + half_response.astype(jnp.float32) * orbitals.astype(jnp.float32)
        ) / NB
        exchange = jnp.dot(half_orbital, cross_y, preferred_element_type=jnp.float32)
        exchange = exchange + jnp.dot(half_response, cross_x, preferred_element_type=jnp.float32)
        contribution = 2.0 * coulomb * half_orbital.astype(jnp.float32) - exchange
        return total + contribution, None

    total, _ = lax.scan(
        one_aux,
        jnp.zeros((NB, NOCC), jnp.float32),
        (factors, block_rows, block_cols, block_count),
    )
    return total
```

```python
import functools
import itertools

import jax
import jax.numpy as jnp
from jax import lax
from jax.experimental import pallas as pl
from jax.experimental.pallas import tpu as pltpu
from jax.sharding import PartitionSpec as P

Y, ZH, CORE, X, ZL = 4, 2, 2, 4, 2
AXES = ("aux", "row")
BLK = 128
ROW_BLOCKS = 6
SLOTS = 96
NOCC = 800
WIDE = 896
CROSS = 832
SHARD = CROSS // 8
STEP = 4
PIECES = ((0, 256, "xyz"), (256, 512, "yzx"), (512, 896, "zxy"))


def permutation(move):
    pairs = []
    for y, zh, c, x, zl in itertools.product(range(Y), range(ZH), range(CORE), range(X), range(ZL)):
        at = dict(y=y, z=zh * ZL + zl, c=c, x=x)
        to = move(dict(at))

        def flat(d):
            return (((d["y"] * ZH + d["z"] // ZL) * CORE + d["c"]) * X + d["x"]) * ZL + d["z"] % ZL

        pairs.append((flat(at), flat(to)))
    return pairs


def around(axis, by):
    def move(d):
        d[axis] = (d[axis] + (by if d["c"] == 0 else -by)) % 4
        return d

    return permutation(move)


def other_core(d):
    d["c"] = 1 - d["c"]
    return d


def other_low(d):
    d["z"] = d["z"] ^ 1
    return d


def other_high(d):
    d["z"] = d["z"] ^ 2
    return d


def send(array, pairs):
    return lax.ppermute(array, AXES, pairs)


def swap_cores(array):
    return send(array, permutation(other_core))


def swap_low(array):
    return send(array, permutation(other_low))


def swap_high(array):
    return send(array, permutation(other_high))


def multiply_kernel(meta, own_blocks, other_blocks, panels, out, blocks, held, total, order, counts, sems):
    copies = [
        pltpu.make_async_copy(own_blocks, blocks.at[pl.ds(0, SLOTS)], sems.at[0]),
        pltpu.make_async_copy(other_blocks, blocks.at[pl.ds(SLOTS, SLOTS)], sems.at[1]),
        pltpu.make_async_copy(panels, held, sems.at[2]),
    ]
    for copy in copies:
        copy.start()
    blocks[2 * SLOTS] = jnp.zeros((BLK, BLK), jnp.bfloat16)

    def clear(i, carry):
        counts[i] = 0
        return carry

    lax.fori_loop(0, 2 * ROW_BLOCKS, clear, 0)
    for q in range(2):

        def place(s, carry):
            group = q * ROW_BLOCKS + meta[q, s]
            n = counts[group]
            order[group, n] = s + q * SLOTS
            counts[group] = n + 1
            return carry

        lax.fori_loop(0, meta[q, 2 * SLOTS], place, 0)

    def fill(group, carry):
        for i in range(STEP):
            order[group, counts[group] + i] = 2 * SLOTS
        return carry

    lax.fori_loop(0, 2 * ROW_BLOCKS, fill, 0)
    for copy in copies:
        copy.wait()

    def one_group(group, carry):
        q = group // ROW_BLOCKS
        total[...] = jnp.zeros_like(total)

        def step(i, carry):
            left, right = [], []
            for k in range(STEP):
                s = order[group, i * STEP + k]
                q_s = jnp.minimum(s // SLOTS, 1)
                column = jnp.where(s < 2 * SLOTS, meta[q_s, SLOTS + s - q_s * SLOTS], 0)
                left.append(blocks[s])
                right.append(held[pl.ds(pl.multiple_of(column * BLK, BLK), BLK), :])
            total[...] += jnp.dot(
                jnp.concatenate(left, axis=1),
                jnp.concatenate(right, axis=0),
                preferred_element_type=jnp.float32,
            )
            return carry

        lax.fori_loop(0, (counts[group] + STEP - 1) // STEP, step, 0)
        out[q, pl.ds(pl.multiple_of((group - q * ROW_BLOCKS) * BLK, BLK), BLK), :] = total[...].astype(
            jnp.bfloat16
        )
        return carry

    lax.fori_loop(0, 2 * ROW_BLOCKS, one_group, 0)


def multiply(meta, own_blocks, other_blocks, panels):
    return pl.pallas_call(
        multiply_kernel,
        out_shape=jax.ShapeDtypeStruct((2, ROW_BLOCKS * BLK, WIDE), jnp.bfloat16),
        in_specs=[
            pl.BlockSpec(memory_space=pltpu.SMEM),
            pl.BlockSpec(memory_space=pl.ANY),
            pl.BlockSpec(memory_space=pl.ANY),
            pl.BlockSpec(memory_space=pl.ANY),
        ],
        out_specs=pl.BlockSpec(memory_space=pltpu.VMEM),
        scratch_shapes=[
            pltpu.VMEM((2 * SLOTS + 1, BLK, BLK), jnp.bfloat16),
            pltpu.VMEM(panels.shape, jnp.bfloat16),
            pltpu.VMEM((BLK, WIDE), jnp.float32),
            pltpu.SMEM((2 * ROW_BLOCKS, SLOTS + 2 * STEP), jnp.int32),
            pltpu.SMEM((2 * ROW_BLOCKS,), jnp.int32),
            pltpu.SemaphoreType.DMA((3,)),
        ],
        compiler_params=pltpu.CompilerParams(vmem_limit_bytes=30 * 1024 * 1024),
        cost_estimate=pl.CostEstimate(flops=2 * 96 * 2 * 128 * 128 * 896, bytes_accessed=2**24, transcendentals=0),
        name="multiply",
    )(meta, own_blocks, other_blocks, panels)


def local(factors, block_rows, block_cols, block_count, orbitals, response):
    aux, row = lax.axis_index("aux"), lax.axis_index("row")
    y, zh, c = aux // (ZH * CORE), (aux // CORE) % ZH, aux % CORE
    x, zl = row // ZL, row % ZL
    place = dict(x=x, y=y, z=zh * ZL + zl)
    sign = 1 - 2 * c
    first = c == 0
    rows = ROW_BLOCKS * BLK
    nb = orbitals.shape[0] * Y * ZH * CORE * X * ZL
    bf16, f32 = jnp.bfloat16, jnp.float32

    def choose(a, b):
        return jnp.where(first, a, b)

    keep = choose(orbitals, response)
    got = swap_cores(choose(response, orbitals))
    both = jnp.stack([choose(keep, got), choose(got, keep)])
    both = jnp.pad(both, ((0, 0), (0, 0), (0, WIDE - NOCC)))

    own_blocks = factors[0]
    other_blocks = swap_cores(own_blocks)
    meta = jnp.concatenate(
        [block_rows[0] % ROW_BLOCKS, block_cols[0], block_count[0], jnp.zeros((256 - 2 * SLOTS - 1,), jnp.int32)]
    )[None]
    meta = jnp.concatenate([meta, swap_cores(meta)])

    def target(axis):
        at = place[axis]
        return {"x": {3: at}, "y": {0: at}, "z": {1: at // ZL, 4: at % ZL}}[axis]

    def gathered(piece, axis, forward):
        plus, minus = around(axis, 1), around(axis, -1)
        me = place[axis]
        from_behind = send(piece, plus)
        from_ahead = send(piece, minus)
        far = send(from_behind, plus) if forward else send(piece, around(axis, 2))
        return [
            (piece, me),
            (from_behind, (me - sign) % 4),
            (from_ahead, (me + sign) % 4),
            (far, (me + 2) % 4),
        ]

    def put(into, piece, axis, at, column=0):
        index = [jnp.int32(0)] * 7
        for dim, i in {"x": {3: at}, "y": {0: at}, "z": {1: at // ZL, 4: at % ZL}}[axis].items():
            index[dim] = i
        index[6] = jnp.int32(column)
        return lax.dynamic_update_slice(into, piece, index)

    sizes = {"x": {3: X}, "y": {0: Y}, "z": {1: ZH, 4: ZL}}
    pieces = []
    for low, high, order in PIECES:
        pieces.append(both[None, None, :, None, None, :, low:high])
    for stage in range(2):
        parts = [gathered(p, PIECES[j][2][stage], stage == 1) for j, p in enumerate(pieces)]
        for j, part in enumerate(parts):
            axis = PIECES[j][2][stage]
            shape = list(pieces[j].shape)
            for dim, n in sizes[axis].items():
                shape[dim] = n
            into = jnp.zeros(shape, bf16)
            for array, at in part:
                into = put(into, array, axis, at)
            pieces[j] = into
    parts = [gathered(p, PIECES[j][2][2], True) for j, p in enumerate(pieces)]
    panels = jnp.zeros((Y, ZH, CORE, X, ZL, orbitals.shape[0], WIDE), bf16)
    for j, part in enumerate(parts):
        for array, at in part:
            panels = put(panels, array, PIECES[j][2][2], at, PIECES[j][0])
    panels = panels.reshape(nb, WIDE)

    slab = lax.dynamic_slice(panels, (row * rows, 0), (rows, WIDE))[:, :NOCC]
    other_slab = swap_cores(slab)
    own_orbitals = choose(slab, other_slab)

    half = multiply(meta, own_blocks, other_blocks, panels)

    contract = (((0,), (0,)), ((), ()))
    cross, weights = [], []
    lane = jnp.arange(NOCC, dtype=jnp.int32)
    for q in range(2):
        product = lax.dot_general(half[q, :, :CROSS], own_orbitals, contract, preferred_element_type=f32)
        value = jnp.sum(half[q, :, :NOCC].astype(f32) * other_slab.astype(f32))
        high = lax.reduce_precision(value, 8, 7)
        middle = lax.reduce_precision(value - high, 8, 7)
        low = lax.reduce_precision(value - high - middle, 8, 7)
        coded = jnp.where(
            lane == 3 * row, high, jnp.where(lane == 3 * row + 1, middle, jnp.where(lane == 3 * row + 2, low, 0.0))
        )
        product = jnp.concatenate([product[:NOCC], coded[None], product[NOCC + 1 :]])
        cross.append(product)

    def scatter_x(array):
        n = array.shape[0] // X

        def chunk(k):
            return lax.dynamic_slice(array, ((k % X) * n, 0), (n, NOCC))

        ahead = send(chunk(x + sign).astype(bf16), around("x", 1))
        behind = send(chunk(x - sign).astype(bf16), around("x", -1))
        far = send(chunk(x + 2).astype(bf16), around("x", 2))
        return chunk(x) + ahead.astype(f32) + behind.astype(f32) + far.astype(f32)

    def scatter_low(array):
        n = array.shape[0] // ZL

        def chunk(k):
            return lax.dynamic_slice(array, (k * n, 0), (n, NOCC))

        return chunk(zl) + swap_low(chunk(1 - zl).astype(bf16)).astype(f32)

    def gather_x(array):
        n = array.shape[0]
        into = jnp.zeros((n * X, NOCC), array.dtype)
        for k, part in (
            (x, array),
            (x - sign, send(array, around("x", 1))),
            (x + sign, send(array, around("x", -1))),
            (x + 2, send(array, around("x", 2))),
        ):
            into = lax.dynamic_update_slice(into, part, ((k % X) * n, 0))
        return into

    def gather_low(array):
        n = array.shape[0]
        into = jnp.zeros((n * ZL, NOCC), array.dtype)
        into = lax.dynamic_update_slice(into, array, (zl * n, 0))
        return lax.dynamic_update_slice(into, swap_low(array), ((1 - zl) * n, 0))

    shards = [scatter_low(scatter_x(cross[0])), scatter_x(scatter_low(cross[1]))]
    last = (x == X - 1) & (zl == ZL - 1)
    at = jnp.arange(SHARD, dtype=jnp.int32)[:, None] + (CROSS - SHARD)
    is_code = last & (at == NOCC)
    shards = [jnp.where(is_code, s, s * (1.0 / nb)).astype(bf16) for s in shards]
    code = [s[NOCC - (CROSS - SHARD)] for s in shards]
    theirs = swap_cores(jnp.stack(shards))
    first_weights = jnp.where(last & (at == NOCC + 1), code[1][None], theirs[0])
    second_weights = jnp.where(last & (at == NOCC + 1), code[0][None], theirs[1])
    weight_of = [gather_low(gather_x(second_weights)), gather_x(gather_low(first_weights))]
    total = None
    for q in range(2):
        weight = weight_of[q]
        coulomb = jnp.sum(weight[NOCC : NOCC + 2].astype(f32)) * (1.0 / nb)
        factor = jnp.where(first, 2.0 * coulomb, 0.0)
        own = half[q, :, :NOCC]
        term = factor * own.astype(f32) - jnp.dot(own, weight[:NOCC], preferred_element_type=f32)
        total = term if total is None else total + term

    n = rows // 2
    mine = lax.dynamic_slice(total, (c * n, 0), (n, NOCC))
    mine = mine + swap_cores(lax.dynamic_slice(total, ((1 - c) * n, 0), (n, NOCC)))
    n = n // Y

    def quarter(k):
        return lax.dynamic_slice(mine, ((k % Y) * n, 0), (n, NOCC))

    ahead = send(quarter(y + sign).astype(bf16), around("y", 1))
    behind = send(quarter(y - sign).astype(bf16), around("y", -1))
    far = send(quarter(y + 2).astype(bf16), around("y", 2))
    part = quarter(y) + ahead.astype(f32) + behind.astype(f32) + far.astype(f32)
    part = part + swap_high(part)
    part = part.astype(bf16)
    into = jnp.zeros((rows // 2, NOCC), bf16)
    for k, array in (
        (y, part),
        (y - sign, send(part, around("y", 1))),
        (y + sign, send(part, around("y", -1))),
        (y + 2, send(part, around("y", 2))),
    ):
        into = lax.dynamic_update_slice(into, array, ((k % Y) * n, 0))
    theirs = swap_cores(into)
    return jnp.concatenate([choose(into, theirs), choose(theirs, into)]).astype(f32)


def solution(mesh):
    in_specs = (
        P("aux", "row", None, None),
        P("aux", "row"),
        P("aux", "row"),
        P("aux", "row"),
        P(("aux", "row"), None),
        P(("aux", "row"), None),
    )
    out_specs = P("row", None)
    return jax.shard_map(local, mesh=mesh, in_specs=in_specs, out_specs=out_specs, check_vma=False)
```

```python
import itertools

import jax
import jax.numpy as jnp
from jax import lax
from jax.experimental import pallas as pl
from jax.experimental.pallas import tpu as pltpu
from jax.sharding import PartitionSpec as P

Y, ZH, CORE, X, ZL = 4, 2, 2, 4, 2
AXES = ("aux", "row")
BLK = 128
ROW_BLOCKS = 6
SLOTS = 96
NOCC = 800
WIDE = 896
CROSS = 832
SHARD = CROSS // 8
STEP = 4
UNROLL = 3
GROUPS = 2 * ROW_BLOCKS
NB = 6144
GRAIN = 16
POSITION = 200
FLIGHT = 5
ORDERS = ("xyz", "yzx", "zxy")
LAST = tuple(order[2] for order in ORDERS)


def permutation(move):
    pairs = []
    for y, zh, c, x, zl in itertools.product(range(Y), range(ZH), range(CORE), range(X), range(ZL)):
        at = dict(y=y, z=zh * ZL + zl, c=c, x=x)
        to = move(dict(at))

        def flat(d):
            return (((d["y"] * ZH + d["z"] // ZL) * CORE + d["c"]) * X + d["x"]) * ZL + d["z"] % ZL

        pairs.append((flat(at), flat(to)))
    return pairs


def around(axis, by):
    def move(d):
        d[axis] = (d[axis] + (by if d["c"] == 0 else -by)) % 4
        return d

    return permutation(move)


def other_core(d):
    d["c"] = 1 - d["c"]
    return d


def other_low(d):
    d["z"] = d["z"] ^ 1
    return d


def other_high(d):
    d["z"] = d["z"] ^ 2
    return d


def send(array, pairs):
    return lax.ppermute(array, AXES, pairs)


def swap_cores(array):
    return send(array, permutation(other_core))


def swap_low(array):
    return send(array, permutation(other_low))


def swap_high(array):
    return send(array, permutation(other_high))


def multiply_kernel(meta, own_blocks, other_blocks, *refs):
    parts = refs[:12]
    out, blocks, held, total, order, counts, steps, sems = refs[12:]
    copies = [
        pltpu.make_async_copy(own_blocks, blocks.at[pl.ds(0, SLOTS)], sems.at[0]),
        pltpu.make_async_copy(other_blocks, blocks.at[pl.ds(SLOTS, SLOTS)], sems.at[1]),
    ]
    for j, (axis, part) in enumerate(zip(LAST, (parts[0:4], parts[4:8], parts[8:12]))):
        for k in range(4):
            at = meta[0, POSITION + 4 * j + k]
            if axis == "z":
                source, into = part[k].at[:, 0, :, :, 0], held.at[:, at // ZL, :, :, at % ZL, j]
            elif axis == "x":
                source, into = part[k].at[:, :, :, 0], held.at[:, :, :, at, :, j]
            else:
                source, into = part[k].at[0], held.at[at, :, :, :, :, j]
            copies.append(pltpu.make_async_copy(source, into, sems.at[2 + 4 * j + k]))
    for copy in copies:
        copy.start()
    blocks[2 * SLOTS] = jnp.zeros((BLK, BLK), jnp.bfloat16)

    def clear(i, carry):
        counts[i] = 0
        total[i] = jnp.zeros((BLK, WIDE), jnp.float32)
        return carry

    lax.fori_loop(0, GROUPS + 1, clear, 0)
    for q in range(2):

        def place(s, carry):
            group = q * ROW_BLOCKS + meta[q, s]
            n = counts[group]
            order[group, n] = s + q * SLOTS
            counts[group] = n + 1
            return carry

        lax.fori_loop(0, meta[q, 2 * SLOTS], place, 0)

    def list_group(group, base):
        n = counts[group]
        for i in range(STEP):
            order[group, n + i] = 2 * SLOTS
        many = (n + STEP - 1) // STEP

        def list_step(i, carry):
            steps[base + i, 0] = group
            for k in range(STEP):
                s = order[group, i * STEP + k]
                q = jnp.minimum(s // SLOTS, 1)
                steps[base + i, 1 + k] = s
                steps[base + i, 1 + STEP + k] = jnp.where(s < 2 * SLOTS, meta[q, SLOTS + s - q * SLOTS], 0)
            return carry

        lax.fori_loop(0, many, list_step, 0)
        return base + many

    many = lax.fori_loop(0, GROUPS, list_group, 0)
    for u in range(UNROLL - 1):
        steps[many + u, 0] = GROUPS
        for k in range(STEP):
            steps[many + u, 1 + k] = 2 * SLOTS
            steps[many + u, 1 + STEP + k] = 0
    for copy in copies:
        copy.wait()
    panels = held.reshape(NB, WIDE)

    def some(i, carry):
        products = []
        for u in range(UNROLL):
            left, right = [], []
            for k in range(STEP):
                left.append(blocks[steps[i * UNROLL + u, 1 + k]])
                column = steps[i * UNROLL + u, 1 + STEP + k]
                right.append(panels[pl.ds(pl.multiple_of(column * BLK, BLK), BLK), :])
            products.append(
                jnp.dot(
                    jnp.concatenate(left, axis=1),
                    jnp.concatenate(right, axis=0),
                    preferred_element_type=jnp.float32,
                )
            )
        for u in range(UNROLL):
            total[steps[i * UNROLL + u, 0]] += products[u]
        return carry

    lax.fori_loop(0, (many + UNROLL - 1) // UNROLL, some, 0)

    def finish(group, carry):
        q = group // ROW_BLOCKS
        start = pl.multiple_of((group - q * ROW_BLOCKS) * BLK, BLK)
        out[q, pl.ds(start, BLK), :] = total[group].astype(jnp.bfloat16)
        return carry

    lax.fori_loop(0, GROUPS, finish, 0)


def multiply(meta, own_blocks, other_blocks, parts):
    most = 2 * SLOTS // STEP + GROUPS + UNROLL
    return pl.pallas_call(
        multiply_kernel,
        out_shape=jax.ShapeDtypeStruct((2, ROW_BLOCKS * BLK, WIDE), jnp.bfloat16),
        in_specs=[pl.BlockSpec(memory_space=pltpu.SMEM)] + [pl.BlockSpec(memory_space=pl.ANY)] * 14,
        out_specs=pl.BlockSpec(memory_space=pltpu.VMEM),
        scratch_shapes=[
            pltpu.VMEM((2 * SLOTS + 1, BLK, BLK), jnp.bfloat16),
            pltpu.VMEM((Y, ZH, CORE, X, ZL, 3, GRAIN, WIDE), jnp.bfloat16),
            pltpu.VMEM((GROUPS + 1, BLK, WIDE), jnp.float32),
            pltpu.SMEM((GROUPS, SLOTS + 2 * STEP), jnp.int32),
            pltpu.SMEM((GROUPS + 1,), jnp.int32),
            pltpu.SMEM((most, 1 + 2 * STEP), jnp.int32),
            pltpu.SemaphoreType.DMA((14,)),
        ],
        compiler_params=pltpu.CompilerParams(vmem_limit_bytes=36 * 1024 * 1024),
        cost_estimate=pl.CostEstimate(flops=2 * 96 * 2 * 128 * 128 * 896, bytes_accessed=2**24, transcendentals=0),
        name="multiply",
    )(meta, own_blocks, other_blocks, *parts)


def local(factors, block_rows, block_cols, block_count, orbitals, response):
    aux, row = lax.axis_index("aux"), lax.axis_index("row")
    y, zh, c = aux // (ZH * CORE), (aux // CORE) % ZH, aux % CORE
    x, zl = row // ZL, row % ZL
    whereabouts = dict(x=x, y=y, z=zh * ZL + zl)
    sign = 1 - 2 * c
    first = c == 0
    rows = ROW_BLOCKS * BLK
    nb = orbitals.shape[0] * Y * ZH * CORE * X * ZL
    bf16, f32 = jnp.bfloat16, jnp.float32

    def choose(a, b):
        return jnp.where(first, a, b)

    flying = []

    def send_next(array, pairs):
        if len(flying) >= FLIGHT:
            array, _ = lax.optimization_barrier((array, flying[-FLIGHT]))
        got = send(array, pairs)
        flying.append(got)
        return got

    keep = choose(orbitals, response)
    got = send_next(choose(response, orbitals), permutation(other_core))
    own_blocks = factors[0]
    other_blocks = send_next(own_blocks, permutation(other_core))
    both = jnp.stack([choose(keep, got), choose(got, keep)])
    both = jnp.pad(both, ((0, 0), (0, 0), (0, WIDE - NOCC)))

    def spot(axis, at):
        return {"x": {3: at}, "y": {0: at}, "z": {1: at // ZL, 4: at % ZL}}[axis]

    def put(into, piece, axis, at):
        index = [jnp.int32(0)] * into.ndim
        for dim, i in spot(axis, at).items():
            index[dim] = i
        return lax.dynamic_update_slice(into, piece, index)

    def cut(array, axes):
        index, size = [jnp.int32(0)] * array.ndim, list(array.shape)
        for dim, i in axes.items():
            index[dim], size[dim] = i, 1
        return lax.dynamic_slice(array, index, size)

    def empty(piece, axis):
        shape = list(piece.shape)
        for dim, n in {"x": {3: X}, "y": {0: Y}, "z": {1: ZH, 4: ZL}}[axis].items():
            shape[dim] = n
        return jnp.zeros(shape, piece.dtype)

    pieces = [both[None, None, :, None, None, j * GRAIN : (j + 1) * GRAIN, :] for j in range(3)]
    for stage in range(3):
        axes = [order[stage] for order in ORDERS]
        if stage == 0:
            arrived = [[], [], []]
            for j, axis in enumerate(axes):
                arrived[j] = [send_next(pieces[j], around(axis, by)) for by in (1, -1, 2)]
        else:
            ahead = [send_next(pieces[j], around(axis, 1)) for j, axis in enumerate(axes)]
            behind = [send_next(pieces[j], around(axis, -1)) for j, axis in enumerate(axes)]
            far = [send_next(ahead[j], around(axis, 1)) for j, axis in enumerate(axes)]
            arrived = list(zip(ahead, behind, far))
        parts = []
        for j, axis in enumerate(axes):
            me = whereabouts[axis]
            where = (me, (me - sign) % 4, (me + sign) % 4, (me + 2) % 4)
            parts.append(list(zip((pieces[j], *arrived[j]), where)))
        if stage < 2:
            for j, axis in enumerate(axes):
                into = empty(pieces[j], axis)
                for array, at in parts[j]:
                    into = put(into, array, axis, at)
                pieces[j] = into

    slabs = []
    for j, axis in enumerate(LAST):
        fixed = {"z": {0: row // 2}, "x": {0: row // 2, 1: row % 2}, "y": {1: row % 2}}[axis]
        rest = {"z": {1: row % 2}, "x": {}, "y": {0: row // 2}}[axis]
        cuts = [(cut(array, fixed), at) for array, at in parts[j]]
        into = empty(cuts[0][0], axis)
        for array, at in cuts:
            into = put(into, array, axis, at)
        slabs.append(cut(into, rest))
    slab = jnp.stack(slabs, axis=5).reshape(rows, WIDE)
    other_slab = swap_cores(slab)
    own_orbitals = choose(slab, other_slab)[:, :NOCC]

    lists = jnp.concatenate([block_rows[0] % ROW_BLOCKS, block_cols[0], block_count[0]])
    lists = jnp.pad(lists, (0, POSITION - 2 * SLOTS - 1))
    where = jnp.stack([at for part in parts for _, at in part]).astype(jnp.int32)
    lists = jnp.concatenate([lists, where, jnp.zeros((256 - POSITION - 12,), jnp.int32)])[None]
    meta = jnp.concatenate([lists, send_next(lists, permutation(other_core))])
    half = multiply(meta, own_blocks, other_blocks, [array for part in parts for array, _ in part])

    contract = (((0,), (0,)), ((), ()))
    cross = []
    lane = jnp.arange(NOCC, dtype=jnp.int32)
    for q in range(2):
        product = lax.dot_general(half[q, :, :CROSS], own_orbitals, contract, preferred_element_type=f32).astype(bf16)
        value = jnp.sum(half[q].astype(f32) * other_slab.astype(f32))
        high = lax.reduce_precision(value, 8, 7)
        middle = lax.reduce_precision(value - high, 8, 7)
        low = lax.reduce_precision(value - high - middle, 8, 7)
        coded = jnp.where(
            lane == 3 * row, high, jnp.where(lane == 3 * row + 1, middle, jnp.where(lane == 3 * row + 2, low, 0.0))
        )
        cross.append(lax.dynamic_update_slice(product, coded.astype(bf16)[None], (NOCC, 0)))

    def scatter_x(array):
        n = array.shape[0] // X

        def chunk(k):
            return lax.dynamic_slice(array, ((k % X) * n, 0), (n, NOCC))

        ahead = send(chunk(x + sign), around("x", 1))
        behind = send(chunk(x - sign), around("x", -1))
        far = send(chunk(x + 2), around("x", 2))
        return chunk(x).astype(f32) + ahead.astype(f32) + behind.astype(f32) + far.astype(f32)

    def scatter_low(array):
        n = array.shape[0] // ZL

        def chunk(k):
            return lax.dynamic_slice(array, (k * n, 0), (n, NOCC))

        return chunk(zl).astype(f32) + swap_low(chunk(1 - zl)).astype(f32)

    def gather_x(array):
        n = array.shape[0]
        into = jnp.zeros((n * X, NOCC), array.dtype)
        for k, part in (
            (x, array),
            (x - sign, send(array, around("x", 1))),
            (x + sign, send(array, around("x", -1))),
            (x + 2, send(array, around("x", 2))),
        ):
            into = lax.dynamic_update_slice(into, part, ((k % X) * n, 0))
        return into

    def gather_low(array):
        n = array.shape[0]
        into = jnp.zeros((n * ZL, NOCC), array.dtype)
        into = lax.dynamic_update_slice(into, array, (zl * n, 0))
        return lax.dynamic_update_slice(into, swap_low(array), ((1 - zl) * n, 0))

    shards = [scatter_low(scatter_x(cross[0]).astype(bf16)), scatter_x(scatter_low(cross[1]).astype(bf16))]
    last = (x == X - 1) & (zl == ZL - 1)
    at = jnp.arange(SHARD, dtype=jnp.int32)[:, None] + (CROSS - SHARD)
    is_code = last & (at == NOCC)
    shards = [jnp.where(is_code, s, s * (1.0 / nb)).astype(bf16) for s in shards]
    code = [s[NOCC - (CROSS - SHARD)] for s in shards]
    theirs = swap_cores(jnp.stack(shards))
    first_weights = jnp.where(last & (at == NOCC + 1), code[1][None], theirs[0])
    second_weights = jnp.where(last & (at == NOCC + 1), code[0][None], theirs[1])
    weight_of = [gather_low(gather_x(second_weights)), gather_x(gather_low(first_weights))]
    total = None
    for q in range(2):
        weight = weight_of[q]
        coulomb = jnp.sum(weight[NOCC : NOCC + 2].astype(f32)) * (1.0 / nb)
        factor = jnp.where(first, 2.0 * coulomb, 0.0)
        own = half[q, :, :NOCC]
        exchange = lax.dot_general(weight[:NOCC], own, (((0,), (1,)), ((), ())), preferred_element_type=f32)
        term = factor * own.T.astype(f32) - exchange
        total = term if total is None else total + term
    total = jnp.pad(total, ((0, CROSS - NOCC), (0, 0)))

    n = CROSS // 2
    mine = lax.dynamic_slice(total, (c * n, 0), (n, rows))
    mine = mine + swap_cores(lax.dynamic_slice(total, ((1 - c) * n, 0), (n, rows)))
    n = n // Y

    def quarter(k):
        return lax.dynamic_slice(mine, ((k % Y) * n, 0), (n, rows))

    ahead = send(quarter(y + sign).astype(bf16), around("y", 1))
    behind = send(quarter(y - sign).astype(bf16), around("y", -1))
    far = send(quarter(y + 2).astype(bf16), around("y", 2))
    part = quarter(y) + ahead.astype(f32) + behind.astype(f32) + far.astype(f32)
    part = (part + swap_high(part)).astype(bf16)
    into = jnp.zeros((CROSS // 2, rows), bf16)
    for k, array in (
        (y, part),
        (y - sign, send(part, around("y", 1))),
        (y + sign, send(part, around("y", -1))),
        (y + 2, send(part, around("y", 2))),
    ):
        into = lax.dynamic_update_slice(into, array, ((k % Y) * n, 0))
    theirs = swap_cores(into)
    return jnp.concatenate([choose(into, theirs), choose(theirs, into)])[:NOCC].astype(f32).T


def solution(mesh):
    in_specs = (
        P("aux", "row", None, None),
        P("aux", "row"),
        P("aux", "row"),
        P("aux", "row"),
        P(("aux", "row"), None),
        P(("aux", "row"), None),
    )
    out_specs = P("row", None)
    return jax.shard_map(local, mesh=mesh, in_specs=in_specs, out_specs=out_specs, check_vma=False)
```

```python
import itertools

import jax
import jax.numpy as jnp
from jax import lax
from jax.experimental import pallas as pl
from jax.experimental.pallas import tpu as pltpu
from jax.sharding import PartitionSpec as P

Y, ZH, CORE, X, ZL = 4, 2, 2, 4, 2
AXES = ("aux", "row")
BLK = 128
ROW_BLOCKS = 6
ROWS = ROW_BLOCKS * BLK
GROUPS = 2 * ROW_BLOCKS
SLOTS = 96
NB = 6144
NOCC = 800
WIDE = 896
SHARD = WIDE // 8
OWN = 48
STEP = 4
UNROLL = 3
FLIGHT = 5
MAIN = 32
bf16, f32 = jnp.bfloat16, jnp.float32


def permutation(move):
    pairs = []
    for y, zh, c, x, zl in itertools.product(range(Y), range(ZH), range(CORE), range(X), range(ZL)):
        at = dict(y=y, z=zh * ZL + zl, c=c, x=x)
        to = move(dict(at))

        def flat(d):
            return (((d["y"] * ZH + d["z"] // ZL) * CORE + d["c"]) * X + d["x"]) * ZL + d["z"] % ZL

        pairs.append((flat(at), flat(to)))
    return pairs


def around(axes, by, mirror):
    def move(d):
        axis = axes[d["c"]]
        d[axis] = (d[axis] + (-by if mirror and d["c"] else by)) % 4
        return d

    return permutation(move)


def other_core(d):
    d["c"] = 1 - d["c"]
    return d


def other_low(d):
    d["z"] = d["z"] ^ 1
    return d


def other_high(d):
    d["z"] = d["z"] ^ 2
    return d


def send(array, pairs):
    return lax.ppermute(array, AXES, pairs)


def swap_cores(array):
    return send(array, permutation(other_core))


def swap_low(array):
    return send(array, permutation(other_low))


def swap_high(array):
    return send(array, permutation(other_high))


def slab_kernel(place, main, rest, out, sems):
    core, row = place[0], place[1]
    copies = []
    for x in range(X):
        a = jnp.where(core == 0, x, row // ZL)
        b = jnp.where(core == 0, row // ZL, x)
        copies.append(
            pltpu.make_async_copy(main.at[b, row % ZL, :, :, a], out.at[:, x, :, pl.ds(0, MAIN)], sems.at[2 * x])
        )
        copies.append(
            pltpu.make_async_copy(
                rest.at[row % ZL, :, :, a, b], out.at[:, x, :, pl.ds(MAIN, OWN - MAIN)], sems.at[2 * x + 1]
            )
        )
    for copy in copies:
        copy.start()
    for copy in copies:
        copy.wait()


def own_slab(place, main, rest):
    return pl.pallas_call(
        slab_kernel,
        out_shape=jax.ShapeDtypeStruct((CORE, X, ZL, OWN, WIDE), bf16),
        in_specs=[pl.BlockSpec(memory_space=pltpu.SMEM)] + [pl.BlockSpec(memory_space=pl.ANY)] * 2,
        out_specs=pl.BlockSpec(memory_space=pltpu.VMEM),
        scratch_shapes=[pltpu.SemaphoreType.DMA((2 * X,))],
        compiler_params=pltpu.CompilerParams(vmem_limit_bytes=4 * 1024 * 1024),
        name="slab",
    )(place, main, rest)


def multiply_kernel(place, meta, own_blocks, other_blocks, main, rest, out, blocks, held, total, order, counts, steps, sems):
    core = place[0]
    copies = [
        pltpu.make_async_copy(own_blocks, blocks.at[pl.ds(0, SLOTS)], sems.at[0]),
        pltpu.make_async_copy(other_blocks, blocks.at[pl.ds(SLOTS, SLOTS)], sems.at[1]),
    ]
    for a in range(4):
        for b in range(4):
            y, x = jnp.where(core == 0, b, a), jnp.where(core == 0, a, b)
            i = 2 + 2 * (4 * a + b)
            copies.append(
                pltpu.make_async_copy(
                    main.at[b, :, :, :, a], held.at[y, :, :, x, :, pl.ds(0, MAIN)], sems.at[i]
                )
            )
            copies.append(
                pltpu.make_async_copy(
                    rest.at[:, :, :, a, b], held.at[y, :, :, x, :, pl.ds(MAIN, OWN - MAIN)], sems.at[i + 1]
                )
            )
    for copy in copies:
        copy.start()
    blocks[2 * SLOTS] = jnp.zeros((BLK, BLK), bf16)

    def clear(i, carry):
        counts[i] = 0
        total[i] = jnp.zeros((BLK, WIDE), f32)
        return carry

    lax.fori_loop(0, GROUPS + 1, clear, 0)
    for q in range(2):

        def put(s, carry):
            group = q * ROW_BLOCKS + meta[q, s]
            n = counts[group]
            order[group, n] = s + q * SLOTS
            counts[group] = n + 1
            return carry

        lax.fori_loop(0, meta[q, 2 * SLOTS], put, 0)

    def list_group(group, base):
        n = counts[group]
        for i in range(STEP):
            order[group, n + i] = 2 * SLOTS
        many = (n + STEP - 1) // STEP

        def list_step(i, carry):
            steps[base + i, 0] = group
            for k in range(STEP):
                s = order[group, i * STEP + k]
                q = jnp.minimum(s // SLOTS, 1)
                steps[base + i, 1 + k] = s
                steps[base + i, 1 + STEP + k] = jnp.where(s < 2 * SLOTS, meta[q, SLOTS + s - q * SLOTS], 0)
            return carry

        lax.fori_loop(0, many, list_step, 0)
        return base + many

    many = lax.fori_loop(0, GROUPS, list_group, 0)
    for u in range(UNROLL - 1):
        steps[many + u, 0] = GROUPS
        for k in range(STEP):
            steps[many + u, 1 + k] = 2 * SLOTS
            steps[many + u, 1 + STEP + k] = 0
    for copy in copies:
        copy.wait()
    panels = held.reshape(NB, WIDE)

    def some(i, carry):
        products = []
        for u in range(UNROLL):
            left, right = [], []
            for k in range(STEP):
                left.append(blocks[steps[i * UNROLL + u, 1 + k]])
                column = steps[i * UNROLL + u, 1 + STEP + k]
                right.append(panels[pl.ds(pl.multiple_of(column * BLK, BLK), BLK), :])
            products.append(
                jnp.dot(jnp.concatenate(left, axis=1), jnp.concatenate(right, axis=0), preferred_element_type=f32)
            )
        for u in range(UNROLL):
            total[steps[i * UNROLL + u, 0]] += products[u]
        return carry

    lax.fori_loop(0, (many + UNROLL - 1) // UNROLL, some, 0)

    def finish(group, carry):
        q = group // ROW_BLOCKS
        start = pl.multiple_of((group - q * ROW_BLOCKS) * BLK, BLK)
        out[q, pl.ds(start, BLK), :] = total[group].astype(bf16)
        return carry

    lax.fori_loop(0, GROUPS, finish, 0)


def multiply(place, meta, own_blocks, other_blocks, main, rest):
    most = 2 * SLOTS // STEP + GROUPS + UNROLL
    return pl.pallas_call(
        multiply_kernel,
        out_shape=jax.ShapeDtypeStruct((2, ROWS, WIDE), bf16),
        in_specs=[pl.BlockSpec(memory_space=pltpu.SMEM)] * 2 + [pl.BlockSpec(memory_space=pl.ANY)] * 4,
        out_specs=pl.BlockSpec(memory_space=pltpu.VMEM),
        scratch_shapes=[
            pltpu.VMEM((2 * SLOTS + 1, BLK, BLK), bf16),
            pltpu.VMEM((Y, ZH, CORE, X, ZL, OWN, WIDE), bf16),
            pltpu.VMEM((GROUPS + 1, BLK, WIDE), f32),
            pltpu.SMEM((GROUPS, SLOTS + 2 * STEP), jnp.int32),
            pltpu.SMEM((GROUPS + 1,), jnp.int32),
            pltpu.SMEM((most, 1 + 2 * STEP), jnp.int32),
            pltpu.SemaphoreType.DMA((34,)),
        ],
        compiler_params=pltpu.CompilerParams(vmem_limit_bytes=30 * 1024 * 1024),
        cost_estimate=pl.CostEstimate(flops=2 * 96 * 2 * 128 * 128 * 896, bytes_accessed=2**24, transcendentals=0),
        name="multiply",
    )(place, meta, own_blocks, other_blocks, main, rest)


def cross_kernel(q, starts, place, half, slab, theirs, *refs):
    outs, used, product = refs[:-2], refs[-2], refs[-1]
    core, row = place[0], place[1]
    used[...] = jnp.where(core == 0, slab[...], theirs[...])
    product[...] = lax.dot_general(
        half[q], used[...], (((0,), (0,)), ((), ())), preferred_element_type=f32
    ).astype(bf16)
    value = jnp.sum(half[q].astype(f32) * theirs[...].astype(f32), keepdims=True)
    high = value.astype(bf16).astype(f32)
    middle = (value - high).astype(bf16).astype(f32)
    low = value - high - middle
    lane = lax.broadcasted_iota(jnp.int32, (16, WIDE), 1)
    line = lax.broadcasted_iota(jnp.int32, (16, WIDE), 0)
    coded = jnp.where(
        lane == 3 * row, high, jnp.where(lane == 3 * row + 1, middle, jnp.where(lane == 3 * row + 2, low, 0.0))
    )
    product[NOCC : NOCC + 16, :] = jnp.where(line == 0, coded, 0.0).astype(bf16)
    for out, start in zip(outs, starts):
        n = out.shape[0]
        out[...] = product[pl.ds(pl.multiple_of(place[start] * n, n), n), :]


def cross(q, starts, n, place, half, slab, theirs):
    def kernel(*refs):
        cross_kernel(q, starts, *refs)

    return pl.pallas_call(
        kernel,
        out_shape=[jax.ShapeDtypeStruct((n, WIDE), bf16)] * len(starts),
        in_specs=[pl.BlockSpec(memory_space=pltpu.SMEM)] + [pl.BlockSpec(memory_space=pltpu.VMEM)] * 3,
        out_specs=[pl.BlockSpec(memory_space=pltpu.VMEM)] * len(starts),
        scratch_shapes=[pltpu.VMEM((ROWS, WIDE), bf16), pltpu.VMEM((WIDE, WIDE), bf16)],
        compiler_params=pltpu.CompilerParams(vmem_limit_bytes=30 * 1024 * 1024),
        cost_estimate=pl.CostEstimate(flops=2 * 768 * 896 * 896, bytes_accessed=2**23, transcendentals=0),
        name="cross",
    )(place, half, slab, theirs)


def exchange_kernel(place, half, first, second, keep, give, turned):
    core = place[0]
    total = None
    for q, weight in enumerate((first, second)):
        line = lax.broadcasted_iota(jnp.int32, (16, WIDE), 0)
        codes = jnp.where(line < 2, weight[NOCC : NOCC + 16, :].astype(f32), 0.0)
        coulomb = jnp.sum(codes, keepdims=True) * (1.0 / NB)
        factor = jnp.where(core == 0, 2.0 * coulomb, 0.0)
        own = half[q]
        term = factor * own.astype(f32) - jnp.dot(own, weight[...], preferred_element_type=f32)
        total = term if total is None else total + term
    turned[...] = total.T
    n = WIDE // 2
    keep[...] = turned[pl.ds(pl.multiple_of(core * n, n), n), :]
    give[...] = turned[pl.ds(pl.multiple_of((1 - core) * n, n), n), :]


def exchange(place, half, first, second):
    return pl.pallas_call(
        exchange_kernel,
        out_shape=[jax.ShapeDtypeStruct((WIDE // 2, ROWS), f32)] * 2,
        in_specs=[pl.BlockSpec(memory_space=pltpu.SMEM)] + [pl.BlockSpec(memory_space=pltpu.VMEM)] * 3,
        out_specs=[pl.BlockSpec(memory_space=pltpu.VMEM)] * 2,
        scratch_shapes=[pltpu.VMEM((WIDE, ROWS), f32)],
        compiler_params=pltpu.CompilerParams(vmem_limit_bytes=36 * 1024 * 1024),
        cost_estimate=pl.CostEstimate(flops=4 * 768 * 896 * 896, bytes_accessed=2**23, transcendentals=0),
        name="exchange",
    )(place, half, first, second)


def local(factors, block_rows, block_cols, block_count, orbitals, response):
    aux, row = lax.axis_index("aux"), lax.axis_index("row")
    y, zh, c = aux // (ZH * CORE), (aux // CORE) % ZH, aux % CORE
    x, zl = row // ZL, row % ZL
    z = zh * ZL + zl
    sign = 1 - 2 * c
    first = c == 0

    def choose(a, b):
        return jnp.where(first, a, b)

    flying = []

    def send_next(array, pairs):
        if len(flying) >= FLIGHT:
            array, _ = lax.optimization_barrier((array, flying[-FLIGHT]))
        got = send(array, pairs)
        flying.append(got)
        return got

    def put(into, array, **at):
        index = [jnp.int32(0)] * into.ndim
        for dim, i in at.items():
            index[int(dim[1:])] = i
        return lax.dynamic_update_slice(into, array, index)

    lists = jnp.concatenate([block_rows % ROW_BLOCKS, block_cols, jnp.broadcast_to(block_count, (1, SLOTS))])
    tail = jnp.pad(lists.astype(bf16), ((0, OWN - 3), (0, 0)))
    got = send_next(
        jnp.concatenate([choose(response, orbitals), tail], axis=1), permutation(other_core)
    )
    own_blocks = factors[0]
    other_blocks = send_next(own_blocks, permutation(other_core))
    other_lists = got[:3, NOCC:].astype(jnp.int32)
    meta = jnp.stack([jnp.concatenate([a[0], a[1], a[2, :64]]) for a in (lists, other_lists)])
    place = jnp.stack(
        [c, row, x, (x + sign) % 4, (x - sign) % 4, (x + 2) % 4, zl, 1 - zl]
    ).astype(jnp.int32)
    keep = jnp.pad(choose(orbitals, response), ((0, 0), (0, WIDE - NOCC)))
    got = jnp.where(jnp.arange(WIDE)[None] < NOCC, got, jnp.zeros((), bf16))
    both = jnp.stack([choose(keep, got), choose(got, keep)])

    one, two = ("x", "y"), ("y", "x")
    at_one, at_two = choose(x, y), choose(y, x)
    shape = (CORE, 4, OWN, WIDE)
    stage = put(jnp.zeros(shape, bf16), both[:, None], d1=at_one)
    ahead = send_next(both, around(one, 1, False))
    behind = send_next(both, around(one, -1, False))
    far = send_next(both, around(one, 2, False))
    stage = put(stage, ahead[:, None], d1=(at_one - 1) % 4)
    stage = put(stage, behind[:, None], d1=(at_one + 1) % 4)
    stage = put(stage, far[:, None], d1=(at_one + 2) % 4)

    main, rest = stage[:, :, :MAIN], stage[:, :, MAIN:]
    zz = ("z", "z")
    main_ahead = send_next(main, around(zz, 1, True))
    main_behind = send_next(main, around(zz, -1, True))
    rest_ahead = send_next(rest, around(two, 1, False))
    rest_behind = send_next(rest, around(two, -1, False))
    main_far = send_next(main_ahead, around(zz, 1, True))
    rest_far = send_next(rest, around(two, 2, False))

    def by_z(into, array, at):
        return put(into, array, d0=at // ZL, d2=at % ZL)

    into = jnp.zeros((ZH, CORE, ZL, 4, MAIN, WIDE), bf16)
    for array, at in (
        (main, z),
        (main_ahead, (z - sign) % 4),
        (main_behind, (z + sign) % 4),
        (main_far, (z + 2) % 4),
    ):
        into = by_z(into, array[None, :, None], at)
    main = into
    into = jnp.zeros((CORE, 4, 4, OWN - MAIN, WIDE), bf16)
    for array, at in (
        (rest, at_two),
        (rest_ahead, (at_two - 1) % 4),
        (rest_behind, (at_two + 1) % 4),
        (rest_far, (at_two + 2) % 4),
    ):
        into = put(into, array[:, :, None], d2=at)
    rest = into

    main_ahead = send_next(main, around(two, 1, False))
    rest_ahead = send_next(rest, around(zz, 1, True))
    main_behind = send_next(main, around(two, -1, False))
    rest_behind = send_next(rest, around(zz, -1, True))
    main_far = [
        send_next(main_ahead[:1], around(two, 1, False)),
        send_next(main_behind[1:], around(two, -1, False)),
    ]
    rest_far = send_next(rest_ahead, around(zz, 1, True))
    into = jnp.zeros((4, *main.shape), bf16)
    for array, at, part in (
        (main, at_two, 0),
        (main_ahead, (at_two - 1) % 4, 0),
        (main_behind, (at_two + 1) % 4, 0),
        (main_far[0], (at_two + 2) % 4, 0),
        (main_far[1], (at_two + 2) % 4, 1),
    ):
        into = put(into, array[None], d0=at, d1=jnp.int32(part))
    main = into
    into = jnp.zeros((ZH, CORE, ZL, 4, 4, OWN - MAIN, WIDE), bf16)
    for array, at in (
        (rest, z),
        (rest_ahead, (z - sign) % 4),
        (rest_behind, (z + sign) % 4),
        (rest_far, (z + 2) % 4),
    ):
        into = by_z(into, array[None, :, None], at)
    rest = into

    slab = own_slab(place, main, rest).reshape(ROWS, WIDE)
    theirs = swap_cores(slab)
    half = multiply(place, meta, own_blocks, other_blocks, main, rest)

    def add(*arrays):
        return sum(a.astype(f32) for a in arrays)

    def rows_of(array, k, n):
        return lax.dynamic_slice(array, (k * n, 0), (n, array.shape[1]))

    xx = ("x", "x")
    ahead, behind = around(xx, 1, True), around(xx, -1, True)
    opposite = around(xx, 2, True)
    mine, to_ahead, to_behind, to_far = cross(0, (2, 3, 4, 5), WIDE // 4, place, half, slab, theirs)
    mine = add(mine, send(to_ahead, ahead), send(to_behind, behind), send(to_far, opposite)).astype(bf16)
    half_mine, to_low = cross(1, (6, 7), WIDE // 2, place, half, slab, theirs)
    half_mine = add(half_mine, swap_low(to_low)).astype(bf16)
    shards = [
        add(rows_of(mine, zl, SHARD), swap_low(rows_of(mine, 1 - zl, SHARD))),
        add(
            rows_of(half_mine, x, SHARD),
            send(rows_of(half_mine, (x + sign) % 4, SHARD), ahead),
            send(rows_of(half_mine, (x - sign) % 4, SHARD), behind),
            send(rows_of(half_mine, (x + 2) % 4, SHARD), opposite),
        ),
    ]

    last = (x == X - 1) & (zl == ZL - 1)
    at = jnp.arange(SHARD, dtype=jnp.int32)[:, None] + (WIDE - SHARD)
    shards = [jnp.where(last & (at == NOCC), s, s * (1.0 / NB)).astype(bf16) for s in shards]
    code = [s[NOCC - (WIDE - SHARD)] for s in shards]
    other_shards = swap_cores(jnp.stack(shards))
    here = last & (at == NOCC + 1)
    by_x = jnp.where(here, code[1][None], other_shards[0])
    by_low = jnp.where(here, code[0][None], other_shards[1])

    def gather_x(array):
        n = array.shape[0]
        into = jnp.zeros((n * X, WIDE), bf16)
        for k, part in (
            (x, array),
            (x - sign, send(array, ahead)),
            (x + sign, send(array, behind)),
            (x + 2, send(array, opposite)),
        ):
            into = lax.dynamic_update_slice(into, part, ((k % X) * n, 0))
        return into

    def gather_low(array):
        n = array.shape[0]
        into = jnp.zeros((n * ZL, WIDE), bf16)
        into = lax.dynamic_update_slice(into, array, (zl * n, 0))
        return lax.dynamic_update_slice(into, swap_low(array), ((1 - zl) * n, 0))

    keep, give = exchange(place, half, gather_low(gather_x(by_low)), gather_x(gather_low(by_x)))

    yy = ("y", "y")
    ahead, behind, opposite = around(yy, 1, True), around(yy, -1, True), around(yy, 2, True)
    mine = keep + swap_cores(give)

    def quarter(k):
        return rows_of(mine, k % Y, SHARD)

    part = quarter(y) + add(
        send(quarter(y + sign).astype(bf16), ahead),
        send(quarter(y - sign).astype(bf16), behind),
        send(quarter(y + 2).astype(bf16), opposite),
    )
    part = (part + swap_high(part)).astype(bf16)
    into = jnp.zeros((WIDE // 2, ROWS), bf16)
    for k, array in (
        (y, part),
        (y - sign, send(part, ahead)),
        (y + sign, send(part, behind)),
        (y + 2, send(part, opposite)),
    ):
        into = lax.dynamic_update_slice(into, array, ((k % Y) * SHARD, 0))
    others = swap_cores(into)
    return jnp.concatenate([choose(into, others), choose(others, into)])[:NOCC].astype(f32).T


def solution(mesh):
    in_specs = (
        P("aux", "row", None, None),
        P("aux", "row"),
        P("aux", "row"),
        P("aux", "row"),
        P(("aux", "row"), None),
        P(("aux", "row"), None),
    )
    out_specs = P("row", None)
    return jax.shard_map(local, mesh=mesh, in_specs=in_specs, out_specs=out_specs, check_vma=False)
```

```python
import itertools

import jax
import jax.numpy as jnp
from jax import lax
from jax.experimental import pallas as pl
from jax.experimental.pallas import tpu as pltpu
from jax.sharding import PartitionSpec as P

Y, ZH, CORE, X, ZL = 4, 2, 2, 4, 2
AXES = ("aux", "row")
BLK = 128
ROW_BLOCKS = 6
ROWS = ROW_BLOCKS * BLK
GROUPS = 2 * ROW_BLOCKS
SLOTS = 96
NB = 6144
NOCC = 800
WIDE = 896
SHARD = WIDE // 8
OWN = 48
STEP = 4
UNROLL = 3
FLIGHT = 5
MAIN = 32
bf16, f32 = jnp.bfloat16, jnp.float32


def permutation(move):
    pairs = []
    for y, zh, c, x, zl in itertools.product(range(Y), range(ZH), range(CORE), range(X), range(ZL)):
        at = dict(y=y, z=zh * ZL + zl, c=c, x=x)
        to = move(dict(at))

        def flat(d):
            return (((d["y"] * ZH + d["z"] // ZL) * CORE + d["c"]) * X + d["x"]) * ZL + d["z"] % ZL

        pairs.append((flat(at), flat(to)))
    return pairs


def around(axes, by, mirror):
    def move(d):
        axis = axes[d["c"]]
        d[axis] = (d[axis] + (-by if mirror and d["c"] else by)) % 4
        return d

    return permutation(move)


def other_core(d):
    d["c"] = 1 - d["c"]
    return d


def other_low(d):
    d["z"] = d["z"] ^ 1
    return d


def other_high(d):
    d["z"] = d["z"] ^ 2
    return d


def send(array, pairs):
    return lax.ppermute(array, AXES, pairs)


def swap_cores(array):
    return send(array, permutation(other_core))


def swap_low(array):
    return send(array, permutation(other_low))


def swap_high(array):
    return send(array, permutation(other_high))


def slab_kernel(place, main0, main1, rest, out, sems):
    core, row = place[0], place[1]
    copies = []
    for x in range(X):
        a = jnp.where(core == 0, x, row // ZL)
        b = jnp.where(core == 0, row // ZL, x)
        for c, main in enumerate((main0, main1)):
            copies.append(
                pltpu.make_async_copy(main.at[b, row % ZL, :, a], out.at[c, x, :, pl.ds(0, MAIN)], sems.at[3 * x + c])
            )
        copies.append(
            pltpu.make_async_copy(
                rest.at[row % ZL, :, :, a, b], out.at[:, x, :, pl.ds(MAIN, OWN - MAIN)], sems.at[3 * x + 2]
            )
        )
    for copy in copies:
        copy.start()
    for copy in copies:
        copy.wait()


def own_slab(place, main0, main1, rest):
    return pl.pallas_call(
        slab_kernel,
        out_shape=jax.ShapeDtypeStruct((CORE, X, ZL, OWN, WIDE), bf16),
        in_specs=[pl.BlockSpec(memory_space=pltpu.SMEM)] + [pl.BlockSpec(memory_space=pl.ANY)] * 3,
        out_specs=pl.BlockSpec(memory_space=pltpu.VMEM),
        scratch_shapes=[pltpu.SemaphoreType.DMA((3 * X,))],
        compiler_params=pltpu.CompilerParams(vmem_limit_bytes=4 * 1024 * 1024),
        name="slab",
    )(place, main0, main1, rest)


def multiply_kernel(place, meta, own_blocks, other_blocks, main0, main1, rest, out, *scratch):
    blocks, held, total, order, counts, steps, sems = scratch
    core = place[0]
    copies = [
        pltpu.make_async_copy(own_blocks, blocks.at[pl.ds(0, SLOTS)], sems.at[0]),
        pltpu.make_async_copy(other_blocks, blocks.at[pl.ds(SLOTS, SLOTS)], sems.at[1]),
    ]
    for a in range(4):
        for b in range(4):
            y, x = jnp.where(core == 0, b, a), jnp.where(core == 0, a, b)
            i = 2 + 3 * (4 * a + b)
            for c, main in enumerate((main0, main1)):
                copies.append(
                    pltpu.make_async_copy(
                        main.at[b, :, :, a], held.at[y, :, c, x, :, pl.ds(0, MAIN)], sems.at[i + c]
                    )
                )
            copies.append(
                pltpu.make_async_copy(
                    rest.at[:, :, :, a, b], held.at[y, :, :, x, :, pl.ds(MAIN, OWN - MAIN)], sems.at[i + 2]
                )
            )
    for copy in copies:
        copy.start()
    blocks[2 * SLOTS] = jnp.zeros((BLK, BLK), bf16)

    def clear(i, carry):
        counts[i] = 0
        total[i] = jnp.zeros((BLK, WIDE), f32)
        return carry

    lax.fori_loop(0, GROUPS + 1, clear, 0)
    for q in range(2):

        def put(s, carry):
            group = q * ROW_BLOCKS + meta[q, s]
            n = counts[group]
            order[group, n] = s + q * SLOTS
            counts[group] = n + 1
            return carry

        lax.fori_loop(0, meta[q, 2 * SLOTS], put, 0)

    def list_group(group, base):
        n = counts[group]
        for i in range(STEP):
            order[group, n + i] = 2 * SLOTS
        many = (n + STEP - 1) // STEP

        def list_step(i, carry):
            steps[base + i, 0] = group
            for k in range(STEP):
                s = order[group, i * STEP + k]
                q = jnp.minimum(s // SLOTS, 1)
                steps[base + i, 1 + k] = s
                steps[base + i, 1 + STEP + k] = jnp.where(s < 2 * SLOTS, meta[q, SLOTS + s - q * SLOTS], 0)
            return carry

        lax.fori_loop(0, many, list_step, 0)
        return base + many

    many = lax.fori_loop(0, GROUPS, list_group, 0)
    for u in range(UNROLL - 1):
        steps[many + u, 0] = GROUPS
        for k in range(STEP):
            steps[many + u, 1 + k] = 2 * SLOTS
            steps[many + u, 1 + STEP + k] = 0
    for copy in copies:
        copy.wait()
    panels = held.reshape(NB, WIDE)

    def some(i, carry):
        products = []
        for u in range(UNROLL):
            left, right = [], []
            for k in range(STEP):
                left.append(blocks[steps[i * UNROLL + u, 1 + k]])
                column = steps[i * UNROLL + u, 1 + STEP + k]
                right.append(panels[pl.ds(pl.multiple_of(column * BLK, BLK), BLK), :])
            products.append(
                jnp.dot(jnp.concatenate(left, axis=1), jnp.concatenate(right, axis=0), preferred_element_type=f32)
            )
        for u in range(UNROLL):
            total[steps[i * UNROLL + u, 0]] += products[u]
        return carry

    lax.fori_loop(0, (many + UNROLL - 1) // UNROLL, some, 0)

    def finish(group, carry):
        q = group // ROW_BLOCKS
        start = pl.multiple_of((group - q * ROW_BLOCKS) * BLK, BLK)
        out[q, pl.ds(start, BLK), :] = total[group].astype(bf16)
        return carry

    lax.fori_loop(0, GROUPS, finish, 0)


def multiply(place, meta, own_blocks, other_blocks, main0, main1, rest):
    most = 2 * SLOTS // STEP + GROUPS + UNROLL
    return pl.pallas_call(
        multiply_kernel,
        out_shape=jax.ShapeDtypeStruct((2, ROWS, WIDE), bf16),
        in_specs=[pl.BlockSpec(memory_space=pltpu.SMEM)] * 2 + [pl.BlockSpec(memory_space=pl.ANY)] * 5,
        out_specs=pl.BlockSpec(memory_space=pltpu.VMEM),
        scratch_shapes=[
            pltpu.VMEM((2 * SLOTS + 1, BLK, BLK), bf16),
            pltpu.VMEM((Y, ZH, CORE, X, ZL, OWN, WIDE), bf16),
            pltpu.VMEM((GROUPS + 1, BLK, WIDE), f32),
            pltpu.SMEM((GROUPS, SLOTS + 2 * STEP), jnp.int32),
            pltpu.SMEM((GROUPS + 1,), jnp.int32),
            pltpu.SMEM((most, 1 + 2 * STEP), jnp.int32),
            pltpu.SemaphoreType.DMA((50,)),
        ],
        compiler_params=pltpu.CompilerParams(vmem_limit_bytes=30 * 1024 * 1024),
        cost_estimate=pl.CostEstimate(flops=2 * 96 * 2 * 128 * 128 * 896, bytes_accessed=2**24, transcendentals=0),
        name="multiply",
    )(place, meta, own_blocks, other_blocks, main0, main1, rest)


def cross_kernel(q, starts, place, half, slab, theirs, *refs):
    outs, used, product = refs[:-2], refs[-2], refs[-1]
    core, row = place[0], place[1]
    used[...] = jnp.where(core == 0, slab[...], theirs[...])
    product[...] = lax.dot_general(
        half[q], used[...], (((0,), (0,)), ((), ())), preferred_element_type=f32
    ).astype(bf16)
    value = jnp.sum(half[q].astype(f32) * theirs[...].astype(f32), keepdims=True)
    high = value.astype(bf16).astype(f32)
    middle = (value - high).astype(bf16).astype(f32)
    low = value - high - middle
    lane = lax.broadcasted_iota(jnp.int32, (16, WIDE), 1)
    line = lax.broadcasted_iota(jnp.int32, (16, WIDE), 0)
    coded = jnp.where(
        lane == 3 * row, high, jnp.where(lane == 3 * row + 1, middle, jnp.where(lane == 3 * row + 2, low, 0.0))
    )
    product[NOCC : NOCC + 16, :] = jnp.where(line == 0, coded, 0.0).astype(bf16)
    for out, start in zip(outs, starts):
        n = out.shape[0]
        out[...] = product[pl.ds(pl.multiple_of(place[start] * n, n), n), :]


def cross(q, starts, n, place, half, slab, theirs):
    def kernel(*refs):
        cross_kernel(q, starts, *refs)

    return pl.pallas_call(
        kernel,
        out_shape=[jax.ShapeDtypeStruct((n, WIDE), bf16)] * len(starts),
        in_specs=[pl.BlockSpec(memory_space=pltpu.SMEM)] + [pl.BlockSpec(memory_space=pltpu.VMEM)] * 3,
        out_specs=[pl.BlockSpec(memory_space=pltpu.VMEM)] * len(starts),
        scratch_shapes=[pltpu.VMEM((ROWS, WIDE), bf16), pltpu.VMEM((WIDE, WIDE), bf16)],
        compiler_params=pltpu.CompilerParams(vmem_limit_bytes=30 * 1024 * 1024),
        cost_estimate=pl.CostEstimate(flops=2 * 768 * 896 * 896, bytes_accessed=2**23, transcendentals=0),
        name="cross",
    )(place, half, slab, theirs)


def exchange_kernel(place, half, first, second, keep, give, turned):
    core = place[0]
    total = None
    for q, weight in enumerate((first, second)):
        line = lax.broadcasted_iota(jnp.int32, (16, WIDE), 0)
        codes = jnp.where(line < 2, weight[NOCC : NOCC + 16, :].astype(f32), 0.0)
        coulomb = jnp.sum(codes, keepdims=True) * (1.0 / NB)
        factor = jnp.where(core == 0, 2.0 * coulomb, 0.0)
        own = half[q]
        term = factor * own.astype(f32) - jnp.dot(own, weight[...], preferred_element_type=f32)
        total = term if total is None else total + term
    turned[...] = total.T
    n = WIDE // 2
    keep[...] = turned[pl.ds(pl.multiple_of(core * n, n), n), :]
    give[...] = turned[pl.ds(pl.multiple_of((1 - core) * n, n), n), :]


def exchange(place, half, first, second):
    return pl.pallas_call(
        exchange_kernel,
        out_shape=[jax.ShapeDtypeStruct((WIDE // 2, ROWS), f32)] * 2,
        in_specs=[pl.BlockSpec(memory_space=pltpu.SMEM)] + [pl.BlockSpec(memory_space=pltpu.VMEM)] * 3,
        out_specs=[pl.BlockSpec(memory_space=pltpu.VMEM)] * 2,
        scratch_shapes=[pltpu.VMEM((WIDE, ROWS), f32)],
        compiler_params=pltpu.CompilerParams(vmem_limit_bytes=36 * 1024 * 1024),
        cost_estimate=pl.CostEstimate(flops=4 * 768 * 896 * 896, bytes_accessed=2**23, transcendentals=0),
        name="exchange",
    )(place, half, first, second)


def local(factors, block_rows, block_cols, block_count, orbitals, response):
    aux, row = lax.axis_index("aux"), lax.axis_index("row")
    y, zh, c = aux // (ZH * CORE), (aux // CORE) % ZH, aux % CORE
    x, zl = row // ZL, row % ZL
    z = zh * ZL + zl
    sign = 1 - 2 * c
    first = c == 0

    def choose(a, b):
        return jnp.where(first, a, b)

    flying = []

    def send_next(array, pairs):
        if len(flying) >= FLIGHT:
            array, _ = lax.optimization_barrier((array, flying[-FLIGHT]))
        got = send(array, pairs)
        flying.append(got)
        return got

    def put(into, array, **at):
        index = [jnp.int32(0)] * into.ndim
        for dim, i in at.items():
            index[int(dim[1:])] = i
        return lax.dynamic_update_slice(into, array, index)

    got = send(choose(response, orbitals), permutation(other_core))
    own_blocks = factors[0]
    other_blocks = swap_cores(own_blocks)
    both = jnp.stack([choose(orbitals, got), choose(got, response)])
    both = jnp.pad(both, ((0, 0), (0, 0), (0, WIDE - NOCC)))

    one, two = ("x", "y"), ("y", "x")
    at_one, at_two = choose(x, y), choose(y, x)
    shape = (CORE, 4, OWN, WIDE)
    stage = put(jnp.zeros(shape, bf16), both[:, None], d1=at_one)
    ahead = send_next(both, around(one, 1, False))
    behind = send_next(both, around(one, -1, False))
    far = send_next(both, around(one, 2, False))
    lists = jnp.concatenate([block_rows[0] % ROW_BLOCKS, block_cols[0], block_count[0]])
    lists = jnp.pad(lists, (0, 256 - 2 * SLOTS - 1))[None]
    meta = jnp.concatenate([lists, swap_cores(lists)])
    place = jnp.stack([c, row, x, (x + sign) % 4, (x - sign) % 4, (x + 2) % 4, zl, 1 - zl]).astype(jnp.int32)
    stage = put(stage, ahead[:, None], d1=(at_one - 1) % 4)
    stage = put(stage, behind[:, None], d1=(at_one + 1) % 4)
    stage = put(stage, far[:, None], d1=(at_one + 2) % 4)
    stage, other_blocks, meta = lax.optimization_barrier((stage, other_blocks, meta))

    main, rest = stage[:, :, :MAIN], stage[:, :, MAIN:]
    zz = ("z", "z")
    main_ahead = send_next(main, around(zz, 1, True))
    main_behind = send_next(main, around(zz, -1, True))
    rest_ahead = send_next(rest, around(two, 1, False))
    rest_behind = send_next(rest, around(two, -1, False))
    main_far = send_next(main_ahead, around(zz, 1, True))
    rest_far = send_next(rest, around(two, 2, False))

    mains = [jnp.zeros((ZH, ZL, 4, MAIN, WIDE), bf16)] * 2
    for array, at in (
        (main, z),
        (main_ahead, (z - sign) % 4),
        (main_behind, (z + sign) % 4),
        (main_far, (z + 2) % 4),
    ):
        mains = [put(into, array[i][None, None], d0=at // ZL, d1=at % ZL) for i, into in enumerate(mains)]
    into = jnp.zeros((CORE, 4, 4, OWN - MAIN, WIDE), bf16)
    for array, at in (
        (rest, at_two),
        (rest_ahead, (at_two - 1) % 4),
        (rest_behind, (at_two + 1) % 4),
        (rest_far, (at_two + 2) % 4),
    ):
        into = put(into, array[:, :, None], d2=at)
    rest = into

    ahead, behind = around(two, 1, False), around(two, -1, False)
    ahead_0 = send_next(mains[0], ahead)
    behind_1 = send_next(mains[1], behind)
    rest_ahead = send_next(rest, around(zz, 1, True))
    rest_behind = send_next(rest, around(zz, -1, True))
    ahead_1 = send_next(mains[1], ahead)
    behind_0 = send_next(mains[0], behind)
    far_0 = send_next(ahead_0, ahead)
    far_1 = send_next(behind_1, behind)
    rest_far = send_next(rest_ahead, around(zz, 1, True))
    arrays = (
        (mains[0], ahead_0, behind_0, far_0),
        (mains[1], ahead_1, behind_1, far_1),
    )
    mains = []
    for four in arrays:
        into = jnp.zeros((4, *four[0].shape), bf16)
        for array, at in zip(four, (at_two, (at_two - 1) % 4, (at_two + 1) % 4, (at_two + 2) % 4)):
            into = put(into, array[None], d0=at)
        mains.append(into)
    into = jnp.zeros((ZH, CORE, ZL, 4, 4, OWN - MAIN, WIDE), bf16)
    for array, at in (
        (rest, z),
        (rest_ahead, (z - sign) % 4),
        (rest_behind, (z + sign) % 4),
        (rest_far, (z + 2) % 4),
    ):
        into = put(into, array[None, :, None], d0=at // ZL, d2=at % ZL)
    rest = into

    slab = own_slab(place, *mains, rest).reshape(ROWS, WIDE)
    theirs = swap_cores(slab)
    half = multiply(place, meta, own_blocks, other_blocks, *mains, rest)

    def add(*arrays):
        return sum(a.astype(f32) for a in arrays)

    def rows_of(array, k, n):
        return lax.dynamic_slice(array, (k * n, 0), (n, array.shape[1]))

    xx = ("x", "x")
    ahead, behind = around(xx, 1, True), around(xx, -1, True)
    opposite = around(xx, 2, True)
    half_mine, to_low = cross(1, (6, 7), WIDE // 2, place, half, slab, theirs)
    from_low = swap_low(to_low)
    mine, to_ahead, to_behind, to_far = cross(0, (2, 3, 4, 5), WIDE // 4, place, half, slab, theirs)
    parts = (mine, send(to_ahead, ahead), send(to_behind, behind), send(to_far, opposite))
    half_mine = add(half_mine, from_low).astype(bf16)
    second = (
        rows_of(half_mine, x, SHARD),
        send(rows_of(half_mine, (x + sign) % 4, SHARD), ahead),
        send(rows_of(half_mine, (x - sign) % 4, SHARD), behind),
        send(rows_of(half_mine, (x + 2) % 4, SHARD), opposite),
    )
    parts, half_mine = lax.optimization_barrier((parts, half_mine))
    mine = add(*parts).astype(bf16)
    shards = [add(rows_of(mine, zl, SHARD), swap_low(rows_of(mine, 1 - zl, SHARD))), add(*second)]

    last = (x == X - 1) & (zl == ZL - 1)
    at = jnp.arange(SHARD, dtype=jnp.int32)[:, None] + (WIDE - SHARD)
    shards = [jnp.where(last & (at == NOCC), s, s * (1.0 / NB)).astype(bf16) for s in shards]
    code = [s[NOCC - (WIDE - SHARD)] for s in shards]
    other_shards = swap_cores(jnp.stack(shards))
    here = last & (at == NOCC + 1)
    by_x = jnp.where(here, code[1][None], other_shards[0])
    by_low = jnp.where(here, code[0][None], other_shards[1])

    def gather_x(array):
        n = array.shape[0]
        into = jnp.zeros((n * X, WIDE), bf16)
        for k, part in (
            (x, array),
            (x - sign, send(array, ahead)),
            (x + sign, send(array, behind)),
            (x + 2, send(array, opposite)),
        ):
            into = lax.dynamic_update_slice(into, part, ((k % X) * n, 0))
        return into

    def gather_low(array):
        n = array.shape[0]
        into = jnp.zeros((n * ZL, WIDE), bf16)
        into = lax.dynamic_update_slice(into, array, (zl * n, 0))
        return lax.dynamic_update_slice(into, swap_low(array), ((1 - zl) * n, 0))

    keep, give = exchange(place, half, gather_low(gather_x(by_low)), gather_x(gather_low(by_x)))

    yy = ("y", "y")
    ahead, behind, opposite = around(yy, 1, True), around(yy, -1, True), around(yy, 2, True)
    mine = keep + swap_cores(give)

    def quarter(k):
        return rows_of(mine, k % Y, SHARD)

    part = quarter(y) + add(
        send(quarter(y + sign).astype(bf16), ahead),
        send(quarter(y - sign).astype(bf16), behind),
        send(quarter(y + 2).astype(bf16), opposite),
    )
    part = (part + swap_high(part)).astype(bf16)
    into = jnp.zeros((WIDE // 2, ROWS), bf16)
    for k, array in (
        (y, part),
        (y - sign, send(part, ahead)),
        (y + sign, send(part, behind)),
        (y + 2, send(part, opposite)),
    ):
        into = lax.dynamic_update_slice(into, array, ((k % Y) * SHARD, 0))
    others = swap_cores(into)
    return jnp.concatenate([choose(into, others), choose(others, into)])[:NOCC].astype(f32).T


def solution(mesh):
    in_specs = (
        P("aux", "row", None, None),
        P("aux", "row"),
        P("aux", "row"),
        P("aux", "row"),
        P(("aux", "row"), None),
        P(("aux", "row"), None),
    )
    out_specs = P("row", None)
    return jax.shard_map(local, mesh=mesh, in_specs=in_specs, out_specs=out_specs, check_vma=False)
```

```python
import itertools

import jax
import jax.numpy as jnp
from jax import lax
from jax.experimental import pallas as pl
from jax.experimental.pallas import tpu as pltpu
from jax.sharding import PartitionSpec as P

Y, ZH, CORE, X, ZL = 4, 2, 2, 4, 2
AXES = ("aux", "row")
BLK = 128
ROW_BLOCKS = 6
ROWS = ROW_BLOCKS * BLK
GROUPS = 2 * ROW_BLOCKS
SLOTS = 96
NB = 6144
NOCC = 800
WIDE = 896
CROSS = 832
SHARD = CROSS // 8
OWN = 48
STEP = 4
UNROLL = 3
MAIN = 32
bf16, f32 = jnp.bfloat16, jnp.float32


def permutation(move):
    pairs = []
    for y, zh, c, x, zl in itertools.product(range(Y), range(ZH), range(CORE), range(X), range(ZL)):
        at = dict(y=y, z=zh * ZL + zl, c=c, x=x)
        to = move(dict(at))

        def flat(d):
            return (((d["y"] * ZH + d["z"] // ZL) * CORE + d["c"]) * X + d["x"]) * ZL + d["z"] % ZL

        pairs.append((flat(at), flat(to)))
    return pairs


def around(axes, by, mirror):
    def move(d):
        axis = axes[d["c"]]
        d[axis] = (d[axis] + (-by if mirror and d["c"] else by)) % 4
        return d

    return permutation(move)


def other_core(d):
    d["c"] = 1 - d["c"]
    return d


def other_low(d):
    d["z"] = d["z"] ^ 1
    return d


def other_high(d):
    d["z"] = d["z"] ^ 2
    return d


def send(array, pairs):
    return lax.ppermute(array, AXES, pairs)


def swap_cores(array):
    return send(array, permutation(other_core))


def swap_low(array):
    return send(array, permutation(other_low))


def swap_high(array):
    return send(array, permutation(other_high))


def here():
    aux, row = lax.axis_index("aux"), lax.axis_index("row")
    return aux % CORE, row, row // ZL, row % ZL


def slab_kernel(main0, main1, rest, out, sems):
    core, row, _, _ = here()
    copies = []
    for x in range(X):
        a = jnp.where(core == 0, x, row // ZL)
        b = jnp.where(core == 0, row // ZL, x)
        for c, main in enumerate((main0, main1)):
            copies.append(
                pltpu.make_async_copy(main.at[b, row % ZL, :, a], out.at[c, x, :, pl.ds(0, MAIN)], sems.at[3 * x + c])
            )
        copies.append(
            pltpu.make_async_copy(
                rest.at[row % ZL, :, :, a, b], out.at[:, x, :, pl.ds(MAIN, OWN - MAIN)], sems.at[3 * x + 2]
            )
        )
    for copy in copies:
        copy.start()
    for copy in copies:
        copy.wait()


def own_slab(main0, main1, rest):
    return pl.pallas_call(
        slab_kernel,
        out_shape=jax.ShapeDtypeStruct((CORE, X, ZL, OWN, WIDE), bf16),
        in_specs=[pl.BlockSpec(memory_space=pl.ANY)] * 3,
        out_specs=pl.BlockSpec(memory_space=pltpu.VMEM),
        scratch_shapes=[pltpu.SemaphoreType.DMA((3 * X,))],
        compiler_params=pltpu.CompilerParams(vmem_limit_bytes=4 * 1024 * 1024),
        name="slab",
    )(main0, main1, rest)


def multiply_kernel(meta, own_blocks, other_blocks, main0, main1, rest, out, *scratch):
    blocks, held, total, order, counts, steps, sems = scratch
    core, _, _, _ = here()
    copies = [
        pltpu.make_async_copy(own_blocks, blocks.at[pl.ds(0, SLOTS)], sems.at[0]),
        pltpu.make_async_copy(other_blocks, blocks.at[pl.ds(SLOTS, SLOTS)], sems.at[1]),
    ]
    for a in range(4):
        for b in range(4):
            y, x = jnp.where(core == 0, b, a), jnp.where(core == 0, a, b)
            i = 2 + 3 * (4 * a + b)
            for c, main in enumerate((main0, main1)):
                copies.append(
                    pltpu.make_async_copy(
                        main.at[b, :, :, a], held.at[y, :, c, x, :, pl.ds(0, MAIN)], sems.at[i + c]
                    )
                )
            copies.append(
                pltpu.make_async_copy(
                    rest.at[:, :, :, a, b], held.at[y, :, :, x, :, pl.ds(MAIN, OWN - MAIN)], sems.at[i + 2]
                )
            )
    for copy in copies:
        copy.start()
    blocks[2 * SLOTS] = jnp.zeros((BLK, BLK), bf16)

    def clear(i, carry):
        counts[i] = 0
        total[i] = jnp.zeros((BLK, WIDE), f32)
        return carry

    lax.fori_loop(0, GROUPS + 1, clear, 0)
    for q in range(2):

        def put(s, carry):
            group = q * ROW_BLOCKS + meta[q, s]
            n = counts[group]
            order[group, n] = s + q * SLOTS
            counts[group] = n + 1
            return carry

        lax.fori_loop(0, meta[q, 2 * SLOTS], put, 0)

    def list_group(group, base):
        n = counts[group]
        for i in range(STEP):
            order[group, n + i] = 2 * SLOTS
        many = (n + STEP - 1) // STEP

        def list_step(i, carry):
            steps[base + i, 0] = group
            for k in range(STEP):
                s = order[group, i * STEP + k]
                q = jnp.minimum(s // SLOTS, 1)
                steps[base + i, 1 + k] = s
                steps[base + i, 1 + STEP + k] = jnp.where(s < 2 * SLOTS, meta[q, SLOTS + s - q * SLOTS], 0)
            return carry

        lax.fori_loop(0, many, list_step, 0)
        return base + many

    many = lax.fori_loop(0, GROUPS, list_group, 0)
    for u in range(UNROLL - 1):
        steps[many + u, 0] = GROUPS
        for k in range(STEP):
            steps[many + u, 1 + k] = 2 * SLOTS
            steps[many + u, 1 + STEP + k] = 0
    for copy in copies:
        copy.wait()
    panels = held.reshape(NB, WIDE)

    def some(i, carry):
        products = []
        for u in range(UNROLL):
            left, right = [], []
            for k in range(STEP):
                left.append(blocks[steps[i * UNROLL + u, 1 + k]])
                column = steps[i * UNROLL + u, 1 + STEP + k]
                right.append(panels[pl.ds(pl.multiple_of(column * BLK, BLK), BLK), :])
            products.append(
                jnp.dot(jnp.concatenate(left, axis=1), jnp.concatenate(right, axis=0), preferred_element_type=f32)
            )
        for u in range(UNROLL):
            total[steps[i * UNROLL + u, 0]] += products[u]
        return carry

    lax.fori_loop(0, (many + UNROLL - 1) // UNROLL, some, 0)

    def finish(group, carry):
        q = group // ROW_BLOCKS
        start = pl.multiple_of((group - q * ROW_BLOCKS) * BLK, BLK)
        out[q, pl.ds(start, BLK), :] = total[group].astype(bf16)
        return carry

    lax.fori_loop(0, GROUPS, finish, 0)


def multiply(meta, own_blocks, other_blocks, main0, main1, rest):
    most = 2 * SLOTS // STEP + GROUPS + UNROLL
    return pl.pallas_call(
        multiply_kernel,
        out_shape=jax.ShapeDtypeStruct((2, ROWS, WIDE), bf16),
        in_specs=[pl.BlockSpec(memory_space=pltpu.SMEM)] + [pl.BlockSpec(memory_space=pl.ANY)] * 5,
        out_specs=pl.BlockSpec(memory_space=pltpu.VMEM),
        scratch_shapes=[
            pltpu.VMEM((2 * SLOTS + 1, BLK, BLK), bf16),
            pltpu.VMEM((Y, ZH, CORE, X, ZL, OWN, WIDE), bf16),
            pltpu.VMEM((GROUPS + 1, BLK, WIDE), f32),
            pltpu.SMEM((GROUPS, SLOTS + 2 * STEP), jnp.int32),
            pltpu.SMEM((GROUPS + 1,), jnp.int32),
            pltpu.SMEM((most, 1 + 2 * STEP), jnp.int32),
            pltpu.SemaphoreType.DMA((50,)),
        ],
        compiler_params=pltpu.CompilerParams(vmem_limit_bytes=30 * 1024 * 1024),
        cost_estimate=pl.CostEstimate(flops=2 * 96 * 2 * 128 * 128 * 896, bytes_accessed=2**24, transcendentals=0),
        name="multiply",
    )(meta, own_blocks, other_blocks, main0, main1, rest)


def cross_kernel(q, starts, half, slab, theirs, *refs):
    outs, used, product = refs[:-2], refs[-2], refs[-1]
    core, row, _, _ = here()
    used[...] = jnp.where(core == 0, slab[...], theirs[...])
    product[...] = lax.dot_general(
        half[q], used[...], (((0,), (0,)), ((), ())), preferred_element_type=f32
    ).astype(bf16)
    value = jnp.sum(half[q].astype(f32) * theirs[...].astype(f32), keepdims=True)
    high = value.astype(bf16).astype(f32)
    middle = (value - high).astype(bf16).astype(f32)
    low = value - high - middle
    lane = lax.broadcasted_iota(jnp.int32, (16, WIDE), 1)
    line = lax.broadcasted_iota(jnp.int32, (16, WIDE), 0)
    coded = jnp.where(
        lane == 3 * row, high, jnp.where(lane == 3 * row + 1, middle, jnp.where(lane == 3 * row + 2, low, 0.0))
    )
    product[NOCC : NOCC + 16, :] = jnp.where(line == 0, coded, 0.0).astype(bf16)
    for out, start in zip(outs, starts()):
        n = out.shape[0]
        out[...] = product[pl.ds(pl.multiple_of(start * n, n), n), :]


def chunks_x():
    core, _, x, _ = here()
    return x, (x + 1 - 2 * core) % X, (x - 1 + 2 * core) % X, (x + 2) % X


def chunks_low():
    zl = here()[3]
    return zl, 1 - zl


def cross(q, starts, many, half, slab, theirs):
    def kernel(*refs):
        cross_kernel(q, starts, *refs)

    return pl.pallas_call(
        kernel,
        out_shape=[jax.ShapeDtypeStruct((CROSS // many, WIDE), bf16)] * many,
        in_specs=[pl.BlockSpec(memory_space=pltpu.VMEM)] * 3,
        out_specs=[pl.BlockSpec(memory_space=pltpu.VMEM)] * many,
        scratch_shapes=[pltpu.VMEM((ROWS, WIDE), bf16), pltpu.VMEM((WIDE, WIDE), bf16)],
        compiler_params=pltpu.CompilerParams(vmem_limit_bytes=30 * 1024 * 1024),
        cost_estimate=pl.CostEstimate(flops=2 * 768 * 896 * 896, bytes_accessed=2**23, transcendentals=0),
        name="cross",
    )(half, slab, theirs)


def exchange_kernel(half, *refs):
    parts, (keep, give, weights, turned, sems) = refs[:6], refs[6:]
    core, _, _, _ = here()
    copies = []
    for i, (q, at) in enumerate([(0, at) for at in chunks_low()] + [(1, at) for at in chunks_arrived()]):
        n = parts[i].shape[0]
        into = weights.at[q, pl.ds(pl.multiple_of(at * n, n), n), :]
        copies.append(pltpu.make_async_copy(parts[i], into, sems.at[i]))
    for copy in copies:
        copy.start()
    for q in range(2):
        weights[q, CROSS:, :] = jnp.zeros((WIDE - CROSS, WIDE), bf16)
    for copy in copies:
        copy.wait()
    line = lax.broadcasted_iota(jnp.int32, (16, WIDE), 0)
    total = None
    for q in range(2):
        codes = jnp.where(line == 0, weights[q, NOCC : NOCC + 16, :].astype(f32), 0.0)
        codes = codes + jnp.where(line == 1, weights[1 - q, NOCC : NOCC + 16, :].astype(f32), 0.0)
        coulomb = jnp.sum(codes, keepdims=True) * (1.0 / NB)
        factor = jnp.where(core == 0, 2.0 * coulomb, 0.0)
        own = half[q]
        term = factor * own.astype(f32) - jnp.dot(own, weights[q], preferred_element_type=f32)
        total = term if total is None else total + term
    turned[...] = total.T
    n = CROSS // 2
    keep[...] = turned[pl.ds(pl.multiple_of(core * n, n), n), :]
    give[...] = turned[pl.ds(pl.multiple_of((1 - core) * n, n), n), :]


def chunks_arrived():
    x, ahead, behind, far = chunks_x()
    return x, behind, ahead, far


def exchange(half, low_parts, x_parts):
    return pl.pallas_call(
        exchange_kernel,
        out_shape=[jax.ShapeDtypeStruct((CROSS // 2, ROWS), f32)] * 2,
        in_specs=[pl.BlockSpec(memory_space=pltpu.VMEM)] + [pl.BlockSpec(memory_space=pl.ANY)] * 6,
        out_specs=[pl.BlockSpec(memory_space=pltpu.VMEM)] * 2,
        scratch_shapes=[
            pltpu.VMEM((2, WIDE, WIDE), bf16),
            pltpu.VMEM((WIDE, ROWS), f32),
            pltpu.SemaphoreType.DMA((6,)),
        ],
        compiler_params=pltpu.CompilerParams(vmem_limit_bytes=36 * 1024 * 1024),
        cost_estimate=pl.CostEstimate(flops=4 * 768 * 896 * 896, bytes_accessed=2**23, transcendentals=0),
        name="exchange",
    )(half, *low_parts, *x_parts)


def local(factors, block_rows, block_cols, block_count, orbitals, response):
    aux, row = lax.axis_index("aux"), lax.axis_index("row")
    y, zh, c = aux // (ZH * CORE), (aux // CORE) % ZH, aux % CORE
    x, zl = row // ZL, row % ZL
    z = zh * ZL + zl
    sign = 1 - 2 * c
    first = c == 0

    def choose(a, b):
        return jnp.where(first, a, b)

    def send_after(array, pairs, *earlier):
        return send(lax.optimization_barrier((array, *earlier))[0], pairs)

    def put(into, array, **at):
        index = [jnp.int32(0)] * into.ndim
        for dim, i in at.items():
            index[int(dim[1:])] = i
        return lax.dynamic_update_slice(into, array, index)

    got = send(choose(response, orbitals), permutation(other_core))
    own_blocks = factors[0]
    other_blocks = send_after(own_blocks, permutation(other_core), got)
    both = jnp.stack([choose(orbitals, got), choose(got, response)])
    both = jnp.pad(both, ((0, 0), (0, 0), (0, WIDE - NOCC)))

    one, two = ("x", "y"), ("y", "x")
    at_one, at_two = choose(x, y), choose(y, x)
    shape = (CORE, 4, OWN, WIDE)
    stage = put(jnp.zeros(shape, bf16), both[:, None], d1=at_one)
    ahead = send(both, around(one, 1, False))
    behind = send(both, around(one, -1, False))
    far = send(both, around(one, 2, False))
    lists = jnp.concatenate([block_rows[0] % ROW_BLOCKS, block_cols[0], block_count[0]])
    lists = jnp.pad(lists, (0, 256 - 2 * SLOTS - 1))[None]
    meta = jnp.concatenate([lists, swap_cores(lists)])
    stage = put(stage, ahead[:, None], d1=(at_one - 1) % 4)
    stage = put(stage, behind[:, None], d1=(at_one + 1) % 4)
    stage = put(stage, far[:, None], d1=(at_one + 2) % 4)
    stage, other_blocks, meta = lax.optimization_barrier((stage, other_blocks, meta))

    main, rest = stage[:, :, :MAIN], stage[:, :, MAIN:]
    zz = ("z", "z")
    main_ahead = send(main, around(zz, 1, True))
    rest_ahead = send(rest, around(two, 1, False))
    rest_behind = send(rest, around(two, -1, False))
    main_far = send(main_ahead, around(zz, 1, True))
    main_behind = send_after(main, around(zz, -1, True), main_ahead)
    rest_far = send_after(rest, around(two, 2, False), rest_ahead)

    mains = [jnp.zeros((ZH, ZL, 4, MAIN, WIDE), bf16)] * 2
    for array, at in (
        (main, z),
        (main_ahead, (z - sign) % 4),
        (main_behind, (z + sign) % 4),
        (main_far, (z + 2) % 4),
    ):
        mains = [put(into, array[i][None, None], d0=at // ZL, d1=at % ZL) for i, into in enumerate(mains)]
    into = jnp.zeros((CORE, 4, 4, OWN - MAIN, WIDE), bf16)
    for array, at in (
        (rest, at_two),
        (rest_ahead, (at_two - 1) % 4),
        (rest_behind, (at_two + 1) % 4),
        (rest_far, (at_two + 2) % 4),
    ):
        into = put(into, array[:, :, None], d2=at)
    rest = into

    ahead, behind = around(two, 1, False), around(two, -1, False)
    mains, rest = lax.optimization_barrier((mains, rest))
    ahead_0 = send(mains[0], ahead)
    behind_1 = send(mains[1], behind)
    rest_ahead = send(rest, around(zz, 1, True))
    rest_behind = send(rest, around(zz, -1, True))
    ahead_1 = send_after(mains[1], ahead, ahead_0)
    behind_0 = send_after(mains[0], behind, behind_1)
    far_0 = send(ahead_0, ahead)
    far_1 = send_after(behind_1, behind, rest_ahead)
    rest_far = send_after(rest_ahead, around(zz, 1, True), rest_behind)
    arrays = (
        (mains[0], ahead_0, behind_0, far_0),
        (mains[1], ahead_1, behind_1, far_1),
    )
    mains = []
    for four in arrays:
        into = jnp.zeros((4, *four[0].shape), bf16)
        for array, at in zip(four, (at_two, (at_two - 1) % 4, (at_two + 1) % 4, (at_two + 2) % 4)):
            into = put(into, array[None], d0=at)
        mains.append(into)
    into = jnp.zeros((ZH, CORE, ZL, 4, 4, OWN - MAIN, WIDE), bf16)
    for array, at in (
        (rest, z),
        (rest_ahead, (z - sign) % 4),
        (rest_behind, (z + sign) % 4),
        (rest_far, (z + 2) % 4),
    ):
        into = put(into, array[None, :, None], d0=at // ZL, d2=at % ZL)
    rest = into

    slab = own_slab(*mains, rest).reshape(ROWS, WIDE)
    theirs = swap_cores(slab)
    half = multiply(meta, own_blocks, other_blocks, *mains, rest)

    def add(*arrays):
        return sum(a.astype(f32) for a in arrays)

    def rows_of(array, k, n):
        return lax.dynamic_slice(array, (k * n, 0), (n, array.shape[1]))

    xx = ("x", "x")
    ahead, behind = around(xx, 1, True), around(xx, -1, True)
    opposite = around(xx, 2, True)
    half_mine, to_low = cross(1, chunks_low, 2, half, slab, theirs)
    from_low = swap_low(to_low)
    mine, to_ahead, to_behind, to_far = cross(0, chunks_x, 4, half, slab, theirs)
    parts = (mine, send(to_ahead, ahead), send(to_behind, behind), send(to_far, opposite))
    half_mine = add(half_mine, from_low).astype(bf16)
    second = (
        rows_of(half_mine, x, SHARD),
        send(rows_of(half_mine, (x + sign) % 4, SHARD), ahead),
        send(rows_of(half_mine, (x - sign) % 4, SHARD), behind),
        send(rows_of(half_mine, (x + 2) % 4, SHARD), opposite),
    )
    parts, half_mine = lax.optimization_barrier((parts, half_mine))
    mine = add(*parts).astype(bf16)
    first_shard = add(rows_of(mine, zl, SHARD), swap_low(rows_of(mine, 1 - zl, SHARD)))
    second_shard = add(*second)

    last = (x == X - 1) & (zl == ZL - 1)
    at = jnp.arange(SHARD, dtype=jnp.int32)[:, None] + (CROSS - SHARD)

    def weights_of(shard):
        own = jnp.where(last & (at == NOCC), shard, shard * (1.0 / NB)).astype(bf16)
        return jnp.where(last & (at == NOCC + 1), own[NOCC - (CROSS - SHARD)][None], swap_cores(own))

    def gather_x(array):
        n = array.shape[0]
        into = jnp.zeros((n * X, WIDE), bf16)
        for k, part in zip((x, x - sign, x + sign, x + 2), parts_x(array)):
            into = lax.dynamic_update_slice(into, part, ((k % X) * n, 0))
        return into

    def parts_x(array):
        return array, send(array, ahead), send(array, behind), send(array, opposite)

    def gather_low(array):
        n = array.shape[0]
        into = jnp.zeros((n * ZL, WIDE), bf16)
        into = lax.dynamic_update_slice(into, array, (zl * n, 0))
        return lax.dynamic_update_slice(into, swap_low(array), ((1 - zl) * n, 0))

    for_second = parts_x(gather_low(weights_of(first_shard)))
    by_low = gather_x(weights_of(second_shard))
    keep, give = exchange(half, (by_low, swap_low(by_low)), for_second)

    yy = ("y", "y")
    ahead, behind, opposite = around(yy, 1, True), around(yy, -1, True), around(yy, 2, True)
    mine = keep + swap_cores(give)

    def quarter(k):
        return rows_of(mine, k % Y, SHARD)

    part = quarter(y) + add(
        send(quarter(y + sign).astype(bf16), ahead),
        send(quarter(y - sign).astype(bf16), behind),
        send(quarter(y + 2).astype(bf16), opposite),
    )
    part = (part + swap_high(part)).astype(bf16)
    into = jnp.zeros((CROSS // 2, ROWS), bf16)
    for k, array in (
        (y, part),
        (y - sign, send(part, ahead)),
        (y + sign, send(part, behind)),
        (y + 2, send(part, opposite)),
    ):
        into = lax.dynamic_update_slice(into, array, ((k % Y) * SHARD, 0))
    others = swap_cores(into)
    return jnp.concatenate([choose(into, others), choose(others, into)])[:NOCC].astype(f32).T


def solution(mesh):
    in_specs = (
        P("aux", "row", None, None),
        P("aux", "row"),
        P("aux", "row"),
        P("aux", "row"),
        P(("aux", "row"), None),
        P(("aux", "row"), None),
    )
    out_specs = P("row", None)
    return jax.shard_map(local, mesh=mesh, in_specs=in_specs, out_specs=out_specs, check_vma=False)
```

```python
import itertools

import jax
import jax.numpy as jnp
from jax import lax
from jax.experimental import pallas as pl
from jax.experimental.pallas import tpu as pltpu
from jax.sharding import PartitionSpec as P

Y, ZH, CORE, X, ZL = 4, 2, 2, 4, 2
AXES = ("aux", "row")
BLK = 128
ROW_BLOCKS = 6
ROWS = ROW_BLOCKS * BLK
SLOTS = 96
NB = 6144
NOCC = 800
WIDE = 896
CROSS = 832
SHARD = CROSS // 8
OWN = 48
STEP = 4
UNROLL = 3
MAIN = 32
bf16, f32 = jnp.bfloat16, jnp.float32


def permutation(move):
    pairs = []
    for y, zh, c, x, zl in itertools.product(range(Y), range(ZH), range(CORE), range(X), range(ZL)):
        at = dict(y=y, z=zh * ZL + zl, c=c, x=x)
        to = move(dict(at))

        def flat(d):
            return (((d["y"] * ZH + d["z"] // ZL) * CORE + d["c"]) * X + d["x"]) * ZL + d["z"] % ZL

        pairs.append((flat(at), flat(to)))
    return pairs


def around(axes, by, mirror):
    def move(d):
        axis = axes[d["c"]]
        d[axis] = (d[axis] + (-by if mirror and d["c"] else by)) % 4
        return d

    return permutation(move)


def other_core(d):
    d["c"] = 1 - d["c"]
    return d


def other_low(d):
    d["z"] = d["z"] ^ 1
    return d


def other_high(d):
    d["z"] = d["z"] ^ 2
    return d


def send(array, pairs):
    return lax.ppermute(array, AXES, pairs)


def swap_cores(array):
    return send(array, permutation(other_core))


def swap_low(array):
    return send(array, permutation(other_low))


def swap_high(array):
    return send(array, permutation(other_high))


def here():
    aux, row = lax.axis_index("aux"), lax.axis_index("row")
    return aux % CORE, row, row // ZL, row % ZL


def slab_kernel(main0, main1, rest, out, sems):
    core, row, _, _ = here()
    copies = []
    for x in range(X):
        a = jnp.where(core == 0, x, row // ZL)
        b = jnp.where(core == 0, row // ZL, x)
        for c, main in enumerate((main0, main1)):
            copies.append(
                pltpu.make_async_copy(main.at[b, row % ZL, :, a], out.at[c, x, :, pl.ds(0, MAIN)], sems.at[3 * x + c])
            )
        copies.append(
            pltpu.make_async_copy(
                rest.at[row % ZL, :, :, a, b], out.at[:, x, :, pl.ds(MAIN, OWN - MAIN)], sems.at[3 * x + 2]
            )
        )
    for copy in copies:
        copy.start()
    for copy in copies:
        copy.wait()


def own_slab(main0, main1, rest):
    return pl.pallas_call(
        slab_kernel,
        out_shape=jax.ShapeDtypeStruct((CORE, X, ZL, OWN, WIDE), bf16),
        in_specs=[pl.BlockSpec(memory_space=pl.ANY)] * 3,
        out_specs=pl.BlockSpec(memory_space=pltpu.VMEM),
        scratch_shapes=[pltpu.SemaphoreType.DMA((3 * X,))],
        compiler_params=pltpu.CompilerParams(vmem_limit_bytes=4 * 1024 * 1024),
        name="slab",
    )(main0, main1, rest)


def assemble(main0, main1, rest, held, sems):
    core = here()[0]
    copies = []
    for a in range(4):
        for b in range(4):
            y, x = jnp.where(core == 0, b, a), jnp.where(core == 0, a, b)
            i = 3 * (4 * a + b)
            for c, main in enumerate((main0, main1)):
                copies.append(
                    pltpu.make_async_copy(
                        main.at[b, :, :, a], held.at[y, :, c, x, :, pl.ds(0, MAIN)], sems.at[i + c]
                    )
                )
            copies.append(
                pltpu.make_async_copy(
                    rest.at[:, :, :, a, b], held.at[y, :, :, x, :, pl.ds(MAIN, OWN - MAIN)], sems.at[i + 2]
                )
            )
    return copies


def list_steps(q, meta, order, counts, steps):
    def clear(i, carry):
        counts[i] = 0
        return carry

    lax.fori_loop(0, ROW_BLOCKS, clear, 0)

    def put(s, carry):
        group = meta[q, s]
        n = counts[group]
        order[group, n] = s
        counts[group] = n + 1
        return carry

    lax.fori_loop(0, meta[q, 2 * SLOTS], put, 0)

    def list_group(group, base):
        n = counts[group]
        for i in range(STEP):
            order[group, n + i] = SLOTS
        many = (n + STEP - 1) // STEP

        def list_step(i, carry):
            steps[base + i, 0] = group
            for k in range(STEP):
                s = order[group, i * STEP + k]
                steps[base + i, 1 + k] = s
                steps[base + i, 1 + STEP + k] = jnp.where(s < SLOTS, meta[q, SLOTS + s], 0)
            return carry

        lax.fori_loop(0, many, list_step, 0)
        return base + many

    many = lax.fori_loop(0, ROW_BLOCKS, list_group, 0)
    for u in range(UNROLL - 1):
        steps[many + u, 0] = ROW_BLOCKS
        for k in range(STEP):
            steps[many + u, 1 + k] = SLOTS
            steps[many + u, 1 + STEP + k] = 0
    return many


def multiply_kernel(q, meta, factors, *refs):
    if q == 1:
        *parts, out, held, blocks, total, order, counts, steps, sems = refs
        copies = assemble(*parts, held, sems)
    else:
        held, out, blocks, total, order, counts, steps, sems = refs
        copies = []
    copies.append(pltpu.make_async_copy(factors, blocks.at[pl.ds(0, SLOTS)], sems.at[48]))
    for copy in copies:
        copy.start()
    blocks[SLOTS] = jnp.zeros((BLK, BLK), bf16)
    total[...] = jnp.zeros_like(total)
    many = list_steps(q, meta, order, counts, steps)
    for copy in copies:
        copy.wait()
    panels = held.reshape(NB, WIDE)

    def some(i, carry):
        products = []
        for u in range(UNROLL):
            left, right = [], []
            for k in range(STEP):
                left.append(blocks[steps[i * UNROLL + u, 1 + k]])
                column = steps[i * UNROLL + u, 1 + STEP + k]
                right.append(panels[pl.ds(pl.multiple_of(column * BLK, BLK), BLK), :])
            products.append(
                jnp.dot(jnp.concatenate(left, axis=1), jnp.concatenate(right, axis=0), preferred_element_type=f32)
            )
        for u in range(UNROLL):
            total[steps[i * UNROLL + u, 0]] += products[u]
        return carry

    lax.fori_loop(0, (many + UNROLL - 1) // UNROLL, some, 0)
    for group in range(ROW_BLOCKS):
        out[group * BLK : (group + 1) * BLK, :] = total[group].astype(bf16)


def multiply(q, meta, factors, *panels):
    most = SLOTS // STEP + ROW_BLOCKS + UNROLL
    half = jax.ShapeDtypeStruct((ROWS, WIDE), bf16)
    held = jax.ShapeDtypeStruct((Y, ZH, CORE, X, ZL, OWN, WIDE), bf16)
    vmem, anywhere = pl.BlockSpec(memory_space=pltpu.VMEM), pl.BlockSpec(memory_space=pl.ANY)

    def kernel(*refs):
        multiply_kernel(q, *refs)

    return pl.pallas_call(
        kernel,
        out_shape=[half, held] if q == 1 else half,
        in_specs=[pl.BlockSpec(memory_space=pltpu.SMEM), anywhere] + ([anywhere] * 3 if q == 1 else [vmem]),
        out_specs=[vmem, vmem] if q == 1 else vmem,
        scratch_shapes=[
            pltpu.VMEM((SLOTS + 1, BLK, BLK), bf16),
            pltpu.VMEM((ROW_BLOCKS + 1, BLK, WIDE), f32),
            pltpu.SMEM((ROW_BLOCKS, SLOTS + 2 * STEP), jnp.int32),
            pltpu.SMEM((ROW_BLOCKS,), jnp.int32),
            pltpu.SMEM((most, 1 + 2 * STEP), jnp.int32),
            pltpu.SemaphoreType.DMA((49,)),
        ],
        compiler_params=pltpu.CompilerParams(vmem_limit_bytes=24 * 1024 * 1024),
        cost_estimate=pl.CostEstimate(flops=96 * 2 * 128 * 128 * 896, bytes_accessed=2**23, transcendentals=0),
        name="multiply",
    )(meta, factors, *panels)


def cross_kernel(starts, half, slab, theirs, *refs):
    outs, used, product = refs[:-2], refs[-2], refs[-1]
    core, row, _, _ = here()
    used[...] = jnp.where(core == 0, slab[...], theirs[...])
    product[...] = lax.dot_general(
        half[...], used[...], (((0,), (0,)), ((), ())), preferred_element_type=f32
    ).astype(bf16)
    value = jnp.sum(half[...].astype(f32) * theirs[...].astype(f32), keepdims=True)
    high = value.astype(bf16).astype(f32)
    middle = (value - high).astype(bf16).astype(f32)
    low = value - high - middle
    lane = lax.broadcasted_iota(jnp.int32, (16, WIDE), 1)
    line = lax.broadcasted_iota(jnp.int32, (16, WIDE), 0)
    coded = jnp.where(
        lane == 3 * row, high, jnp.where(lane == 3 * row + 1, middle, jnp.where(lane == 3 * row + 2, low, 0.0))
    )
    product[NOCC : NOCC + 16, :] = jnp.where(line == 0, coded, 0.0).astype(bf16)
    for out, start in zip(outs, starts()):
        n = out.shape[0]
        out[...] = product[pl.ds(pl.multiple_of(start * n, n), n), :]


def chunks_x():
    core, _, x, _ = here()
    return x, (x + 1 - 2 * core) % X, (x - 1 + 2 * core) % X, (x + 2) % X


def chunks_low():
    zl = here()[3]
    return zl, 1 - zl


def cross(starts, many, half, slab, theirs):
    def kernel(*refs):
        cross_kernel(starts, *refs)

    return pl.pallas_call(
        kernel,
        out_shape=[jax.ShapeDtypeStruct((CROSS // many, WIDE), bf16)] * many,
        in_specs=[pl.BlockSpec(memory_space=pltpu.VMEM)] * 3,
        out_specs=[pl.BlockSpec(memory_space=pltpu.VMEM)] * many,
        scratch_shapes=[pltpu.VMEM((ROWS, WIDE), bf16), pltpu.VMEM((WIDE, WIDE), bf16)],
        compiler_params=pltpu.CompilerParams(vmem_limit_bytes=30 * 1024 * 1024),
        cost_estimate=pl.CostEstimate(flops=2 * 768 * 896 * 896, bytes_accessed=2**23, transcendentals=0),
        name="cross",
    )(half, slab, theirs)


def exchange_kernel(*refs):
    halves, parts, (keep, give, weights, turned, sems) = refs[:2], refs[2:8], refs[8:]
    core, _, _, _ = here()
    copies = []
    for i, (q, at) in enumerate([(0, at) for at in chunks_low()] + [(1, at) for at in chunks_arrived()]):
        n = parts[i].shape[0]
        into = weights.at[q, pl.ds(pl.multiple_of(at * n, n), n), :]
        copies.append(pltpu.make_async_copy(parts[i], into, sems.at[i]))
    for copy in copies:
        copy.start()
    for q in range(2):
        weights[q, CROSS:, :] = jnp.zeros((WIDE - CROSS, WIDE), bf16)
    for copy in copies:
        copy.wait()
    line = lax.broadcasted_iota(jnp.int32, (16, WIDE), 0)
    total = None
    for q in range(2):
        codes = jnp.where(line == 0, weights[q, NOCC : NOCC + 16, :].astype(f32), 0.0)
        codes = codes + jnp.where(line == 1, weights[1 - q, NOCC : NOCC + 16, :].astype(f32), 0.0)
        coulomb = jnp.sum(codes, keepdims=True) * (1.0 / NB)
        factor = jnp.where(core == 0, 2.0 * coulomb, 0.0)
        own = halves[q][...]
        term = factor * own.astype(f32) - jnp.dot(own, weights[q], preferred_element_type=f32)
        total = term if total is None else total + term
    turned[...] = total.T
    n = CROSS // 2
    keep[...] = turned[pl.ds(pl.multiple_of(core * n, n), n), :]
    give[...] = turned[pl.ds(pl.multiple_of((1 - core) * n, n), n), :]


def chunks_arrived():
    x, ahead, behind, far = chunks_x()
    return x, behind, ahead, far


def exchange(halves, low_parts, x_parts):
    return pl.pallas_call(
        exchange_kernel,
        out_shape=[jax.ShapeDtypeStruct((CROSS // 2, ROWS), f32)] * 2,
        in_specs=[pl.BlockSpec(memory_space=pltpu.VMEM)] * 2 + [pl.BlockSpec(memory_space=pl.ANY)] * 6,
        out_specs=[pl.BlockSpec(memory_space=pltpu.VMEM)] * 2,
        scratch_shapes=[
            pltpu.VMEM((2, WIDE, WIDE), bf16),
            pltpu.VMEM((WIDE, ROWS), f32),
            pltpu.SemaphoreType.DMA((6,)),
        ],
        compiler_params=pltpu.CompilerParams(vmem_limit_bytes=36 * 1024 * 1024),
        cost_estimate=pl.CostEstimate(flops=4 * 768 * 896 * 896, bytes_accessed=2**23, transcendentals=0),
        name="exchange",
    )(*halves, *low_parts, *x_parts)


def local(factors, block_rows, block_cols, block_count, orbitals, response):
    aux, row = lax.axis_index("aux"), lax.axis_index("row")
    y, zh, c = aux // (ZH * CORE), (aux // CORE) % ZH, aux % CORE
    x, zl = row // ZL, row % ZL
    z = zh * ZL + zl
    sign = 1 - 2 * c
    first = c == 0

    def choose(a, b):
        return jnp.where(first, a, b)

    def send_after(array, pairs, *earlier):
        return send(lax.optimization_barrier((array, *earlier))[0], pairs)

    def put(into, array, **at):
        index = [jnp.int32(0)] * into.ndim
        for dim, i in at.items():
            index[int(dim[1:])] = i
        return lax.dynamic_update_slice(into, array, index)

    got = send(choose(response, orbitals), permutation(other_core))
    own_blocks = factors[0]
    other_blocks = send_after(own_blocks, permutation(other_core), got)
    both = jnp.stack([choose(orbitals, got), choose(got, response)])
    both = jnp.pad(both, ((0, 0), (0, 0), (0, WIDE - NOCC)))

    one, two = ("x", "y"), ("y", "x")
    at_one, at_two = choose(x, y), choose(y, x)
    shape = (CORE, 4, OWN, WIDE)
    stage = put(jnp.zeros(shape, bf16), both[:, None], d1=at_one)
    ahead = send(both, around(one, 1, False))
    behind = send(both, around(one, -1, False))
    far = send(both, around(one, 2, False))
    lists = jnp.concatenate([block_rows[0] % ROW_BLOCKS, block_cols[0], block_count[0]])
    lists = jnp.pad(lists, (0, 256 - 2 * SLOTS - 1))[None]
    meta = jnp.concatenate([lists, swap_cores(lists)])
    stage = put(stage, ahead[:, None], d1=(at_one - 1) % 4)
    stage = put(stage, behind[:, None], d1=(at_one + 1) % 4)
    stage = put(stage, far[:, None], d1=(at_one + 2) % 4)
    stage, other_blocks, meta = lax.optimization_barrier((stage, other_blocks, meta))

    main, rest = stage[:, :, :MAIN], stage[:, :, MAIN:]
    zz = ("z", "z")
    main_ahead = send(main, around(zz, 1, True))
    rest_ahead = send(rest, around(two, 1, False))
    rest_behind = send(rest, around(two, -1, False))
    main_far = send(main_ahead, around(zz, 1, True))
    main_behind = send_after(main, around(zz, -1, True), main_ahead)
    rest_far = send_after(rest, around(two, 2, False), rest_ahead)

    mains = [jnp.zeros((ZH, ZL, 4, MAIN, WIDE), bf16)] * 2
    for array, at in (
        (main, z),
        (main_ahead, (z - sign) % 4),
        (main_behind, (z + sign) % 4),
        (main_far, (z + 2) % 4),
    ):
        mains = [put(into, array[i][None, None], d0=at // ZL, d1=at % ZL) for i, into in enumerate(mains)]
    into = jnp.zeros((CORE, 4, 4, OWN - MAIN, WIDE), bf16)
    for array, at in (
        (rest, at_two),
        (rest_ahead, (at_two - 1) % 4),
        (rest_behind, (at_two + 1) % 4),
        (rest_far, (at_two + 2) % 4),
    ):
        into = put(into, array[:, :, None], d2=at)
    rest = into

    ahead, behind = around(two, 1, False), around(two, -1, False)
    mains, rest = lax.optimization_barrier((mains, rest))
    ahead_0 = send(mains[0], ahead)
    behind_1 = send(mains[1], behind)
    rest_ahead = send(rest, around(zz, 1, True))
    rest_behind = send(rest, around(zz, -1, True))
    ahead_1 = send_after(mains[1], ahead, ahead_0)
    behind_0 = send_after(mains[0], behind, behind_1)
    far_0 = send(ahead_0, ahead)
    far_1 = send_after(behind_1, behind, rest_ahead)
    rest_far = send_after(rest_ahead, around(zz, 1, True), rest_behind)
    arrays = (
        (mains[0], ahead_0, behind_0, far_0),
        (mains[1], ahead_1, behind_1, far_1),
    )
    mains = []
    for four in arrays:
        into = jnp.zeros((4, *four[0].shape), bf16)
        for array, at in zip(four, (at_two, (at_two - 1) % 4, (at_two + 1) % 4, (at_two + 2) % 4)):
            into = put(into, array[None], d0=at)
        mains.append(into)
    into = jnp.zeros((ZH, CORE, ZL, 4, 4, OWN - MAIN, WIDE), bf16)
    for array, at in (
        (rest, z),
        (rest_ahead, (z - sign) % 4),
        (rest_behind, (z + sign) % 4),
        (rest_far, (z + 2) % 4),
    ):
        into = put(into, array[None, :, None], d0=at // ZL, d2=at % ZL)
    rest = into

    slab = own_slab(*mains, rest).reshape(ROWS, WIDE)
    theirs = swap_cores(slab)
    second_half, panels = multiply(1, meta, other_blocks, *mains, rest)

    def add(*arrays):
        return sum(a.astype(f32) for a in arrays)

    def rows_of(array, k, n):
        return lax.dynamic_slice(array, (k * n, 0), (n, array.shape[1]))

    xx = ("x", "x")
    ahead, behind = around(xx, 1, True), around(xx, -1, True)
    opposite = around(xx, 2, True)
    half_mine, to_low = cross(chunks_low, 2, second_half, slab, theirs)
    from_low = swap_low(to_low)
    panels, half_mine = lax.optimization_barrier((panels, half_mine))
    first_half = multiply(0, meta, own_blocks, panels)
    mine, to_ahead, to_behind, to_far = cross(chunks_x, 4, first_half, slab, theirs)
    parts = (mine, send(to_ahead, ahead), send(to_behind, behind), send(to_far, opposite))
    half_mine = add(half_mine, from_low).astype(bf16)
    second = (
        rows_of(half_mine, x, SHARD),
        send(rows_of(half_mine, (x + sign) % 4, SHARD), ahead),
        send(rows_of(half_mine, (x - sign) % 4, SHARD), behind),
        send(rows_of(half_mine, (x + 2) % 4, SHARD), opposite),
    )
    parts, half_mine = lax.optimization_barrier((parts, half_mine))
    mine = add(*parts).astype(bf16)
    first_shard = add(rows_of(mine, zl, SHARD), swap_low(rows_of(mine, 1 - zl, SHARD)))
    second_shard = add(*second)

    last = (x == X - 1) & (zl == ZL - 1)
    at = jnp.arange(SHARD, dtype=jnp.int32)[:, None] + (CROSS - SHARD)

    def weights_of(shard):
        own = jnp.where(last & (at == NOCC), shard, shard * (1.0 / NB)).astype(bf16)
        return jnp.where(last & (at == NOCC + 1), own[NOCC - (CROSS - SHARD)][None], swap_cores(own))

    def parts_x(array):
        return array, send(array, ahead), send(array, behind), send(array, opposite)

    def joined(parts, places):
        n = parts[0].shape[0]
        into = jnp.zeros((n * len(parts), WIDE), bf16)
        for part, k in zip(parts, places):
            into = lax.dynamic_update_slice(into, part, ((k % len(parts)) * n, 0))
        return into

    array = weights_of(first_shard)
    from_low = swap_low(array)
    by_x = joined((array, from_low), (zl, 1 - zl))
    by_low = joined(parts_x(weights_of(second_shard)), (x, x - sign, x + sign, x + 2))
    by_low, by_x = lax.optimization_barrier((by_low, by_x))
    keep, give = exchange((first_half, second_half), (by_low, swap_low(by_low)), parts_x(by_x))

    yy = ("y", "y")
    ahead, behind, opposite = around(yy, 1, True), around(yy, -1, True), around(yy, 2, True)
    mine = keep + swap_cores(give)

    def quarter(k):
        return rows_of(mine, k % Y, SHARD)

    part = quarter(y) + add(
        send(quarter(y + sign).astype(bf16), ahead),
        send(quarter(y - sign).astype(bf16), behind),
        send(quarter(y + 2).astype(bf16), opposite),
    )
    part = (part + swap_high(part)).astype(bf16)
    into = jnp.zeros((CROSS // 2, ROWS), bf16)
    for k, array in (
        (y, part),
        (y - sign, send(part, ahead)),
        (y + sign, send(part, behind)),
        (y + 2, send(part, opposite)),
    ):
        into = lax.dynamic_update_slice(into, array, ((k % Y) * SHARD, 0))
    others = swap_cores(into)
    return jnp.concatenate([choose(into, others), choose(others, into)])[:NOCC].astype(f32).T


def solution(mesh):
    in_specs = (
        P("aux", "row", None, None),
        P("aux", "row"),
        P("aux", "row"),
        P("aux", "row"),
        P(("aux", "row"), None),
        P(("aux", "row"), None),
    )
    out_specs = P("row", None)
    return jax.shard_map(local, mesh=mesh, in_specs=in_specs, out_specs=out_specs, check_vma=False)
```

```python
import itertools

import jax
import jax.numpy as jnp
from jax import lax
from jax.experimental import pallas as pl
from jax.experimental.pallas import tpu as pltpu
from jax.sharding import PartitionSpec as P

Y, ZH, CORE, X, ZL = 4, 2, 2, 4, 2
AXES = ("aux", "row")
BLK = 128
ROW_BLOCKS = 6
ROWS = ROW_BLOCKS * BLK
SLOTS = 96
NB = 6144
NOCC = 800
WIDE = 896
CROSS = 832
SHARD = CROSS // 8
OWN = 48
STEP = 4
UNROLL = 3
MAIN = 32
bf16, f32 = jnp.bfloat16, jnp.float32


def permutation(move):
    pairs = []
    for y, zh, c, x, zl in itertools.product(range(Y), range(ZH), range(CORE), range(X), range(ZL)):
        at = dict(y=y, z=zh * ZL + zl, c=c, x=x)
        to = move(dict(at))

        def flat(d):
            return (((d["y"] * ZH + d["z"] // ZL) * CORE + d["c"]) * X + d["x"]) * ZL + d["z"] % ZL

        pairs.append((flat(at), flat(to)))
    return pairs


def around(axes, by, mirror):
    def move(d):
        axis = axes[d["c"]]
        d[axis] = (d[axis] + (-by if mirror and d["c"] else by)) % 4
        return d

    return permutation(move)


def other_core(d):
    d["c"] = 1 - d["c"]
    return d


def other_low(d):
    d["z"] = d["z"] ^ 1
    return d


def other_high(d):
    d["z"] = d["z"] ^ 2
    return d


def send(array, pairs):
    return lax.ppermute(array, AXES, pairs)


def swap_cores(array):
    return send(array, permutation(other_core))


def swap_low(array):
    return send(array, permutation(other_low))


def swap_high(array):
    return send(array, permutation(other_high))


def here():
    aux, row = lax.axis_index("aux"), lax.axis_index("row")
    return aux % CORE, row, row // ZL, row % ZL


def slab_kernel(main0, main1, rest, out, sems):
    core, row, _, _ = here()
    copies = []
    for x in range(X):
        a = jnp.where(core == 0, x, row // ZL)
        b = jnp.where(core == 0, row // ZL, x)
        for c, main in enumerate((main0, main1)):
            copies.append(
                pltpu.make_async_copy(main.at[b, row % ZL, :, a], out.at[c, x, :, pl.ds(0, MAIN)], sems.at[3 * x + c])
            )
        copies.append(
            pltpu.make_async_copy(
                rest.at[row % ZL, :, :, a, b], out.at[:, x, :, pl.ds(MAIN, OWN - MAIN)], sems.at[3 * x + 2]
            )
        )
    for copy in copies:
        copy.start()
    for copy in copies:
        copy.wait()


def own_slab(main0, main1, rest):
    return pl.pallas_call(
        slab_kernel,
        out_shape=jax.ShapeDtypeStruct((CORE, X, ZL, OWN, WIDE), bf16),
        in_specs=[pl.BlockSpec(memory_space=pl.ANY)] * 3,
        out_specs=pl.BlockSpec(memory_space=pltpu.VMEM),
        scratch_shapes=[pltpu.SemaphoreType.DMA((3 * X,))],
        compiler_params=pltpu.CompilerParams(vmem_limit_bytes=4 * 1024 * 1024),
        name="slab",
    )(main0, main1, rest)


def assemble(main0, main1, rest, held, sems):
    core = here()[0]
    copies = []
    for a in range(4):
        for b in range(4):
            y, x = jnp.where(core == 0, b, a), jnp.where(core == 0, a, b)
            i = 3 * (4 * a + b)
            for c, main in enumerate((main0, main1)):
                copies.append(
                    pltpu.make_async_copy(
                        main.at[b, :, :, a], held.at[y, :, c, x, :, pl.ds(0, MAIN)], sems.at[i + c]
                    )
                )
            copies.append(
                pltpu.make_async_copy(
                    rest.at[:, :, :, a, b], held.at[y, :, :, x, :, pl.ds(MAIN, OWN - MAIN)], sems.at[i + 2]
                )
            )
    return copies


def list_steps(q, meta, order, counts, steps):
    def clear(i, carry):
        counts[i] = 0
        return carry

    lax.fori_loop(0, ROW_BLOCKS, clear, 0)

    def put(s, carry):
        group = meta[q, s]
        n = counts[group]
        order[group, n] = s
        counts[group] = n + 1
        return carry

    lax.fori_loop(0, meta[q, 2 * SLOTS], put, 0)

    def list_group(group, base):
        n = counts[group]
        for i in range(STEP):
            order[group, n + i] = SLOTS
        many = (n + STEP - 1) // STEP

        def list_step(i, carry):
            steps[base + i, 0] = group
            for k in range(STEP):
                s = order[group, i * STEP + k]
                steps[base + i, 1 + k] = s
                steps[base + i, 1 + STEP + k] = jnp.where(s < SLOTS, meta[q, SLOTS + s], 0)
            return carry

        lax.fori_loop(0, many, list_step, 0)
        return base + many

    many = lax.fori_loop(0, ROW_BLOCKS, list_group, 0)
    for u in range(UNROLL - 1):
        steps[many + u, 0] = ROW_BLOCKS
        for k in range(STEP):
            steps[many + u, 1 + k] = SLOTS
            steps[many + u, 1 + STEP + k] = 0
    return many


def multiply_kernel(q, meta, factors, *refs):
    if q == 1:
        *parts, out, held, blocks, total, order, counts, steps, sems = refs
        copies = assemble(*parts, held, sems)
    else:
        held, out, blocks, total, order, counts, steps, sems = refs
        copies = []
    copies.append(pltpu.make_async_copy(factors, blocks.at[pl.ds(0, SLOTS)], sems.at[48]))
    for copy in copies:
        copy.start()
    blocks[SLOTS] = jnp.zeros((BLK, BLK), bf16)
    total[...] = jnp.zeros_like(total)
    many = list_steps(q, meta, order, counts, steps)
    for copy in copies:
        copy.wait()
    panels = held.reshape(NB, WIDE)

    def some(i, carry):
        products = []
        for u in range(UNROLL):
            left, right = [], []
            for k in range(STEP):
                left.append(blocks[steps[i * UNROLL + u, 1 + k]])
                column = steps[i * UNROLL + u, 1 + STEP + k]
                right.append(panels[pl.ds(pl.multiple_of(column * BLK, BLK), BLK), :])
            products.append(
                jnp.dot(jnp.concatenate(left, axis=1), jnp.concatenate(right, axis=0), preferred_element_type=f32)
            )
        for u in range(UNROLL):
            total[steps[i * UNROLL + u, 0]] += products[u]
        return carry

    lax.fori_loop(0, (many + UNROLL - 1) // UNROLL, some, 0)
    for group in range(ROW_BLOCKS):
        out[group * BLK : (group + 1) * BLK, :] = total[group].astype(bf16)


def multiply(q, meta, factors, *panels):
    most = SLOTS // STEP + ROW_BLOCKS + UNROLL
    half = jax.ShapeDtypeStruct((ROWS, WIDE), bf16)
    held = jax.ShapeDtypeStruct((Y, ZH, CORE, X, ZL, OWN, WIDE), bf16)
    vmem, anywhere = pl.BlockSpec(memory_space=pltpu.VMEM), pl.BlockSpec(memory_space=pl.ANY)

    def kernel(*refs):
        multiply_kernel(q, *refs)

    return pl.pallas_call(
        kernel,
        out_shape=[half, held] if q == 1 else half,
        in_specs=[pl.BlockSpec(memory_space=pltpu.SMEM), anywhere] + ([anywhere] * 3 if q == 1 else [vmem]),
        out_specs=[vmem, vmem] if q == 1 else vmem,
        scratch_shapes=[
            pltpu.VMEM((SLOTS + 1, BLK, BLK), bf16),
            pltpu.VMEM((ROW_BLOCKS + 1, BLK, WIDE), f32),
            pltpu.SMEM((ROW_BLOCKS, SLOTS + 2 * STEP), jnp.int32),
            pltpu.SMEM((ROW_BLOCKS,), jnp.int32),
            pltpu.SMEM((most, 1 + 2 * STEP), jnp.int32),
            pltpu.SemaphoreType.DMA((49,)),
        ],
        compiler_params=pltpu.CompilerParams(vmem_limit_bytes=(22 if q == 1 else 12) * 1024 * 1024),
        cost_estimate=pl.CostEstimate(flops=96 * 2 * 128 * 128 * 896, bytes_accessed=2**23, transcendentals=0),
        name="multiply",
    )(meta, factors, *panels)


def cross_kernel(starts, half, slab, theirs, *refs):
    outs, used, product = refs[:-2], refs[-2], refs[-1]
    core, row, _, _ = here()
    used[...] = jnp.where(core == 0, slab[...], theirs[...])
    product[...] = lax.dot_general(
        half[...], used[...], (((0,), (0,)), ((), ())), preferred_element_type=f32
    ).astype(bf16)
    value = jnp.sum(half[...].astype(f32) * theirs[...].astype(f32), keepdims=True)
    high = value.astype(bf16).astype(f32)
    middle = (value - high).astype(bf16).astype(f32)
    low = value - high - middle
    lane = lax.broadcasted_iota(jnp.int32, (16, WIDE), 1)
    line = lax.broadcasted_iota(jnp.int32, (16, WIDE), 0)
    coded = jnp.where(
        lane == 3 * row, high, jnp.where(lane == 3 * row + 1, middle, jnp.where(lane == 3 * row + 2, low, 0.0))
    )
    product[NOCC : NOCC + 16, :] = jnp.where(line == 0, coded, 0.0).astype(bf16)
    for out, start in zip(outs, starts()):
        n = out.shape[0]
        out[...] = product[pl.ds(pl.multiple_of(start * n, n), n), :]


def chunks_x():
    core, _, x, _ = here()
    return x, (x + 1 - 2 * core) % X, (x - 1 + 2 * core) % X, (x + 2) % X


def chunks_low():
    zl = here()[3]
    return zl, 1 - zl


def cross(starts, many, half, slab, theirs):
    def kernel(*refs):
        cross_kernel(starts, *refs)

    return pl.pallas_call(
        kernel,
        out_shape=[jax.ShapeDtypeStruct((CROSS // many, WIDE), bf16)] * many,
        in_specs=[pl.BlockSpec(memory_space=pltpu.VMEM)] * 3,
        out_specs=[pl.BlockSpec(memory_space=pltpu.VMEM)] * many,
        scratch_shapes=[pltpu.VMEM((ROWS, WIDE), bf16), pltpu.VMEM((WIDE, WIDE), bf16)],
        compiler_params=pltpu.CompilerParams(vmem_limit_bytes=14 * 1024 * 1024),
        cost_estimate=pl.CostEstimate(flops=2 * 768 * 896 * 896, bytes_accessed=2**23, transcendentals=0),
        name="cross",
    )(half, slab, theirs)


def exchange_kernel(*refs):
    halves, parts, (keep, give, weights, turned, sems) = refs[:2], refs[2:8], refs[8:]
    core, _, _, _ = here()
    copies = []
    for i, (q, at) in enumerate([(0, at) for at in chunks_low()] + [(1, at) for at in chunks_arrived()]):
        n = parts[i].shape[0]
        into = weights.at[q, pl.ds(pl.multiple_of(at * n, n), n), :]
        copies.append(pltpu.make_async_copy(parts[i], into, sems.at[i]))
    for copy in copies:
        copy.start()
    for q in range(2):
        weights[q, CROSS:, :] = jnp.zeros((WIDE - CROSS, WIDE), bf16)
    for copy in copies:
        copy.wait()
    line = lax.broadcasted_iota(jnp.int32, (16, WIDE), 0)
    total = None
    for q in range(2):
        codes = jnp.where(line == 0, weights[q, NOCC : NOCC + 16, :].astype(f32), 0.0)
        codes = codes + jnp.where(line == 1, weights[1 - q, NOCC : NOCC + 16, :].astype(f32), 0.0)
        coulomb = jnp.sum(codes, keepdims=True) * (1.0 / NB)
        factor = jnp.where(core == 0, 2.0 * coulomb, 0.0)
        own = halves[q][...]
        term = factor * own.astype(f32) - jnp.dot(own, weights[q], preferred_element_type=f32)
        total = term if total is None else total + term
    turned[...] = total.T
    n = CROSS // 2
    keep[...] = turned[pl.ds(pl.multiple_of(core * n, n), n), :]
    give[...] = turned[pl.ds(pl.multiple_of((1 - core) * n, n), n), :]


def chunks_arrived():
    x, ahead, behind, far = chunks_x()
    return x, behind, ahead, far


def exchange(halves, low_parts, x_parts):
    return pl.pallas_call(
        exchange_kernel,
        out_shape=[jax.ShapeDtypeStruct((CROSS // 2, ROWS), f32)] * 2,
        in_specs=[pl.BlockSpec(memory_space=pltpu.VMEM)] * 2 + [pl.BlockSpec(memory_space=pl.ANY)] * 6,
        out_specs=[pl.BlockSpec(memory_space=pltpu.VMEM)] * 2,
        scratch_shapes=[
            pltpu.VMEM((2, WIDE, WIDE), bf16),
            pltpu.VMEM((WIDE, ROWS), f32),
            pltpu.SemaphoreType.DMA((6,)),
        ],
        compiler_params=pltpu.CompilerParams(vmem_limit_bytes=20 * 1024 * 1024),
        cost_estimate=pl.CostEstimate(flops=4 * 768 * 896 * 896, bytes_accessed=2**23, transcendentals=0),
        name="exchange",
    )(*halves, *low_parts, *x_parts)


def local(factors, block_rows, block_cols, block_count, orbitals, response):
    aux, row = lax.axis_index("aux"), lax.axis_index("row")
    y, zh, c = aux // (ZH * CORE), (aux // CORE) % ZH, aux % CORE
    x, zl = row // ZL, row % ZL
    z = zh * ZL + zl
    sign = 1 - 2 * c
    first = c == 0

    def choose(a, b):
        return jnp.where(first, a, b)

    def send_after(array, pairs, *earlier):
        return send(lax.optimization_barrier((array, *earlier))[0], pairs)

    def put(into, array, **at):
        index = [jnp.int32(0)] * into.ndim
        for dim, i in at.items():
            index[int(dim[1:])] = i
        return lax.dynamic_update_slice(into, array, index)

    got = send(choose(response, orbitals), permutation(other_core))
    own_blocks = factors[0]
    other_blocks = send_after(own_blocks, permutation(other_core), got)
    both = jnp.stack([choose(orbitals, got), choose(got, response)])
    both = jnp.pad(both, ((0, 0), (0, 0), (0, WIDE - NOCC)))

    one, two = ("x", "y"), ("y", "x")
    at_one, at_two = choose(x, y), choose(y, x)
    shape = (CORE, 4, OWN, WIDE)
    stage = put(jnp.zeros(shape, bf16), both[:, None], d1=at_one)
    ahead = send(both, around(one, 1, False))
    behind = send(both, around(one, -1, False))
    far = send(both, around(one, 2, False))
    stage = put(stage, ahead[:, None], d1=(at_one - 1) % 4)
    stage = put(stage, behind[:, None], d1=(at_one + 1) % 4)
    stage = put(stage, far[:, None], d1=(at_one + 2) % 4)
    stage, other_blocks = lax.optimization_barrier((stage, other_blocks))

    main, rest = stage[:, :, :MAIN], stage[:, :, MAIN:]
    zz = ("z", "z")
    main_ahead = send(main, around(zz, 1, True))
    rest_ahead = send(rest, around(two, 1, False))
    rest_behind = send(rest, around(two, -1, False))
    main_far = send(main_ahead, around(zz, 1, True))
    main_behind = send(main, around(zz, -1, True))
    rest_far = send_after(rest, around(two, 2, False), rest_ahead, main_ahead)

    mains = [jnp.zeros((ZH, ZL, 4, MAIN, WIDE), bf16)] * 2
    for array, at in (
        (main, z),
        (main_ahead, (z - sign) % 4),
        (main_behind, (z + sign) % 4),
        (main_far, (z + 2) % 4),
    ):
        mains = [put(into, array[i][None, None], d0=at // ZL, d1=at % ZL) for i, into in enumerate(mains)]
    into = jnp.zeros((CORE, 4, 4, OWN - MAIN, WIDE), bf16)
    for array, at in (
        (rest, at_two),
        (rest_ahead, (at_two - 1) % 4),
        (rest_behind, (at_two + 1) % 4),
        (rest_far, (at_two + 2) % 4),
    ):
        into = put(into, array[:, :, None], d2=at)
    rest = into

    ahead, behind = around(two, 1, False), around(two, -1, False)
    mains, rest = lax.optimization_barrier((mains, rest))
    ahead_0 = send(mains[0], ahead)
    behind_1 = send(mains[1], behind)
    rest_ahead = send(rest, around(zz, 1, True))
    rest_behind = send(rest, around(zz, -1, True))
    ahead_1 = send_after(mains[1], ahead, ahead_0)
    behind_0 = send_after(mains[0], behind, behind_1)
    far_0 = send(ahead_0, ahead)
    far_1 = send_after(behind_1, behind, rest_ahead)
    lists = lax.optimization_barrier((block_rows[0], block_cols[0], block_count[0], ahead_0))
    lists = jnp.concatenate([lists[0] % ROW_BLOCKS, lists[1], lists[2]])
    lists = jnp.pad(lists, (0, 256 - 2 * SLOTS - 1))[None]
    meta = jnp.concatenate([lists, swap_cores(lists)])
    rest_far = send_after(rest_ahead, around(zz, 1, True), rest_behind)
    arrays = (
        (mains[0], ahead_0, behind_0, far_0),
        (mains[1], ahead_1, behind_1, far_1),
    )
    mains = []
    for four in arrays:
        into = jnp.zeros((4, *four[0].shape), bf16)
        for array, at in zip(four, (at_two, (at_two - 1) % 4, (at_two + 1) % 4, (at_two + 2) % 4)):
            into = put(into, array[None], d0=at)
        mains.append(into)
    into = jnp.zeros((ZH, CORE, ZL, 4, 4, OWN - MAIN, WIDE), bf16)
    for array, at in (
        (rest, z),
        (rest_ahead, (z - sign) % 4),
        (rest_behind, (z + sign) % 4),
        (rest_far, (z + 2) % 4),
    ):
        into = put(into, array[None, :, None], d0=at // ZL, d2=at % ZL)
    rest = into

    slab = own_slab(*mains, rest).reshape(ROWS, WIDE)
    theirs = swap_cores(slab)
    second_half, panels = multiply(1, meta, other_blocks, *mains, rest)

    def add(*arrays):
        return sum(a.astype(f32) for a in arrays)

    def rows_of(array, k, n):
        return lax.dynamic_slice(array, (k * n, 0), (n, array.shape[1]))

    xx = ("x", "x")
    ahead, behind = around(xx, 1, True), around(xx, -1, True)
    opposite = around(xx, 2, True)
    half_mine, to_low = cross(chunks_low, 2, second_half, slab, theirs)
    from_low = swap_low(to_low)
    panels, half_mine = lax.optimization_barrier((panels, half_mine))
    first_half = multiply(0, meta, own_blocks, panels)
    mine, to_ahead, to_behind, to_far = cross(chunks_x, 4, first_half, slab, theirs)
    parts = (mine, send(to_ahead, ahead), send(to_behind, behind), send(to_far, opposite))
    half_mine = add(half_mine, from_low).astype(bf16)
    second = (
        rows_of(half_mine, x, SHARD),
        send(rows_of(half_mine, (x + sign) % 4, SHARD), ahead),
        send(rows_of(half_mine, (x - sign) % 4, SHARD), behind),
        send(rows_of(half_mine, (x + 2) % 4, SHARD), opposite),
    )
    parts, second = lax.optimization_barrier((parts, second[:2])), second
    parts, second = parts[0], (*parts[1], *second[2:])
    mine = add(*parts).astype(bf16)
    first_shard = add(rows_of(mine, zl, SHARD), swap_low(rows_of(mine, 1 - zl, SHARD)))
    second_shard = add(*second)

    last = (x == X - 1) & (zl == ZL - 1)
    at = jnp.arange(SHARD, dtype=jnp.int32)[:, None] + (CROSS - SHARD)

    def weights_of(shard):
        own = jnp.where(last & (at == NOCC), shard, shard * (1.0 / NB)).astype(bf16)
        return jnp.where(last & (at == NOCC + 1), own[NOCC - (CROSS - SHARD)][None], swap_cores(own))

    def parts_x(array):
        return array, send(array, ahead), send(array, behind), send(array, opposite)

    def joined(parts, places):
        n = parts[0].shape[0]
        into = jnp.zeros((n * len(parts), WIDE), bf16)
        for part, k in zip(parts, places):
            into = lax.dynamic_update_slice(into, part, ((k % len(parts)) * n, 0))
        return into

    array = weights_of(first_shard)
    from_low = swap_low(array)
    by_x = joined((array, from_low), (zl, 1 - zl))
    by_low = joined(parts_x(weights_of(second_shard)), (x, x - sign, x + sign, x + 2))
    by_low, by_x = lax.optimization_barrier((by_low, by_x))
    keep, give = exchange((first_half, second_half), (by_low, swap_low(by_low)), parts_x(by_x))

    yy = ("y", "y")
    ahead, behind, opposite = around(yy, 1, True), around(yy, -1, True), around(yy, 2, True)
    mine = keep + swap_cores(give)

    def quarter(k):
        return rows_of(mine, k % Y, SHARD)

    part = quarter(y) + add(
        send(quarter(y + sign).astype(bf16), ahead),
        send(quarter(y - sign).astype(bf16), behind),
        send(quarter(y + 2).astype(bf16), opposite),
    )
    part = (part + swap_high(part)).astype(bf16)
    into = jnp.zeros((CROSS // 2, ROWS), bf16)
    for k, array in (
        (y, part),
        (y - sign, send(part, ahead)),
        (y + sign, send(part, behind)),
        (y + 2, send(part, opposite)),
    ):
        into = lax.dynamic_update_slice(into, array, ((k % Y) * SHARD, 0))
    others = swap_cores(into)
    return jnp.concatenate([choose(into, others), choose(others, into)])[:NOCC].astype(f32).T


def solution(mesh):
    in_specs = (
        P("aux", "row", None, None),
        P("aux", "row"),
        P("aux", "row"),
        P("aux", "row"),
        P(("aux", "row"), None),
        P(("aux", "row"), None),
    )
    out_specs = P("row", None)
    return jax.shard_map(local, mesh=mesh, in_specs=in_specs, out_specs=out_specs, check_vma=False)
```

```python
import itertools

import jax
import jax.numpy as jnp
from jax import lax
from jax.experimental import pallas as pl
from jax.experimental.pallas import tpu as pltpu
from jax.sharding import PartitionSpec as P

Y, ZH, CORE, X, ZL = 4, 2, 2, 4, 2
AXES = ("aux", "row")
BLK = 128
ROW_BLOCKS = 6
ROWS = ROW_BLOCKS * BLK
SLOTS = 96
NB = 6144
NOCC = 800
WIDE = 896
CROSS = 832
SHARD = CROSS // 8
OWN = 48
STEP = 4
UNROLL = 3
MAIN = 32
bf16, f32 = jnp.bfloat16, jnp.float32


def permutation(move):
    pairs = []
    for y, zh, c, x, zl in itertools.product(range(Y), range(ZH), range(CORE), range(X), range(ZL)):
        at = dict(y=y, z=zh * ZL + zl, c=c, x=x)
        to = move(dict(at))

        def flat(d):
            return (((d["y"] * ZH + d["z"] // ZL) * CORE + d["c"]) * X + d["x"]) * ZL + d["z"] % ZL

        pairs.append((flat(at), flat(to)))
    return pairs


def around(axes, by, mirror):
    def move(d):
        axis = axes[d["c"]]
        d[axis] = (d[axis] + (-by if mirror and d["c"] else by)) % 4
        return d

    return permutation(move)


def other_core(d):
    d["c"] = 1 - d["c"]
    return d


def other_low(d):
    d["z"] = d["z"] ^ 1
    return d


def other_high(d):
    d["z"] = d["z"] ^ 2
    return d


def send(array, pairs):
    return lax.ppermute(array, AXES, pairs)


def swap_cores(array):
    return send(array, permutation(other_core))


def swap_low(array):
    return send(array, permutation(other_low))


def swap_high(array):
    return send(array, permutation(other_high))


def here():
    aux, row = lax.axis_index("aux"), lax.axis_index("row")
    return aux % CORE, row, row // ZL, row % ZL


def slab_kernel(main0, main1, rest, out, sems):
    core, row, _, _ = here()
    copies = []
    for x in range(X):
        a = jnp.where(core == 0, x, row // ZL)
        b = jnp.where(core == 0, row // ZL, x)
        for c, main in enumerate((main0, main1)):
            copies.append(
                pltpu.make_async_copy(main.at[b, row % ZL, :, a], out.at[c, x, :, pl.ds(0, MAIN)], sems.at[3 * x + c])
            )
        copies.append(
            pltpu.make_async_copy(
                rest.at[row % ZL, :, :, a, b], out.at[:, x, :, pl.ds(MAIN, OWN - MAIN)], sems.at[3 * x + 2]
            )
        )
    for copy in copies:
        copy.start()
    for copy in copies:
        copy.wait()


def own_slab(main0, main1, rest):
    return pl.pallas_call(
        slab_kernel,
        out_shape=jax.ShapeDtypeStruct((CORE, X, ZL, OWN, WIDE), bf16),
        in_specs=[pl.BlockSpec(memory_space=pl.ANY)] * 3,
        out_specs=pl.BlockSpec(memory_space=pltpu.VMEM),
        scratch_shapes=[pltpu.SemaphoreType.DMA((3 * X,))],
        compiler_params=pltpu.CompilerParams(vmem_limit_bytes=4 * 1024 * 1024),
        name="slab",
    )(main0, main1, rest)


def assemble(main0, main1, rest, held, sems):
    core = here()[0]
    copies = []
    for a in range(4):
        for b in range(4):
            y, x = jnp.where(core == 0, b, a), jnp.where(core == 0, a, b)
            i = 3 * (4 * a + b)
            for c, main in enumerate((main0, main1)):
                copies.append(
                    pltpu.make_async_copy(
                        main.at[b, :, :, a], held.at[y, :, c, x, :, pl.ds(0, MAIN)], sems.at[i + c]
                    )
                )
            copies.append(
                pltpu.make_async_copy(
                    rest.at[:, :, :, a, b], held.at[y, :, :, x, :, pl.ds(MAIN, OWN - MAIN)], sems.at[i + 2]
                )
            )
    return copies


def list_steps(q, meta, order, counts, steps):
    def clear(i, carry):
        counts[i] = 0
        return carry

    lax.fori_loop(0, ROW_BLOCKS, clear, 0)

    def put(s, carry):
        group = meta[q, s]
        n = counts[group]
        order[group, n] = s
        counts[group] = n + 1
        return carry

    lax.fori_loop(0, meta[q, 2 * SLOTS], put, 0)

    def list_group(group, base):
        n = counts[group]
        for i in range(STEP):
            order[group, n + i] = SLOTS
        many = (n + STEP - 1) // STEP

        def list_step(i, carry):
            steps[base + i, 0] = group
            for k in range(STEP):
                s = order[group, i * STEP + k]
                steps[base + i, 1 + k] = s
                steps[base + i, 1 + STEP + k] = jnp.where(s < SLOTS, meta[q, SLOTS + s], 0)
            return carry

        lax.fori_loop(0, many, list_step, 0)
        return base + many

    many = lax.fori_loop(0, ROW_BLOCKS, list_group, 0)
    for u in range(UNROLL - 1):
        steps[many + u, 0] = ROW_BLOCKS
        for k in range(STEP):
            steps[many + u, 1 + k] = SLOTS
            steps[many + u, 1 + STEP + k] = 0
    return many


def multiply_kernel(q, meta, factors, *refs):
    if q == 1:
        *parts, out, held, blocks, total, order, counts, steps, sems = refs
        copies = assemble(*parts, held, sems)
    else:
        held, out, blocks, total, order, counts, steps, sems = refs
        copies = []
    copies.append(pltpu.make_async_copy(factors, blocks.at[pl.ds(0, SLOTS)], sems.at[48]))
    for copy in copies:
        copy.start()
    blocks[SLOTS] = jnp.zeros((BLK, BLK), bf16)
    total[...] = jnp.zeros_like(total)
    many = list_steps(q, meta, order, counts, steps)
    for copy in copies:
        copy.wait()
    panels = held.reshape(NB, WIDE)

    def some(i, carry):
        products = []
        for u in range(UNROLL):
            left, right = [], []
            for k in range(STEP):
                left.append(blocks[steps[i * UNROLL + u, 1 + k]])
                column = steps[i * UNROLL + u, 1 + STEP + k]
                right.append(panels[pl.ds(pl.multiple_of(column * BLK, BLK), BLK), :])
            products.append(
                jnp.dot(jnp.concatenate(left, axis=1), jnp.concatenate(right, axis=0), preferred_element_type=f32)
            )
        for u in range(UNROLL):
            total[steps[i * UNROLL + u, 0]] += products[u]
        return carry

    lax.fori_loop(0, (many + UNROLL - 1) // UNROLL, some, 0)
    for group in range(ROW_BLOCKS):
        out[group * BLK : (group + 1) * BLK, :] = total[group].astype(bf16)


def multiply(q, meta, factors, *panels):
    most = SLOTS // STEP + ROW_BLOCKS + UNROLL
    half = jax.ShapeDtypeStruct((ROWS, WIDE), bf16)
    held = jax.ShapeDtypeStruct((Y, ZH, CORE, X, ZL, OWN, WIDE), bf16)
    vmem, anywhere = pl.BlockSpec(memory_space=pltpu.VMEM), pl.BlockSpec(memory_space=pl.ANY)

    def kernel(*refs):
        multiply_kernel(q, *refs)

    return pl.pallas_call(
        kernel,
        out_shape=[half, held] if q == 1 else half,
        in_specs=[pl.BlockSpec(memory_space=pltpu.SMEM), anywhere] + ([anywhere] * 3 if q == 1 else [vmem]),
        out_specs=[vmem, vmem] if q == 1 else vmem,
        scratch_shapes=[
            pltpu.VMEM((SLOTS + 1, BLK, BLK), bf16),
            pltpu.VMEM((ROW_BLOCKS + 1, BLK, WIDE), f32),
            pltpu.SMEM((ROW_BLOCKS, SLOTS + 2 * STEP), jnp.int32),
            pltpu.SMEM((ROW_BLOCKS,), jnp.int32),
            pltpu.SMEM((most, 1 + 2 * STEP), jnp.int32),
            pltpu.SemaphoreType.DMA((49,)),
        ],
        compiler_params=pltpu.CompilerParams(vmem_limit_bytes=24 * 1024 * 1024),
        cost_estimate=pl.CostEstimate(flops=96 * 2 * 128 * 128 * 896, bytes_accessed=2**23, transcendentals=0),
        name="multiply",
    )(meta, factors, *panels)


def cross_kernel(starts, half, slab, theirs, *refs):
    outs, used, product = refs[:-2], refs[-2], refs[-1]
    core, row, _, _ = here()
    used[...] = jnp.where(core == 0, slab[...], theirs[...])
    product[...] = lax.dot_general(
        half[...], used[...], (((0,), (0,)), ((), ())), preferred_element_type=f32
    ).astype(bf16)
    value = jnp.sum(half[...].astype(f32) * theirs[...].astype(f32), keepdims=True)
    high = value.astype(bf16).astype(f32)
    middle = (value - high).astype(bf16).astype(f32)
    low = value - high - middle
    lane = lax.broadcasted_iota(jnp.int32, (16, WIDE), 1)
    line = lax.broadcasted_iota(jnp.int32, (16, WIDE), 0)
    coded = jnp.where(
        lane == 3 * row, high, jnp.where(lane == 3 * row + 1, middle, jnp.where(lane == 3 * row + 2, low, 0.0))
    )
    product[NOCC : NOCC + 16, :] = jnp.where(line == 0, coded, 0.0).astype(bf16)
    for out, start in zip(outs, starts()):
        n = out.shape[0]
        out[...] = product[pl.ds(pl.multiple_of(start * n, n), n), :]


def chunks_x():
    core, _, x, _ = here()
    return x, (x + 1 - 2 * core) % X, (x - 1 + 2 * core) % X, (x + 2) % X


def chunks_low():
    zl = here()[3]
    return zl, 1 - zl


def cross(starts, many, half, slab, theirs):
    def kernel(*refs):
        cross_kernel(starts, *refs)

    return pl.pallas_call(
        kernel,
        out_shape=[jax.ShapeDtypeStruct((CROSS // many, WIDE), bf16)] * many,
        in_specs=[pl.BlockSpec(memory_space=pltpu.VMEM)] * 3,
        out_specs=[pl.BlockSpec(memory_space=pltpu.VMEM)] * many,
        scratch_shapes=[pltpu.VMEM((ROWS, WIDE), bf16), pltpu.VMEM((WIDE, WIDE), bf16)],
        compiler_params=pltpu.CompilerParams(vmem_limit_bytes=30 * 1024 * 1024),
        cost_estimate=pl.CostEstimate(flops=2 * 768 * 896 * 896, bytes_accessed=2**23, transcendentals=0),
        name="cross",
    )(half, slab, theirs)


def exchange_kernel(*refs):
    halves, parts, (keep, give, held, weights, turned, sems) = refs[:2], refs[2:8], refs[8:]
    core, _, _, _ = here()
    copies = [pltpu.make_async_copy(halves[q], held.at[q], sems.at[6 + q]) for q in range(2)]
    for i, (q, at) in enumerate([(0, at) for at in chunks_low()] + [(1, at) for at in chunks_arrived()]):
        n = parts[i].shape[0]
        into = weights.at[q, pl.ds(pl.multiple_of(at * n, n), n), :]
        copies.append(pltpu.make_async_copy(parts[i], into, sems.at[i]))
    for copy in copies:
        copy.start()
    for q in range(2):
        weights[q, CROSS:, :] = jnp.zeros((WIDE - CROSS, WIDE), bf16)
    for copy in copies:
        copy.wait()
    line = lax.broadcasted_iota(jnp.int32, (16, WIDE), 0)
    total = None
    for q in range(2):
        codes = jnp.where(line == 0, weights[q, NOCC : NOCC + 16, :].astype(f32), 0.0)
        codes = codes + jnp.where(line == 1, weights[1 - q, NOCC : NOCC + 16, :].astype(f32), 0.0)
        coulomb = jnp.sum(codes, keepdims=True) * (1.0 / NB)
        factor = jnp.where(core == 0, 2.0 * coulomb, 0.0)
        own = held[q]
        term = factor * own.astype(f32) - jnp.dot(own, weights[q], preferred_element_type=f32)
        total = term if total is None else total + term
    turned[...] = total.T
    n = CROSS // 2
    keep[...] = turned[pl.ds(pl.multiple_of(core * n, n), n), :]
    give[...] = turned[pl.ds(pl.multiple_of((1 - core) * n, n), n), :]


def chunks_arrived():
    x, ahead, behind, far = chunks_x()
    return x, behind, ahead, far


def exchange(halves, low_parts, x_parts):
    return pl.pallas_call(
        exchange_kernel,
        out_shape=[jax.ShapeDtypeStruct((CROSS // 2, ROWS), f32)] * 2,
        in_specs=[pl.BlockSpec(memory_space=pl.ANY)] * 8,
        out_specs=[pl.BlockSpec(memory_space=pltpu.VMEM)] * 2,
        scratch_shapes=[
            pltpu.VMEM((2, ROWS, WIDE), bf16),
            pltpu.VMEM((2, WIDE, WIDE), bf16),
            pltpu.VMEM((WIDE, ROWS), f32),
            pltpu.SemaphoreType.DMA((8,)),
        ],
        compiler_params=pltpu.CompilerParams(vmem_limit_bytes=48 * 1024 * 1024),
        cost_estimate=pl.CostEstimate(flops=4 * 768 * 896 * 896, bytes_accessed=2**23, transcendentals=0),
        name="exchange",
    )(*halves, *low_parts, *x_parts)


def local(factors, block_rows, block_cols, block_count, orbitals, response):
    aux, row = lax.axis_index("aux"), lax.axis_index("row")
    y, zh, c = aux // (ZH * CORE), (aux // CORE) % ZH, aux % CORE
    x, zl = row // ZL, row % ZL
    z = zh * ZL + zl
    sign = 1 - 2 * c
    first = c == 0

    def choose(a, b):
        return jnp.where(first, a, b)

    def send_after(array, pairs, *earlier):
        return send(lax.optimization_barrier((array, *earlier))[0], pairs)

    def put(into, array, **at):
        index = [jnp.int32(0)] * into.ndim
        for dim, i in at.items():
            index[int(dim[1:])] = i
        return lax.dynamic_update_slice(into, array, index)

    got = send(choose(response, orbitals), permutation(other_core))
    own_blocks = factors[0]
    other_blocks = send_after(own_blocks, permutation(other_core), got)
    both = jnp.stack([choose(orbitals, got), choose(got, response)])
    both = jnp.pad(both, ((0, 0), (0, 0), (0, WIDE - NOCC)))

    one, two = ("x", "y"), ("y", "x")
    at_one, at_two = choose(x, y), choose(y, x)
    shape = (CORE, 4, OWN, WIDE)
    stage = put(jnp.zeros(shape, bf16), both[:, None], d1=at_one)
    ahead = send(both, around(one, 1, False))
    behind = send(both, around(one, -1, False))
    far = send(both, around(one, 2, False))
    stage = put(stage, ahead[:, None], d1=(at_one - 1) % 4)
    stage = put(stage, behind[:, None], d1=(at_one + 1) % 4)
    stage = put(stage, far[:, None], d1=(at_one + 2) % 4)
    stage, other_blocks = lax.optimization_barrier((stage, other_blocks))

    main, rest = stage[:, :, :MAIN], stage[:, :, MAIN:]
    zz = ("z", "z")
    main_ahead = send(main, around(zz, 1, True))
    rest_ahead = send(rest, around(two, 1, False))
    rest_behind = send(rest, around(two, -1, False))
    main_far = send(main_ahead, around(zz, 1, True))
    main_behind = send(main, around(zz, -1, True))
    rest_far = send_after(rest, around(two, 2, False), rest_ahead, main_ahead)

    lists = lax.optimization_barrier((block_rows[0], block_cols[0], block_count[0], rest_ahead))
    lists = jnp.concatenate([lists[0] % ROW_BLOCKS, lists[1], lists[2]])
    lists = jnp.pad(lists, (0, 256 - 2 * SLOTS - 1))[None]
    meta = jnp.concatenate([lists, swap_cores(lists)])

    mains = [jnp.zeros((ZH, ZL, 4, MAIN, WIDE), bf16)] * 2
    for array, at in (
        (main, z),
        (main_ahead, (z - sign) % 4),
        (main_behind, (z + sign) % 4),
        (main_far, (z + 2) % 4),
    ):
        mains = [put(into, array[i][None, None], d0=at // ZL, d1=at % ZL) for i, into in enumerate(mains)]
    into = jnp.zeros((CORE, 4, 4, OWN - MAIN, WIDE), bf16)
    for array, at in (
        (rest, at_two),
        (rest_ahead, (at_two - 1) % 4),
        (rest_behind, (at_two + 1) % 4),
        (rest_far, (at_two + 2) % 4),
    ):
        into = put(into, array[:, :, None], d2=at)
    rest = into

    ahead, behind = around(two, 1, False), around(two, -1, False)
    mains, rest, meta = lax.optimization_barrier((mains, rest, meta))
    ahead_0 = send(mains[0], ahead)
    behind_1 = send(mains[1], behind)
    rest_ahead = send(rest, around(zz, 1, True))
    rest_behind = send(rest, around(zz, -1, True))
    ahead_1 = send_after(mains[1], ahead, ahead_0)
    behind_0 = send_after(mains[0], behind, behind_1)
    far_0 = send(ahead_0, ahead)
    far_1 = send_after(behind_1, behind, rest_ahead)
    rest_far = send_after(rest_ahead, around(zz, 1, True), rest_behind)
    arrays = (
        (mains[0], ahead_0, behind_0, far_0),
        (mains[1], ahead_1, behind_1, far_1),
    )
    mains = []
    for four in arrays:
        into = jnp.zeros((4, *four[0].shape), bf16)
        for array, at in zip(four, (at_two, (at_two - 1) % 4, (at_two + 1) % 4, (at_two + 2) % 4)):
            into = put(into, array[None], d0=at)
        mains.append(into)
    into = jnp.zeros((ZH, CORE, ZL, 4, 4, OWN - MAIN, WIDE), bf16)
    for array, at in (
        (rest, z),
        (rest_ahead, (z - sign) % 4),
        (rest_behind, (z + sign) % 4),
        (rest_far, (z + 2) % 4),
    ):
        into = put(into, array[None, :, None], d0=at // ZL, d2=at % ZL)
    rest = into

    slab = own_slab(*mains, rest).reshape(ROWS, WIDE)
    theirs = swap_cores(slab)
    second_half, panels = multiply(1, meta, other_blocks, *mains, rest)

    def add(*arrays):
        return sum(a.astype(f32) for a in arrays)

    def rows_of(array, k, n):
        return lax.dynamic_slice(array, (k * n, 0), (n, array.shape[1]))

    xx = ("x", "x")
    ahead, behind = around(xx, 1, True), around(xx, -1, True)
    opposite = around(xx, 2, True)
    half_mine, to_low = cross(chunks_low, 2, second_half, slab, theirs)
    from_low = swap_low(to_low)
    panels, half_mine = lax.optimization_barrier((panels, half_mine))
    first_half = multiply(0, meta, own_blocks, panels)
    mine, to_ahead, to_behind, to_far = cross(chunks_x, 4, first_half, slab, theirs)
    parts = (mine, send(to_ahead, ahead), send(to_behind, behind), send(to_far, opposite))
    half_mine = add(half_mine, from_low).astype(bf16)
    second = (
        rows_of(half_mine, x, SHARD),
        send(rows_of(half_mine, (x + sign) % 4, SHARD), ahead),
        send(rows_of(half_mine, (x - sign) % 4, SHARD), behind),
        send(rows_of(half_mine, (x + 2) % 4, SHARD), opposite),
    )
    parts, half_mine = lax.optimization_barrier((parts, half_mine))
    mine = add(*parts).astype(bf16)
    first_shard = add(rows_of(mine, zl, SHARD), swap_low(rows_of(mine, 1 - zl, SHARD)))
    second_shard = add(*second)

    last = (x == X - 1) & (zl == ZL - 1)
    at = jnp.arange(SHARD, dtype=jnp.int32)[:, None] + (CROSS - SHARD)

    def weights_of(shard):
        own = jnp.where(last & (at == NOCC), shard, shard * (1.0 / NB)).astype(bf16)
        return jnp.where(last & (at == NOCC + 1), own[NOCC - (CROSS - SHARD)][None], swap_cores(own))

    def parts_x(array):
        return array, send(array, ahead), send(array, behind), send(array, opposite)

    def joined(parts, places):
        n = parts[0].shape[0]
        into = jnp.zeros((n * len(parts), WIDE), bf16)
        for part, k in zip(parts, places):
            into = lax.dynamic_update_slice(into, part, ((k % len(parts)) * n, 0))
        return into

    array = weights_of(first_shard)
    from_low = swap_low(array)
    by_x = joined((array, from_low), (zl, 1 - zl))
    by_low = joined(parts_x(weights_of(second_shard)), (x, x - sign, x + sign, x + 2))
    by_low, by_x = lax.optimization_barrier((by_low, by_x))
    keep, give = exchange((first_half, second_half), (by_low, swap_low(by_low)), parts_x(by_x))

    yy = ("y", "y")
    ahead, behind, opposite = around(yy, 1, True), around(yy, -1, True), around(yy, 2, True)
    mine = keep + swap_cores(give)

    def quarter(k):
        return rows_of(mine, k % Y, SHARD)

    part = quarter(y) + add(
        send(quarter(y + sign).astype(bf16), ahead),
        send(quarter(y - sign).astype(bf16), behind),
        send(quarter(y + 2).astype(bf16), opposite),
    )
    part = (part + swap_high(part)).astype(bf16)
    into = jnp.zeros((CROSS // 2, ROWS), bf16)
    for k, array in (
        (y, part),
        (y - sign, send(part, ahead)),
        (y + sign, send(part, behind)),
        (y + 2, send(part, opposite)),
    ):
        into = lax.dynamic_update_slice(into, array, ((k % Y) * SHARD, 0))
    others = swap_cores(into)
    return jnp.concatenate([choose(into, others), choose(others, into)])[:NOCC].astype(f32).T


def solution(mesh):
    in_specs = (
        P("aux", "row", None, None),
        P("aux", "row"),
        P("aux", "row"),
        P("aux", "row"),
        P(("aux", "row"), None),
        P(("aux", "row"), None),
    )
    out_specs = P("row", None)
    return jax.shard_map(local, mesh=mesh, in_specs=in_specs, out_specs=out_specs, check_vma=False)
```

```python
import itertools

import jax
import jax.numpy as jnp
from jax import lax
from jax.experimental import pallas as pl
from jax.experimental.pallas import tpu as pltpu
from jax.sharding import PartitionSpec as P

Y, ZH, CORE, X, ZL = 4, 2, 2, 4, 2
AXES = ("aux", "row")
BLK = 128
ROW_BLOCKS = 6
ROWS = ROW_BLOCKS * BLK
SLOTS = 96
NB = 6144
NOCC = 800
WIDE = 896
CROSS = 832
SHARD = CROSS // 8
OWN = 48
STEP = 4
UNROLL = 3
MAIN = 32
bf16, f32 = jnp.bfloat16, jnp.float32


def permutation(move):
    pairs = []
    for y, zh, c, x, zl in itertools.product(range(Y), range(ZH), range(CORE), range(X), range(ZL)):
        at = dict(y=y, z=zh * ZL + zl, c=c, x=x)
        to = move(dict(at))

        def flat(d):
            return (((d["y"] * ZH + d["z"] // ZL) * CORE + d["c"]) * X + d["x"]) * ZL + d["z"] % ZL

        pairs.append((flat(at), flat(to)))
    return pairs


def around(axes, by, mirror):
    def move(d):
        axis = axes[d["c"]]
        d[axis] = (d[axis] + (-by if mirror and d["c"] else by)) % 4
        return d

    return permutation(move)


def other_core(d):
    d["c"] = 1 - d["c"]
    return d


def other_low(d):
    d["z"] = d["z"] ^ 1
    return d


def other_high(d):
    d["z"] = d["z"] ^ 2
    return d


def send(array, pairs):
    return lax.ppermute(array, AXES, pairs)


def swap_cores(array):
    return send(array, permutation(other_core))


def swap_low(array):
    return send(array, permutation(other_low))


def swap_high(array):
    return send(array, permutation(other_high))


def here():
    aux, row = lax.axis_index("aux"), lax.axis_index("row")
    return aux % CORE, row, row // ZL, row % ZL


def slab_kernel(main0, main1, rest, out, sems):
    core, row, _, _ = here()
    copies = []
    for x in range(X):
        a = jnp.where(core == 0, x, row // ZL)
        b = jnp.where(core == 0, row // ZL, x)
        for c, main in enumerate((main0, main1)):
            copies.append(
                pltpu.make_async_copy(main.at[b, row % ZL, :, a], out.at[c, x, :, pl.ds(0, MAIN)], sems.at[3 * x + c])
            )
        copies.append(
            pltpu.make_async_copy(
                rest.at[row % ZL, :, :, a, b], out.at[:, x, :, pl.ds(MAIN, OWN - MAIN)], sems.at[3 * x + 2]
            )
        )
    for copy in copies:
        copy.start()
    for copy in copies:
        copy.wait()


def own_slab(main0, main1, rest):
    return pl.pallas_call(
        slab_kernel,
        out_shape=jax.ShapeDtypeStruct((CORE, X, ZL, OWN, WIDE), bf16),
        in_specs=[pl.BlockSpec(memory_space=pl.ANY)] * 3,
        out_specs=pl.BlockSpec(memory_space=pltpu.VMEM),
        scratch_shapes=[pltpu.SemaphoreType.DMA((3 * X,))],
        compiler_params=pltpu.CompilerParams(vmem_limit_bytes=4 * 1024 * 1024),
        name="slab",
    )(main0, main1, rest)


def assemble(main0, main1, rest, held, sems):
    core = here()[0]
    copies = []
    for a in range(4):
        for b in range(4):
            y, x = jnp.where(core == 0, b, a), jnp.where(core == 0, a, b)
            i = 3 * (4 * a + b)
            for c, main in enumerate((main0, main1)):
                copies.append(
                    pltpu.make_async_copy(
                        main.at[b, :, :, a], held.at[y, :, c, x, :, pl.ds(0, MAIN)], sems.at[i + c]
                    )
                )
            copies.append(
                pltpu.make_async_copy(
                    rest.at[:, :, :, a, b], held.at[y, :, :, x, :, pl.ds(MAIN, OWN - MAIN)], sems.at[i + 2]
                )
            )
    return copies


def list_steps(q, meta, order, counts, steps):
    def clear(i, carry):
        counts[i] = 0
        return carry

    lax.fori_loop(0, ROW_BLOCKS, clear, 0)

    def put(s, carry):
        group = meta[q, s]
        n = counts[group]
        order[group, n] = s
        counts[group] = n + 1
        return carry

    lax.fori_loop(0, meta[q, 2 * SLOTS], put, 0)

    def list_group(group, base):
        n = counts[group]
        for i in range(STEP):
            order[group, n + i] = SLOTS
        many = (n + STEP - 1) // STEP

        def list_step(i, carry):
            steps[base + i, 0] = group
            for k in range(STEP):
                s = order[group, i * STEP + k]
                steps[base + i, 1 + k] = s
                steps[base + i, 1 + STEP + k] = jnp.where(s < SLOTS, meta[q, SLOTS + s], 0)
            return carry

        lax.fori_loop(0, many, list_step, 0)
        return base + many

    many = lax.fori_loop(0, ROW_BLOCKS, list_group, 0)
    for u in range(UNROLL - 1):
        steps[many + u, 0] = ROW_BLOCKS
        for k in range(STEP):
            steps[many + u, 1 + k] = SLOTS
            steps[many + u, 1 + STEP + k] = 0
    return many


def multiply_kernel(q, meta, factors, *refs):
    if q == 1:
        *parts, out, held, blocks, total, order, counts, steps, sems = refs
        copies = assemble(*parts, held, sems)
    else:
        held, out, blocks, total, order, counts, steps, sems = refs
        copies = []
    copies.append(pltpu.make_async_copy(factors, blocks.at[pl.ds(0, SLOTS)], sems.at[48]))
    for copy in copies:
        copy.start()
    blocks[SLOTS] = jnp.zeros((BLK, BLK), bf16)
    total[...] = jnp.zeros_like(total)
    many = list_steps(q, meta, order, counts, steps)
    for copy in copies:
        copy.wait()
    panels = held.reshape(NB, WIDE)

    def some(i, carry):
        products = []
        for u in range(UNROLL):
            left, right = [], []
            for k in range(STEP):
                left.append(blocks[steps[i * UNROLL + u, 1 + k]])
                column = steps[i * UNROLL + u, 1 + STEP + k]
                right.append(panels[pl.ds(pl.multiple_of(column * BLK, BLK), BLK), :])
            products.append(
                jnp.dot(jnp.concatenate(left, axis=1), jnp.concatenate(right, axis=0), preferred_element_type=f32)
            )
        for u in range(UNROLL):
            total[steps[i * UNROLL + u, 0]] += products[u]
        return carry

    lax.fori_loop(0, (many + UNROLL - 1) // UNROLL, some, 0)
    for group in range(ROW_BLOCKS):
        out[group * BLK : (group + 1) * BLK, :] = total[group].astype(bf16)


def multiply(q, meta, factors, *panels):
    most = SLOTS // STEP + ROW_BLOCKS + UNROLL
    half = jax.ShapeDtypeStruct((ROWS, WIDE), bf16)
    held = jax.ShapeDtypeStruct((Y, ZH, CORE, X, ZL, OWN, WIDE), bf16)
    vmem, anywhere = pl.BlockSpec(memory_space=pltpu.VMEM), pl.BlockSpec(memory_space=pl.ANY)

    def kernel(*refs):
        multiply_kernel(q, *refs)

    return pl.pallas_call(
        kernel,
        out_shape=[half, held] if q == 1 else half,
        in_specs=[pl.BlockSpec(memory_space=pltpu.SMEM), anywhere] + ([anywhere] * 3 if q == 1 else [vmem]),
        out_specs=[vmem, vmem] if q == 1 else vmem,
        scratch_shapes=[
            pltpu.VMEM((SLOTS + 1, BLK, BLK), bf16),
            pltpu.VMEM((ROW_BLOCKS + 1, BLK, WIDE), f32),
            pltpu.SMEM((ROW_BLOCKS, SLOTS + 2 * STEP), jnp.int32),
            pltpu.SMEM((ROW_BLOCKS,), jnp.int32),
            pltpu.SMEM((most, 1 + 2 * STEP), jnp.int32),
            pltpu.SemaphoreType.DMA((49,)),
        ],
        compiler_params=pltpu.CompilerParams(vmem_limit_bytes=24 * 1024 * 1024),
        cost_estimate=pl.CostEstimate(flops=96 * 2 * 128 * 128 * 896, bytes_accessed=2**23, transcendentals=0),
        name="multiply",
    )(meta, factors, *panels)


def cross_kernel(starts, half, slab, theirs, *refs):
    outs, used, product = refs[:-2], refs[-2], refs[-1]
    core, row, _, _ = here()
    used[...] = jnp.where(core == 0, slab[...], theirs[...])
    product[...] = lax.dot_general(
        half[...], used[...], (((0,), (0,)), ((), ())), preferred_element_type=f32
    ).astype(bf16)
    value = jnp.sum(half[...].astype(f32) * theirs[...].astype(f32), keepdims=True)
    high = value.astype(bf16).astype(f32)
    middle = (value - high).astype(bf16).astype(f32)
    low = value - high - middle
    lane = lax.broadcasted_iota(jnp.int32, (16, WIDE), 1)
    line = lax.broadcasted_iota(jnp.int32, (16, WIDE), 0)
    coded = jnp.where(
        lane == 3 * row, high, jnp.where(lane == 3 * row + 1, middle, jnp.where(lane == 3 * row + 2, low, 0.0))
    )
    product[NOCC : NOCC + 16, :] = jnp.where(line == 0, coded, 0.0).astype(bf16)
    for out, start in zip(outs, starts()):
        n = out.shape[0]
        out[...] = product[pl.ds(pl.multiple_of(start * n, n), n), :]


def chunks_x():
    core, _, x, _ = here()
    return x, (x + 1 - 2 * core) % X, (x - 1 + 2 * core) % X, (x + 2) % X


def chunks_low():
    zl = here()[3]
    return zl, 1 - zl


def cross(starts, many, half, slab, theirs):
    def kernel(*refs):
        cross_kernel(starts, *refs)

    return pl.pallas_call(
        kernel,
        out_shape=[jax.ShapeDtypeStruct((CROSS // many, WIDE), bf16)] * many,
        in_specs=[pl.BlockSpec(memory_space=pltpu.VMEM)] * 3,
        out_specs=[pl.BlockSpec(memory_space=pltpu.VMEM)] * many,
        scratch_shapes=[pltpu.VMEM((ROWS, WIDE), bf16), pltpu.VMEM((WIDE, WIDE), bf16)],
        compiler_params=pltpu.CompilerParams(vmem_limit_bytes=30 * 1024 * 1024),
        cost_estimate=pl.CostEstimate(flops=2 * 768 * 896 * 896, bytes_accessed=2**23, transcendentals=0),
        name="cross",
    )(half, slab, theirs)


def sum_kernel(starts, many, *refs):
    arrays, outs, total = refs[:many], refs[many:-1], refs[-1]
    total[...] = sum(array[...].astype(f32) for array in arrays)
    for out, start in zip(outs, starts()):
        n = out.shape[0]
        out[...] = total[pl.ds(pl.multiple_of(start * n, n), n), :].astype(out.dtype)


def sum_chunks(starts, pieces, *arrays):
    n, width = arrays[0].shape
    own = jax.ShapeDtypeStruct((n // pieces, width), f32)
    sent = jax.ShapeDtypeStruct((n // pieces, width), bf16)

    def kernel(*refs):
        sum_kernel(starts, len(arrays), *refs)

    return pl.pallas_call(
        kernel,
        out_shape=[own] + [sent] * (pieces - 1),
        in_specs=[pl.BlockSpec(memory_space=pltpu.VMEM)] * len(arrays),
        out_specs=[pl.BlockSpec(memory_space=pltpu.VMEM)] * pieces,
        scratch_shapes=[pltpu.VMEM((n, width), f32)],
        compiler_params=pltpu.CompilerParams(vmem_limit_bytes=24 * 1024 * 1024),
        cost_estimate=pl.CostEstimate(flops=n * width, bytes_accessed=2**21, transcendentals=0),
        name="sum_chunks",
    )(*arrays)


def chunks_y():
    y, c = lax.axis_index("aux") // (ZH * CORE), here()[0]
    return y, (y + 1 - 2 * c) % Y, (y - 1 + 2 * c) % Y, (y + 2) % Y


def exchange_kernel(*refs):
    halves, parts, (keep, give, held, weights, turned, sems) = refs[:2], refs[2:8], refs[8:]
    core, _, _, _ = here()
    copies = [pltpu.make_async_copy(halves[q], held.at[q], sems.at[6 + q]) for q in range(2)]
    for i, (q, at) in enumerate([(0, at) for at in chunks_low()] + [(1, at) for at in chunks_arrived()]):
        n = parts[i].shape[0]
        into = weights.at[q, pl.ds(pl.multiple_of(at * n, n), n), :]
        copies.append(pltpu.make_async_copy(parts[i], into, sems.at[i]))
    for copy in copies:
        copy.start()
    for q in range(2):
        weights[q, CROSS:, :] = jnp.zeros((WIDE - CROSS, WIDE), bf16)
    for copy in copies:
        copy.wait()
    line = lax.broadcasted_iota(jnp.int32, (16, WIDE), 0)
    total = None
    for q in range(2):
        codes = jnp.where(line == 0, weights[q, NOCC : NOCC + 16, :].astype(f32), 0.0)
        codes = codes + jnp.where(line == 1, weights[1 - q, NOCC : NOCC + 16, :].astype(f32), 0.0)
        coulomb = jnp.sum(codes, keepdims=True) * (1.0 / NB)
        factor = jnp.where(core == 0, 2.0 * coulomb, 0.0)
        own = held[q]
        term = factor * own.astype(f32) - jnp.dot(own, weights[q], preferred_element_type=f32)
        total = term if total is None else total + term
    turned[...] = total.T
    n = CROSS // 2
    keep[...] = turned[pl.ds(pl.multiple_of(core * n, n), n), :]
    give[...] = turned[pl.ds(pl.multiple_of((1 - core) * n, n), n), :]


def chunks_arrived():
    x, ahead, behind, far = chunks_x()
    return x, behind, ahead, far


def exchange(halves, low_parts, x_parts):
    return pl.pallas_call(
        exchange_kernel,
        out_shape=[jax.ShapeDtypeStruct((CROSS // 2, ROWS), f32)] * 2,
        in_specs=[pl.BlockSpec(memory_space=pl.ANY)] * 8,
        out_specs=[pl.BlockSpec(memory_space=pltpu.VMEM)] * 2,
        scratch_shapes=[
            pltpu.VMEM((2, ROWS, WIDE), bf16),
            pltpu.VMEM((2, WIDE, WIDE), bf16),
            pltpu.VMEM((WIDE, ROWS), f32),
            pltpu.SemaphoreType.DMA((8,)),
        ],
        compiler_params=pltpu.CompilerParams(vmem_limit_bytes=48 * 1024 * 1024),
        cost_estimate=pl.CostEstimate(flops=4 * 768 * 896 * 896, bytes_accessed=2**23, transcendentals=0),
        name="exchange",
    )(*halves, *low_parts, *x_parts)


def local(factors, block_rows, block_cols, block_count, orbitals, response):
    aux, row = lax.axis_index("aux"), lax.axis_index("row")
    y, zh, c = aux // (ZH * CORE), (aux // CORE) % ZH, aux % CORE
    x, zl = row // ZL, row % ZL
    z = zh * ZL + zl
    sign = 1 - 2 * c
    first = c == 0

    def choose(a, b):
        return jnp.where(first, a, b)

    def send_after(array, pairs, *earlier):
        return send(lax.optimization_barrier((array, *earlier))[0], pairs)

    def put(into, array, **at):
        index = [jnp.int32(0)] * into.ndim
        for dim, i in at.items():
            index[int(dim[1:])] = i
        return lax.dynamic_update_slice(into, array, index)

    got = send(choose(response, orbitals), permutation(other_core))
    own_blocks = factors[0]
    other_blocks = send_after(own_blocks, permutation(other_core), got)
    both = jnp.stack([choose(orbitals, got), choose(got, response)])
    both = jnp.pad(both, ((0, 0), (0, 0), (0, WIDE - NOCC)))

    one, two = ("x", "y"), ("y", "x")
    at_one, at_two = choose(x, y), choose(y, x)
    shape = (CORE, 4, OWN, WIDE)
    stage = put(jnp.zeros(shape, bf16), both[:, None], d1=at_one)
    ahead = send(both, around(one, 1, False))
    behind = send(both, around(one, -1, False))
    far = send(both, around(one, 2, False))
    stage = put(stage, ahead[:, None], d1=(at_one - 1) % 4)
    stage = put(stage, behind[:, None], d1=(at_one + 1) % 4)
    stage = put(stage, far[:, None], d1=(at_one + 2) % 4)
    stage, other_blocks = lax.optimization_barrier((stage, other_blocks))

    main, rest = stage[:, :, :MAIN], stage[:, :, MAIN:]
    zz = ("z", "z")
    main_ahead = send(main, around(zz, 1, True))
    rest_ahead = send(rest, around(two, 1, False))
    rest_behind = send(rest, around(two, -1, False))
    main_far = send(main_ahead, around(zz, 1, True))
    main_behind = send(main, around(zz, -1, True))
    rest_far = send(rest, around(two, 2, False))

    lists = lax.optimization_barrier((block_rows[0], block_cols[0], block_count[0], rest_ahead))
    lists = jnp.concatenate([lists[0] % ROW_BLOCKS, lists[1], lists[2]])
    lists = jnp.pad(lists, (0, 256 - 2 * SLOTS - 1))[None]

    mains = [jnp.zeros((ZH, ZL, 4, MAIN, WIDE), bf16)] * 2
    for array, at in (
        (main, z),
        (main_ahead, (z - sign) % 4),
        (main_behind, (z + sign) % 4),
        (main_far, (z + 2) % 4),
    ):
        mains = [put(into, array[i][None, None], d0=at // ZL, d1=at % ZL) for i, into in enumerate(mains)]
    into = jnp.zeros((CORE, 4, 4, OWN - MAIN, WIDE), bf16)
    for array, at in (
        (rest, at_two),
        (rest_ahead, (at_two - 1) % 4),
        (rest_behind, (at_two + 1) % 4),
        (rest_far, (at_two + 2) % 4),
    ):
        into = put(into, array[:, :, None], d2=at)
    rest = into

    ahead, behind = around(two, 1, False), around(two, -1, False)
    mains, rest, lists = lax.optimization_barrier((mains, rest, lists))
    ahead_0 = send(mains[0], ahead)
    behind_1 = send(mains[1], behind)
    rest_ahead = send(rest, around(zz, 1, True))
    rest_behind = send(rest, around(zz, -1, True))
    meta = jnp.concatenate([lists, swap_cores(lists)])
    ahead_1 = send_after(mains[1], ahead, ahead_0, meta)
    behind_0 = send_after(mains[0], behind, behind_1, meta)
    far_0 = send(ahead_0, ahead)
    far_1 = send_after(behind_1, behind, rest_ahead)
    rest_far = send_after(rest_ahead, around(zz, 1, True), rest_behind)
    arrays = (
        (mains[0], ahead_0, behind_0, far_0),
        (mains[1], ahead_1, behind_1, far_1),
    )
    mains = []
    for four in arrays:
        into = jnp.zeros((4, *four[0].shape), bf16)
        for array, at in zip(four, (at_two, (at_two - 1) % 4, (at_two + 1) % 4, (at_two + 2) % 4)):
            into = put(into, array[None], d0=at)
        mains.append(into)
    into = jnp.zeros((ZH, CORE, ZL, 4, 4, OWN - MAIN, WIDE), bf16)
    for array, at in (
        (rest, z),
        (rest_ahead, (z - sign) % 4),
        (rest_behind, (z + sign) % 4),
        (rest_far, (z + 2) % 4),
    ):
        into = put(into, array[None, :, None], d0=at // ZL, d2=at % ZL)
    rest = into

    slab = own_slab(*mains, rest).reshape(ROWS, WIDE)
    theirs = swap_cores(slab)
    second_half, panels = multiply(1, meta, other_blocks, *mains, rest)

    def add(*arrays):
        return sum(a.astype(f32) for a in arrays)

    xx = ("x", "x")
    ahead, behind = around(xx, 1, True), around(xx, -1, True)
    opposite = around(xx, 2, True)
    half_mine, to_low = cross(chunks_low, 2, second_half, slab, theirs)
    from_low = swap_low(to_low)
    panels, half_mine = lax.optimization_barrier((panels, half_mine))
    first_half = multiply(0, meta, own_blocks, panels)
    mine, to_ahead, to_behind, to_far = cross(chunks_x, 4, first_half, slab, theirs)
    parts = (mine, send(to_ahead, ahead), send(to_behind, behind), send(to_far, opposite))
    own, *sent = sum_chunks(chunks_x, 4, half_mine, from_low)
    second = (own, send(sent[0], ahead), send(sent[1], behind), send(sent[2], opposite))
    parts, _ = lax.optimization_barrier((parts, sent))
    own, sent = sum_chunks(chunks_low, 2, *parts)
    first_shard = add(own, swap_low(sent))
    second_shard = add(*second)

    last = (x == X - 1) & (zl == ZL - 1)
    at = jnp.arange(SHARD, dtype=jnp.int32)[:, None] + (CROSS - SHARD)

    def weights_of(shard):
        own = jnp.where(last & (at == NOCC), shard, shard * (1.0 / NB)).astype(bf16)
        return jnp.where(last & (at == NOCC + 1), own[NOCC - (CROSS - SHARD)][None], swap_cores(own))

    def parts_x(array):
        return array, send(array, ahead), send(array, behind), send(array, opposite)

    def joined(parts, places):
        n = parts[0].shape[0]
        into = jnp.zeros((n * len(parts), WIDE), bf16)
        for part, k in zip(parts, places):
            into = lax.dynamic_update_slice(into, part, ((k % len(parts)) * n, 0))
        return into

    array = weights_of(first_shard)
    from_low = swap_low(array)
    by_x = joined((array, from_low), (zl, 1 - zl))
    by_low = joined(parts_x(weights_of(second_shard)), (x, x - sign, x + sign, x + 2))
    by_low, by_x = lax.optimization_barrier((by_low, by_x))
    keep, give = exchange((first_half, second_half), (by_low, swap_low(by_low)), parts_x(by_x))

    yy = ("y", "y")
    ahead, behind, opposite = around(yy, 1, True), around(yy, -1, True), around(yy, 2, True)
    own, *sent = sum_chunks(chunks_y, 4, keep, swap_cores(give))
    part = own + add(send(sent[0], ahead), send(sent[1], behind), send(sent[2], opposite))
    part = (part + swap_high(part)).astype(bf16)
    into = jnp.zeros((CROSS // 2, ROWS), bf16)
    for k, array in (
        (y, part),
        (y - sign, send(part, ahead)),
        (y + sign, send(part, behind)),
        (y + 2, send(part, opposite)),
    ):
        into = lax.dynamic_update_slice(into, array, ((k % Y) * SHARD, 0))
    others = swap_cores(into)
    return jnp.concatenate([choose(into, others), choose(others, into)])[:NOCC].astype(f32).T


def solution(mesh):
    in_specs = (
        P("aux", "row", None, None),
        P("aux", "row"),
        P("aux", "row"),
        P("aux", "row"),
        P(("aux", "row"), None),
        P(("aux", "row"), None),
    )
    out_specs = P("row", None)
    return jax.shard_map(local, mesh=mesh, in_specs=in_specs, out_specs=out_specs, check_vma=False)
```

```python
import itertools

import jax
import jax.numpy as jnp
from jax import lax
from jax.experimental import pallas as pl
from jax.experimental.pallas import tpu as pltpu
from jax.sharding import PartitionSpec as P

Y, ZH, CORE, X, ZL = 4, 2, 2, 4, 2
AXES = ("aux", "row")
BLK = 128
ROW_BLOCKS = 6
ROWS = ROW_BLOCKS * BLK
SLOTS = 96
NB = 6144
NOCC = 800
WIDE = 896
CROSS = 832
SHARD = CROSS // 8
OWN = 48
STEP = 4
UNROLL = 3
MAIN = 32
PARTS = 24
bf16, f32 = jnp.bfloat16, jnp.float32


def permutation(move):
    pairs = []
    for y, zh, c, x, zl in itertools.product(range(Y), range(ZH), range(CORE), range(X), range(ZL)):
        at = dict(y=y, z=zh * ZL + zl, c=c, x=x)
        to = move(dict(at))

        def flat(d):
            return (((d["y"] * ZH + d["z"] // ZL) * CORE + d["c"]) * X + d["x"]) * ZL + d["z"] % ZL

        pairs.append((flat(at), flat(to)))
    return pairs


def around(axes, by, mirror):
    def move(d):
        axis = axes[d["c"]]
        d[axis] = (d[axis] + (-by if mirror and d["c"] else by)) % 4
        return d

    return permutation(move)


def other_core(d):
    d["c"] = 1 - d["c"]
    return d


def other_low(d):
    d["z"] = d["z"] ^ 1
    return d


def other_high(d):
    d["z"] = d["z"] ^ 2
    return d


def send(array, pairs):
    return lax.ppermute(array, AXES, pairs)


def swap_cores(array):
    return send(array, permutation(other_core))


def swap_low(array):
    return send(array, permutation(other_low))


def swap_high(array):
    return send(array, permutation(other_high))


def here():
    aux, row = lax.axis_index("aux"), lax.axis_index("row")
    return aux % CORE, row, row // ZL, row % ZL


def place_parts(main0, main1, rest, at_two, at_z, held, sems):
    core = here()[0]
    copies = []
    for a in range(4):
        y, x = jnp.where(core == 0, at_two, a), jnp.where(core == 0, a, at_two)
        for c, main in enumerate((main0, main1)):
            copies.append((main.at[:, :, a], held.at[y, :, c, x, :, pl.ds(0, MAIN)]))
        for b in range(4):
            y, x = jnp.where(core == 0, b, a), jnp.where(core == 0, a, b)
            into = held.at[y, at_z // ZL, :, x, at_z % ZL, pl.ds(MAIN, OWN - MAIN)]
            copies.append((rest.at[:, a, b], into))
    return [pltpu.make_async_copy(*copy, sems.at[i]) for i, copy in enumerate(copies)]


def positions():
    aux = lax.axis_index("aux")
    core, _, x, zl = here()
    y, z = aux // (ZH * CORE), aux // CORE % ZH * ZL + zl
    return jnp.where(core == 0, y, x), z, 1 - 2 * core


def near_kernel(*refs):
    parts, held, sems = refs[:9], refs[9], refs[10]
    at_two, z, sign = positions()
    copies = []
    for k, (two, along) in enumerate(((0, 0), (3, 4 - sign), (1, 4 + sign))):
        where = ((at_two + two) % 4, (z + along) % 4)
        copies += place_parts(*parts[3 * k : 3 * k + 3], *where, held, sems.at[k])
    for copy in copies:
        copy.start()
    for copy in copies:
        copy.wait()


def far_kernel(main0, main1, rest, near, held, slab, sems):
    at_two, z, _ = positions()
    row = here()[1]
    copies = place_parts(main0, main1, rest, (at_two + 2) % 4, (z + 2) % 4, held, sems)
    for copy in copies:
        copy.start()
    for copy in copies:
        copy.wait()
    copy = pltpu.make_async_copy(held.at[row // ZL, row % ZL], slab, sems.at[PARTS])
    copy.start()
    copy.wait()


def panels_and_slab(near, far):
    anywhere = pl.BlockSpec(memory_space=pl.ANY)
    held = jax.ShapeDtypeStruct((Y, ZH, CORE, X, ZL, OWN, WIDE), bf16)
    panels = pl.pallas_call(
        near_kernel,
        out_shape=held,
        in_specs=[anywhere] * 9,
        out_specs=anywhere,
        scratch_shapes=[pltpu.SemaphoreType.DMA((3, PARTS))],
        compiler_params=pltpu.CompilerParams(vmem_limit_bytes=4 * 1024 * 1024),
        name="near",
    )(*near)
    return pl.pallas_call(
        far_kernel,
        out_shape=[held, jax.ShapeDtypeStruct((CORE, X, ZL, OWN, WIDE), bf16)],
        in_specs=[anywhere] * 4,
        out_specs=[anywhere] * 2,
        input_output_aliases={3: 0},
        scratch_shapes=[pltpu.SemaphoreType.DMA((PARTS + 1,))],
        compiler_params=pltpu.CompilerParams(vmem_limit_bytes=4 * 1024 * 1024),
        name="far",
    )(*far, panels)


def list_steps(q, meta, order, counts, steps):
    def clear(i, carry):
        counts[i] = 0
        return carry

    lax.fori_loop(0, ROW_BLOCKS, clear, 0)

    def put(s, carry):
        group = meta[q, s]
        n = counts[group]
        order[group, n] = s
        counts[group] = n + 1
        return carry

    lax.fori_loop(0, meta[q, 2 * SLOTS], put, 0)

    def list_group(group, base):
        n = counts[group]
        for i in range(STEP):
            order[group, n + i] = SLOTS
        many = (n + STEP - 1) // STEP

        def list_step(i, carry):
            steps[base + i, 0] = group
            for k in range(STEP):
                s = order[group, i * STEP + k]
                steps[base + i, 1 + k] = s
                steps[base + i, 1 + STEP + k] = jnp.where(s < SLOTS, meta[q, SLOTS + s], 0)
            return carry

        lax.fori_loop(0, many, list_step, 0)
        return base + many

    many = lax.fori_loop(0, ROW_BLOCKS, list_group, 0)
    for u in range(UNROLL - 1):
        steps[many + u, 0] = ROW_BLOCKS
        for k in range(STEP):
            steps[many + u, 1 + k] = SLOTS
            steps[many + u, 1 + STEP + k] = 0
    return many


def multiply_kernel(q, meta, factors, held, out, total, order, counts, steps):
    total[...] = jnp.zeros_like(total)
    many = list_steps(q, meta, order, counts, steps)
    panels = held.reshape(NB, WIDE)

    def some(i, carry):
        products = []
        for u in range(UNROLL):
            left, right = [], []
            for k in range(STEP):
                slot = steps[i * UNROLL + u, 1 + k]
                block = factors[jnp.minimum(slot, SLOTS - 1)]
                left.append(jnp.where(slot < SLOTS, block, jnp.zeros_like(block)))
                column = steps[i * UNROLL + u, 1 + STEP + k]
                right.append(panels[pl.ds(pl.multiple_of(column * BLK, BLK), BLK), :])
            products.append(
                jnp.dot(jnp.concatenate(left, axis=1), jnp.concatenate(right, axis=0), preferred_element_type=f32)
            )
        for u in range(UNROLL):
            total[steps[i * UNROLL + u, 0]] += products[u]
        return carry

    lax.fori_loop(0, (many + UNROLL - 1) // UNROLL, some, 0)
    for group in range(ROW_BLOCKS):
        out[group * BLK : (group + 1) * BLK, :] = total[group].astype(bf16)


def multiply(q, meta, factors, panels):
    most = SLOTS // STEP + ROW_BLOCKS + UNROLL
    vmem = pl.BlockSpec(memory_space=pltpu.VMEM)

    def kernel(*refs):
        multiply_kernel(q, *refs)

    return pl.pallas_call(
        kernel,
        out_shape=jax.ShapeDtypeStruct((ROWS, WIDE), bf16),
        in_specs=[pl.BlockSpec(memory_space=pltpu.SMEM), vmem, vmem],
        out_specs=vmem,
        scratch_shapes=[
            pltpu.VMEM((ROW_BLOCKS + 1, BLK, WIDE), f32),
            pltpu.SMEM((ROW_BLOCKS, SLOTS + 2 * STEP), jnp.int32),
            pltpu.SMEM((ROW_BLOCKS,), jnp.int32),
            pltpu.SMEM((most, 1 + 2 * STEP), jnp.int32),
        ],
        compiler_params=pltpu.CompilerParams(vmem_limit_bytes=24 * 1024 * 1024),
        cost_estimate=pl.CostEstimate(flops=96 * 2 * 128 * 128 * 896, bytes_accessed=2**23, transcendentals=0),
        name="multiply",
    )(meta, factors, panels)


def cross_kernel(starts, half, slab, theirs, *refs):
    outs, used, product = refs[:-2], refs[-2], refs[-1]
    core, row, _, _ = here()
    used[...] = jnp.where(core == 0, slab[...], theirs[...])
    product[...] = lax.dot_general(
        half[...], used[...], (((0,), (0,)), ((), ())), preferred_element_type=f32
    ).astype(bf16)
    value = jnp.sum(half[...].astype(f32) * theirs[...].astype(f32), keepdims=True)
    high = value.astype(bf16).astype(f32)
    middle = (value - high).astype(bf16).astype(f32)
    low = value - high - middle
    lane = lax.broadcasted_iota(jnp.int32, (16, WIDE), 1)
    line = lax.broadcasted_iota(jnp.int32, (16, WIDE), 0)
    coded = jnp.where(
        lane == 3 * row, high, jnp.where(lane == 3 * row + 1, middle, jnp.where(lane == 3 * row + 2, low, 0.0))
    )
    product[NOCC : NOCC + 16, :] = jnp.where(line == 0, coded, 0.0).astype(bf16)
    for out, start in zip(outs, starts()):
        n = out.shape[0]
        out[...] = product[pl.ds(pl.multiple_of(start * n, n), n), :]


def chunks_x():
    core, _, x, _ = here()
    return x, (x + 1 - 2 * core) % X, (x - 1 + 2 * core) % X, (x + 2) % X


def chunks_low():
    zl = here()[3]
    return zl, 1 - zl


def cross(starts, many, half, slab, theirs):
    def kernel(*refs):
        cross_kernel(starts, *refs)

    return pl.pallas_call(
        kernel,
        out_shape=[jax.ShapeDtypeStruct((CROSS // many, WIDE), bf16)] * many,
        in_specs=[pl.BlockSpec(memory_space=pltpu.VMEM)] * 3,
        out_specs=[pl.BlockSpec(memory_space=pltpu.VMEM)] * many,
        scratch_shapes=[pltpu.VMEM((ROWS, WIDE), bf16), pltpu.VMEM((WIDE, WIDE), bf16)],
        compiler_params=pltpu.CompilerParams(vmem_limit_bytes=30 * 1024 * 1024),
        cost_estimate=pl.CostEstimate(flops=2 * 768 * 896 * 896, bytes_accessed=2**23, transcendentals=0),
        name="cross",
    )(half, slab, theirs)


def sum_kernel(starts, many, *refs):
    arrays, outs, total = refs[:many], refs[many:-1], refs[-1]
    total[...] = sum(array[...].astype(f32) for array in arrays)
    for out, start in zip(outs, starts()):
        n = out.shape[0]
        out[...] = total[pl.ds(pl.multiple_of(start * n, n), n), :].astype(out.dtype)


def sum_chunks(starts, pieces, *arrays):
    n, width = arrays[0].shape
    own = jax.ShapeDtypeStruct((n // pieces, width), f32)
    sent = jax.ShapeDtypeStruct((n // pieces, width), bf16)

    def kernel(*refs):
        sum_kernel(starts, len(arrays), *refs)

    return pl.pallas_call(
        kernel,
        out_shape=[own] + [sent] * (pieces - 1),
        in_specs=[pl.BlockSpec(memory_space=pltpu.VMEM)] * len(arrays),
        out_specs=[pl.BlockSpec(memory_space=pltpu.VMEM)] * pieces,
        scratch_shapes=[pltpu.VMEM((n, width), f32)],
        compiler_params=pltpu.CompilerParams(vmem_limit_bytes=24 * 1024 * 1024),
        cost_estimate=pl.CostEstimate(flops=n * width, bytes_accessed=2**21, transcendentals=0),
        name="sum_chunks",
    )(*arrays)


def chunks_y():
    y, c = lax.axis_index("aux") // (ZH * CORE), here()[0]
    return y, (y + 1 - 2 * c) % Y, (y - 1 + 2 * c) % Y, (y + 2) % Y


def exchange_kernel(*refs):
    halves, parts, (keep, give, held, weights, turned, sems) = refs[:2], refs[2:8], refs[8:]
    core, _, _, _ = here()
    copies = [pltpu.make_async_copy(halves[q], held.at[q], sems.at[6 + q]) for q in range(2)]
    for i, (q, at) in enumerate([(0, at) for at in chunks_low()] + [(1, at) for at in chunks_arrived()]):
        n = parts[i].shape[0]
        into = weights.at[q, pl.ds(pl.multiple_of(at * n, n), n), :]
        copies.append(pltpu.make_async_copy(parts[i], into, sems.at[i]))
    for copy in copies:
        copy.start()
    for q in range(2):
        weights[q, CROSS:, :] = jnp.zeros((WIDE - CROSS, WIDE), bf16)
    for copy in copies:
        copy.wait()
    line = lax.broadcasted_iota(jnp.int32, (16, WIDE), 0)
    total = None
    for q in range(2):
        codes = jnp.where(line == 0, weights[q, NOCC : NOCC + 16, :].astype(f32), 0.0)
        codes = codes + jnp.where(line == 1, weights[1 - q, NOCC : NOCC + 16, :].astype(f32), 0.0)
        coulomb = jnp.sum(codes, keepdims=True) * (1.0 / NB)
        factor = jnp.where(core == 0, 2.0 * coulomb, 0.0)
        own = held[q]
        term = factor * own.astype(f32) - jnp.dot(own, weights[q], preferred_element_type=f32)
        total = term if total is None else total + term
    turned[...] = total.T
    n = CROSS // 2
    keep[...] = turned[pl.ds(pl.multiple_of(core * n, n), n), :]
    give[...] = turned[pl.ds(pl.multiple_of((1 - core) * n, n), n), :]


def chunks_arrived():
    x, ahead, behind, far = chunks_x()
    return x, behind, ahead, far


def exchange(halves, low_parts, x_parts):
    return pl.pallas_call(
        exchange_kernel,
        out_shape=[jax.ShapeDtypeStruct((CROSS // 2, ROWS), f32)] * 2,
        in_specs=[pl.BlockSpec(memory_space=pl.ANY)] * 8,
        out_specs=[pl.BlockSpec(memory_space=pltpu.VMEM)] * 2,
        scratch_shapes=[
            pltpu.VMEM((2, ROWS, WIDE), bf16),
            pltpu.VMEM((2, WIDE, WIDE), bf16),
            pltpu.VMEM((WIDE, ROWS), f32),
            pltpu.SemaphoreType.DMA((8,)),
        ],
        compiler_params=pltpu.CompilerParams(vmem_limit_bytes=48 * 1024 * 1024),
        cost_estimate=pl.CostEstimate(flops=4 * 768 * 896 * 896, bytes_accessed=2**23, transcendentals=0),
        name="exchange",
    )(*halves, *low_parts, *x_parts)


def widen_kernel(own, others, out):
    core, n = here()[0], CROSS // 2
    out[:n, :] = jnp.where(core == 0, own[...], others[...]).astype(f32)
    out[n:, :] = jnp.where(core == 0, others[...], own[...])[: NOCC - n].astype(f32)


def widen(own, others):
    return pl.pallas_call(
        widen_kernel,
        out_shape=jax.ShapeDtypeStruct((NOCC, ROWS), f32),
        in_specs=[pl.BlockSpec(memory_space=pltpu.VMEM)] * 2,
        out_specs=pl.BlockSpec(memory_space=pltpu.VMEM),
        compiler_params=pltpu.CompilerParams(vmem_limit_bytes=16 * 1024 * 1024),
        name="widen",
    )(own, others)


def local(factors, block_rows, block_cols, block_count, orbitals, response):
    aux, row = lax.axis_index("aux"), lax.axis_index("row")
    y, zh, c = aux // (ZH * CORE), (aux // CORE) % ZH, aux % CORE
    x, zl = row // ZL, row % ZL
    z = zh * ZL + zl
    sign = 1 - 2 * c
    first = c == 0

    def choose(a, b):
        return jnp.where(first, a, b)

    def send_after(array, pairs, *earlier):
        return send(lax.optimization_barrier((array, *earlier))[0], pairs)

    def put(into, array, **at):
        index = [jnp.int32(0)] * into.ndim
        for dim, i in at.items():
            index[int(dim[1:])] = i
        return lax.dynamic_update_slice(into, array, index)

    got = send(choose(response, orbitals), permutation(other_core))
    own_blocks = factors[0]
    other_blocks = send_after(own_blocks, permutation(other_core), got)
    both = jnp.stack([choose(orbitals, got), choose(got, response)])
    both = jnp.pad(both, ((0, 0), (0, 0), (0, WIDE - NOCC)))

    one, two = ("x", "y"), ("y", "x")
    at_one, at_two = choose(x, y), choose(y, x)
    shape = (CORE, 4, OWN, WIDE)
    stage = put(jnp.zeros(shape, bf16), both[:, None], d1=at_one)
    ahead = send(both, around(one, 1, False))
    behind = send(both, around(one, -1, False))
    far = send(both, around(one, 2, False))
    stage = put(stage, ahead[:, None], d1=(at_one - 1) % 4)
    stage = put(stage, behind[:, None], d1=(at_one + 1) % 4)
    stage = put(stage, far[:, None], d1=(at_one + 2) % 4)
    stage, other_blocks = lax.optimization_barrier((stage, other_blocks))

    main, rest = stage[:, :, :MAIN], stage[:, :, MAIN:]
    zz = ("z", "z")
    main_ahead = send(main, around(zz, 1, True))
    rest_ahead = send(rest, around(two, 1, False))
    rest_behind = send(rest, around(two, -1, False))
    main_far = send(main_ahead, around(zz, 1, True))
    main_behind = send(main, around(zz, -1, True))
    rest_far = send(rest, around(two, 2, False))

    lists = lax.optimization_barrier((block_rows[0], block_cols[0], block_count[0], rest_ahead))
    lists = jnp.concatenate([lists[0] % ROW_BLOCKS, lists[1], lists[2]])
    lists = jnp.pad(lists, (0, 256 - 2 * SLOTS - 1))[None]

    mains = [jnp.zeros((ZH, ZL, 4, MAIN, WIDE), bf16)] * 2
    for array, at in (
        (main, z),
        (main_ahead, (z - sign) % 4),
        (main_behind, (z + sign) % 4),
        (main_far, (z + 2) % 4),
    ):
        mains = [put(into, array[i][None, None], d0=at // ZL, d1=at % ZL) for i, into in enumerate(mains)]
    into = jnp.zeros((CORE, 4, 4, OWN - MAIN, WIDE), bf16)
    for array, at in (
        (rest, at_two),
        (rest_ahead, (at_two - 1) % 4),
        (rest_behind, (at_two + 1) % 4),
        (rest_far, (at_two + 2) % 4),
    ):
        into = put(into, array[:, :, None], d2=at)
    rest = into

    ahead, behind = around(two, 1, False), around(two, -1, False)
    mains, rest, lists = lax.optimization_barrier((mains, rest, lists))
    ahead_0 = send(mains[0], ahead)
    behind_1 = send(mains[1], behind)
    rest_ahead = send(rest, around(zz, 1, True))
    rest_behind = send(rest, around(zz, -1, True))
    meta = jnp.concatenate([lists, swap_cores(lists)])
    ahead_1 = send_after(mains[1], ahead, ahead_0, meta)
    behind_0 = send_after(mains[0], behind, behind_1, meta)
    far_0 = send(ahead_0, ahead)
    far_1 = send_after(behind_1, behind, rest_ahead)
    rest_far = send_after(rest_ahead, around(zz, 1, True), rest_behind)
    near = [mains[0], mains[1], rest, ahead_0, ahead_1, rest_ahead, behind_0, behind_1, rest_behind]
    panels, slab = panels_and_slab(near, (far_0, far_1, rest_far))
    slab = slab.reshape(ROWS, WIDE)
    theirs = swap_cores(slab)
    second_half = multiply(1, meta, other_blocks, panels)

    def add(*arrays):
        return sum(a.astype(f32) for a in arrays)

    xx = ("x", "x")
    ahead, behind = around(xx, 1, True), around(xx, -1, True)
    opposite = around(xx, 2, True)
    half_mine, to_low = cross(chunks_low, 2, second_half, slab, theirs)
    from_low = swap_low(to_low)
    panels, half_mine = lax.optimization_barrier((panels, half_mine))
    first_half = multiply(0, meta, own_blocks, panels)
    mine, to_ahead, to_behind, to_far = cross(chunks_x, 4, first_half, slab, theirs)
    parts = (mine, send(to_ahead, ahead), send(to_behind, behind), send(to_far, opposite))
    own, *sent = sum_chunks(chunks_x, 4, half_mine, from_low)
    second = (own, send(sent[0], ahead), send(sent[1], behind), send(sent[2], opposite))
    parts, _ = lax.optimization_barrier((parts, sent))
    own, sent = sum_chunks(chunks_low, 2, *parts)
    first_shard = add(own, swap_low(sent))
    second_shard = add(*second)

    last = (x == X - 1) & (zl == ZL - 1)
    at = jnp.arange(SHARD, dtype=jnp.int32)[:, None] + (CROSS - SHARD)

    def weights_of(shard):
        own = jnp.where(last & (at == NOCC), shard, shard * (1.0 / NB)).astype(bf16)
        return jnp.where(last & (at == NOCC + 1), own[NOCC - (CROSS - SHARD)][None], swap_cores(own))

    def parts_x(array):
        return array, send(array, ahead), send(array, behind), send(array, opposite)

    def joined(parts, places):
        n = parts[0].shape[0]
        into = jnp.zeros((n * len(parts), WIDE), bf16)
        for part, k in zip(parts, places):
            into = lax.dynamic_update_slice(into, part, ((k % len(parts)) * n, 0))
        return into

    array = weights_of(first_shard)
    from_low = swap_low(array)
    by_x = joined((array, from_low), (zl, 1 - zl))
    by_low = joined(parts_x(weights_of(second_shard)), (x, x - sign, x + sign, x + 2))
    by_low, by_x = lax.optimization_barrier((by_low, by_x))
    keep, give = exchange((first_half, second_half), (by_low, swap_low(by_low)), parts_x(by_x))

    yy = ("y", "y")
    ahead, behind, opposite = around(yy, 1, True), around(yy, -1, True), around(yy, 2, True)
    own, *sent = sum_chunks(chunks_y, 4, keep, swap_cores(give))
    part = own + add(send(sent[0], ahead), send(sent[1], behind), send(sent[2], opposite))
    part = (part + swap_high(part)).astype(bf16)
    into = jnp.zeros((CROSS // 2, ROWS), bf16)
    for k, array in (
        (y, part),
        (y - sign, send(part, ahead)),
        (y + sign, send(part, behind)),
        (y + 2, send(part, opposite)),
    ):
        into = lax.dynamic_update_slice(into, array, ((k % Y) * SHARD, 0))
    return widen(into, swap_cores(into)).T


def solution(mesh):
    in_specs = (
        P("aux", "row", None, None),
        P("aux", "row"),
        P("aux", "row"),
        P("aux", "row"),
        P(("aux", "row"), None),
        P(("aux", "row"), None),
    )
    out_specs = P("row", None)
    return jax.shard_map(local, mesh=mesh, in_specs=in_specs, out_specs=out_specs, check_vma=False)
```

```python
import itertools

import jax
import jax.numpy as jnp
from jax import lax
from jax.experimental import pallas as pl
from jax.experimental.pallas import tpu as pltpu
from jax.sharding import PartitionSpec as P

Y, ZH, CORE, X, ZL = 4, 2, 2, 4, 2
AXES = ("aux", "row")
BLK = 128
ROW_BLOCKS = 6
ROWS = ROW_BLOCKS * BLK
SLOTS = 96
NB = 6144
NOCC = 800
WIDE = 896
CROSS = 832
SHARD = CROSS // 8
OWN = 48
STEP = 4
UNROLL = 3
MAIN = 32
PARTS = 24
bf16, f32 = jnp.bfloat16, jnp.float32


def permutation(move):
    pairs = []
    for y, zh, c, x, zl in itertools.product(range(Y), range(ZH), range(CORE), range(X), range(ZL)):
        at = dict(y=y, z=zh * ZL + zl, c=c, x=x)
        to = move(dict(at))

        def flat(d):
            return (((d["y"] * ZH + d["z"] // ZL) * CORE + d["c"]) * X + d["x"]) * ZL + d["z"] % ZL

        pairs.append((flat(at), flat(to)))
    return pairs


def around(axes, by, mirror):
    def move(d):
        axis = axes[d["c"]]
        d[axis] = (d[axis] + (-by if mirror and d["c"] else by)) % 4
        return d

    return permutation(move)


def other_core(d):
    d["c"] = 1 - d["c"]
    return d


def other_low(d):
    d["z"] = d["z"] ^ 1
    return d


def other_high(d):
    d["z"] = d["z"] ^ 2
    return d


def send(array, pairs):
    return lax.ppermute(array, AXES, pairs)


def swap_cores(array):
    return send(array, permutation(other_core))


def swap_low(array):
    return send(array, permutation(other_low))


def swap_high(array):
    return send(array, permutation(other_high))


def here():
    aux, row = lax.axis_index("aux"), lax.axis_index("row")
    return aux % CORE, row, row // ZL, row % ZL


def place_parts(main0, main1, rest, at_two, at_z, held, sems):
    core = here()[0]
    copies = []
    for a in range(4):
        y, x = jnp.where(core == 0, at_two, a), jnp.where(core == 0, a, at_two)
        for c, main in enumerate((main0, main1)):
            copies.append((main.at[:, :, a], held.at[y, :, c, x, :, pl.ds(0, MAIN)]))
        for b in range(4):
            y, x = jnp.where(core == 0, b, a), jnp.where(core == 0, a, b)
            into = held.at[y, at_z // ZL, :, x, at_z % ZL, pl.ds(MAIN, OWN - MAIN)]
            copies.append((rest.at[:, a, b], into))
    return [pltpu.make_async_copy(*copy, sems.at[i]) for i, copy in enumerate(copies)]


def positions():
    aux = lax.axis_index("aux")
    core, _, x, zl = here()
    y, z = aux // (ZH * CORE), aux // CORE % ZH * ZL + zl
    return jnp.where(core == 0, y, x), z, 1 - 2 * core


def near_kernel(*refs):
    parts, held, sems = refs[:9], refs[9], refs[10]
    at_two, z, sign = positions()
    copies = []
    for k, (two, along) in enumerate(((0, 0), (3, 4 - sign), (1, 4 + sign))):
        where = ((at_two + two) % 4, (z + along) % 4)
        copies += place_parts(*parts[3 * k : 3 * k + 3], *where, held, sems.at[k])
    for copy in copies:
        copy.start()
    for copy in copies:
        copy.wait()


def far_kernel(main0, main1, rest, near, held, slab, sems):
    at_two, z, _ = positions()
    row = here()[1]
    copies = place_parts(main0, main1, rest, (at_two + 2) % 4, (z + 2) % 4, held, sems)
    for copy in copies:
        copy.start()
    for copy in copies:
        copy.wait()
    copy = pltpu.make_async_copy(held.at[row // ZL, row % ZL], slab, sems.at[PARTS])
    copy.start()
    copy.wait()


def panels_and_slab(near, far):
    anywhere = pl.BlockSpec(memory_space=pl.ANY)
    held = jax.ShapeDtypeStruct((Y, ZH, CORE, X, ZL, OWN, WIDE), bf16)
    panels = pl.pallas_call(
        near_kernel,
        out_shape=held,
        in_specs=[anywhere] * 9,
        out_specs=anywhere,
        scratch_shapes=[pltpu.SemaphoreType.DMA((3, PARTS))],
        compiler_params=pltpu.CompilerParams(vmem_limit_bytes=4 * 1024 * 1024),
        name="near",
    )(*near)
    return pl.pallas_call(
        far_kernel,
        out_shape=[held, jax.ShapeDtypeStruct((CORE, X, ZL, OWN, WIDE), bf16)],
        in_specs=[anywhere] * 4,
        out_specs=[anywhere] * 2,
        input_output_aliases={3: 0},
        scratch_shapes=[pltpu.SemaphoreType.DMA((PARTS + 1,))],
        compiler_params=pltpu.CompilerParams(vmem_limit_bytes=4 * 1024 * 1024),
        name="far",
    )(*far, panels)


def list_steps(q, meta, order, counts, steps):
    def clear(i, carry):
        counts[i] = 0
        return carry

    lax.fori_loop(0, ROW_BLOCKS, clear, 0)

    def put(s, carry):
        group = meta[q, s]
        n = counts[group]
        order[group, n] = s
        counts[group] = n + 1
        return carry

    lax.fori_loop(0, meta[q, 2 * SLOTS], put, 0)

    def list_group(group, base):
        n = counts[group]
        for i in range(STEP):
            order[group, n + i] = SLOTS
        many = (n + STEP - 1) // STEP

        def list_step(i, carry):
            steps[base + i, 0] = group
            for k in range(STEP):
                s = order[group, i * STEP + k]
                steps[base + i, 1 + k] = s
                steps[base + i, 1 + STEP + k] = jnp.where(s < SLOTS, meta[q, SLOTS + s], 0)
            return carry

        lax.fori_loop(0, many, list_step, 0)
        return base + many

    many = lax.fori_loop(0, ROW_BLOCKS, list_group, 0)
    for u in range(UNROLL - 1):
        steps[many + u, 0] = ROW_BLOCKS
        for k in range(STEP):
            steps[many + u, 1 + k] = SLOTS
            steps[many + u, 1 + STEP + k] = 0
    return many


def multiply_kernel(q, meta, factors, held, out, total, order, counts, steps):
    total[...] = jnp.zeros_like(total)
    many = list_steps(q, meta, order, counts, steps)
    panels = held.reshape(NB, WIDE)

    def some(i, carry):
        products = []
        for u in range(UNROLL):
            left, right = [], []
            for k in range(STEP):
                slot = steps[i * UNROLL + u, 1 + k]
                block = factors[jnp.minimum(slot, SLOTS - 1)]
                left.append(jnp.where(slot < SLOTS, block, jnp.zeros_like(block)))
                column = steps[i * UNROLL + u, 1 + STEP + k]
                right.append(panels[pl.ds(pl.multiple_of(column * BLK, BLK), BLK), :])
            products.append(
                jnp.dot(jnp.concatenate(left, axis=1), jnp.concatenate(right, axis=0), preferred_element_type=f32)
            )
        for u in range(UNROLL):
            total[steps[i * UNROLL + u, 0]] += products[u]
        return carry

    lax.fori_loop(0, (many + UNROLL - 1) // UNROLL, some, 0)
    for group in range(ROW_BLOCKS):
        out[group * BLK : (group + 1) * BLK, :] = total[group].astype(bf16)


def multiply(q, meta, factors, panels):
    most = SLOTS // STEP + ROW_BLOCKS + UNROLL
    vmem = pl.BlockSpec(memory_space=pltpu.VMEM)

    def kernel(*refs):
        multiply_kernel(q, *refs)

    return pl.pallas_call(
        kernel,
        out_shape=jax.ShapeDtypeStruct((ROWS, WIDE), bf16),
        in_specs=[pl.BlockSpec(memory_space=pltpu.SMEM), vmem, vmem],
        out_specs=vmem,
        scratch_shapes=[
            pltpu.VMEM((ROW_BLOCKS + 1, BLK, WIDE), f32),
            pltpu.SMEM((ROW_BLOCKS, SLOTS + 2 * STEP), jnp.int32),
            pltpu.SMEM((ROW_BLOCKS,), jnp.int32),
            pltpu.SMEM((most, 1 + 2 * STEP), jnp.int32),
        ],
        compiler_params=pltpu.CompilerParams(vmem_limit_bytes=24 * 1024 * 1024),
        cost_estimate=pl.CostEstimate(flops=96 * 2 * 128 * 128 * 896, bytes_accessed=2**23, transcendentals=0),
        name="multiply",
    )(meta, factors, panels)


def cross_kernel(starts, half, slab, theirs, *refs):
    outs, used, product = refs[:-2], refs[-2], refs[-1]
    core, row, _, _ = here()
    used[...] = jnp.where(core == 0, slab[...], theirs[...])
    product[...] = lax.dot_general(
        half[...], used[...], (((0,), (0,)), ((), ())), preferred_element_type=f32
    ).astype(bf16)
    value = jnp.sum(half[...].astype(f32) * theirs[...].astype(f32), keepdims=True)
    high = value.astype(bf16).astype(f32)
    middle = (value - high).astype(bf16).astype(f32)
    low = value - high - middle
    lane = lax.broadcasted_iota(jnp.int32, (16, WIDE), 1)
    line = lax.broadcasted_iota(jnp.int32, (16, WIDE), 0)
    coded = jnp.where(
        lane == 3 * row, high, jnp.where(lane == 3 * row + 1, middle, jnp.where(lane == 3 * row + 2, low, 0.0))
    )
    product[NOCC : NOCC + 16, :] = jnp.where(line == 0, coded, 0.0).astype(bf16)
    for out, start in zip(outs, starts()):
        n = out.shape[0]
        out[...] = product[pl.ds(pl.multiple_of(start * n, n), n), :]


def chunks_x():
    core, _, x, _ = here()
    return x, (x + 1 - 2 * core) % X, (x - 1 + 2 * core) % X, (x + 2) % X


def chunks_low():
    zl = here()[3]
    return zl, 1 - zl


def cross(starts, many, half, slab, theirs):
    def kernel(*refs):
        cross_kernel(starts, *refs)

    return pl.pallas_call(
        kernel,
        out_shape=[jax.ShapeDtypeStruct((CROSS // many, WIDE), bf16)] * many,
        in_specs=[pl.BlockSpec(memory_space=pltpu.VMEM)] * 3,
        out_specs=[pl.BlockSpec(memory_space=pltpu.VMEM)] * many,
        scratch_shapes=[pltpu.VMEM((ROWS, WIDE), bf16), pltpu.VMEM((WIDE, WIDE), bf16)],
        compiler_params=pltpu.CompilerParams(vmem_limit_bytes=30 * 1024 * 1024),
        cost_estimate=pl.CostEstimate(flops=2 * 768 * 896 * 896, bytes_accessed=2**23, transcendentals=0),
        name="cross",
    )(half, slab, theirs)


def sum_kernel(starts, many, *refs):
    arrays, outs, total = refs[:many], refs[many:-1], refs[-1]
    total[...] = sum(array[...].astype(f32) for array in arrays)
    for out, start in zip(outs, starts()):
        n = out.shape[0]
        out[...] = total[pl.ds(pl.multiple_of(start * n, n), n), :].astype(out.dtype)


def sum_chunks(starts, pieces, *arrays):
    n, width = arrays[0].shape
    own = jax.ShapeDtypeStruct((n // pieces, width), f32)
    sent = jax.ShapeDtypeStruct((n // pieces, width), bf16)

    def kernel(*refs):
        sum_kernel(starts, len(arrays), *refs)

    return pl.pallas_call(
        kernel,
        out_shape=[own] + [sent] * (pieces - 1),
        in_specs=[pl.BlockSpec(memory_space=pltpu.VMEM)] * len(arrays),
        out_specs=[pl.BlockSpec(memory_space=pltpu.VMEM)] * pieces,
        scratch_shapes=[pltpu.VMEM((n, width), f32)],
        compiler_params=pltpu.CompilerParams(vmem_limit_bytes=24 * 1024 * 1024),
        cost_estimate=pl.CostEstimate(flops=n * width, bytes_accessed=2**21, transcendentals=0),
        name="sum_chunks",
    )(*arrays)


def chunks_y():
    y, c = lax.axis_index("aux") // (ZH * CORE), here()[0]
    return y, (y + 1 - 2 * c) % Y, (y - 1 + 2 * c) % Y, (y + 2) % Y


def exchange_kernel(*refs):
    halves, parts, (keep, give, held, weights, turned, sems) = refs[:2], refs[2:8], refs[8:]
    core, _, _, _ = here()
    copies = [[pltpu.make_async_copy(halves[q], held.at[q], sems.at[6 + q])] for q in range(2)]
    for i, (q, at) in enumerate([(0, at) for at in chunks_low()] + [(1, at) for at in chunks_arrived()]):
        n = parts[i].shape[0]
        into = weights.at[q, pl.ds(pl.multiple_of(at * n, n), n), :]
        copies[q].append(pltpu.make_async_copy(parts[i], into, sems.at[i]))
    for copy in copies[0] + copies[1]:
        copy.start()
    exchanged = []
    for q in range(2):
        weights[q, CROSS:, :] = jnp.zeros((WIDE - CROSS, WIDE), bf16)
        for copy in copies[q]:
            copy.wait()
        exchanged.append(jnp.dot(held[q], weights[q], preferred_element_type=f32))
    line = lax.broadcasted_iota(jnp.int32, (16, WIDE), 0)
    total = None
    for q in range(2):
        codes = jnp.where(line == 0, weights[q, NOCC : NOCC + 16, :].astype(f32), 0.0)
        codes = codes + jnp.where(line == 1, weights[1 - q, NOCC : NOCC + 16, :].astype(f32), 0.0)
        coulomb = jnp.sum(codes, keepdims=True) * (1.0 / NB)
        factor = jnp.where(core == 0, 2.0 * coulomb, 0.0)
        term = factor * held[q].astype(f32) - exchanged[q]
        total = term if total is None else total + term
    turned[...] = total.T
    n = CROSS // 2
    keep[...] = turned[pl.ds(pl.multiple_of(core * n, n), n), :]
    give[...] = turned[pl.ds(pl.multiple_of((1 - core) * n, n), n), :]


def chunks_arrived():
    x, ahead, behind, far = chunks_x()
    return x, behind, ahead, far


def exchange(halves, low_parts, x_parts):
    return pl.pallas_call(
        exchange_kernel,
        out_shape=[jax.ShapeDtypeStruct((CROSS // 2, ROWS), f32)] * 2,
        in_specs=[pl.BlockSpec(memory_space=pl.ANY)] * 8,
        out_specs=[pl.BlockSpec(memory_space=pltpu.VMEM)] * 2,
        scratch_shapes=[
            pltpu.VMEM((2, ROWS, WIDE), bf16),
            pltpu.VMEM((2, WIDE, WIDE), bf16),
            pltpu.VMEM((WIDE, ROWS), f32),
            pltpu.SemaphoreType.DMA((8,)),
        ],
        compiler_params=pltpu.CompilerParams(vmem_limit_bytes=48 * 1024 * 1024),
        cost_estimate=pl.CostEstimate(flops=4 * 768 * 896 * 896, bytes_accessed=2**23, transcendentals=0),
        name="exchange",
    )(*halves, *low_parts, *x_parts)


def widen_kernel(own, others, out):
    core, n = here()[0], CROSS // 2
    out[:n, :] = jnp.where(core == 0, own[...], others[...]).astype(f32)
    out[n:, :] = jnp.where(core == 0, others[...], own[...])[: NOCC - n].astype(f32)


def widen(own, others):
    return pl.pallas_call(
        widen_kernel,
        out_shape=jax.ShapeDtypeStruct((NOCC, ROWS), f32),
        in_specs=[pl.BlockSpec(memory_space=pltpu.VMEM)] * 2,
        out_specs=pl.BlockSpec(memory_space=pltpu.VMEM),
        compiler_params=pltpu.CompilerParams(vmem_limit_bytes=16 * 1024 * 1024),
        name="widen",
    )(own, others)


def local(factors, block_rows, block_cols, block_count, orbitals, response):
    aux, row = lax.axis_index("aux"), lax.axis_index("row")
    y, zh, c = aux // (ZH * CORE), (aux // CORE) % ZH, aux % CORE
    x, zl = row // ZL, row % ZL
    z = zh * ZL + zl
    sign = 1 - 2 * c
    first = c == 0

    def choose(a, b):
        return jnp.where(first, a, b)

    def send_after(array, pairs, *earlier):
        return send(lax.optimization_barrier((array, *earlier))[0], pairs)

    def put(into, array, **at):
        index = [jnp.int32(0)] * into.ndim
        for dim, i in at.items():
            index[int(dim[1:])] = i
        return lax.dynamic_update_slice(into, array, index)

    got = send(choose(response, orbitals), permutation(other_core))
    own_blocks = factors[0]
    other_blocks = send_after(own_blocks, permutation(other_core), got)
    both = jnp.stack([choose(orbitals, got), choose(got, response)])
    both = jnp.pad(both, ((0, 0), (0, 0), (0, WIDE - NOCC)))

    one, two = ("x", "y"), ("y", "x")
    at_one, at_two = choose(x, y), choose(y, x)
    shape = (CORE, 4, OWN, WIDE)
    stage = put(jnp.zeros(shape, bf16), both[:, None], d1=at_one)
    ahead = send(both, around(one, 1, False))
    behind = send(both, around(one, -1, False))
    far = send(both, around(one, 2, False))
    stage = put(stage, ahead[:, None], d1=(at_one - 1) % 4)
    stage = put(stage, behind[:, None], d1=(at_one + 1) % 4)
    stage = put(stage, far[:, None], d1=(at_one + 2) % 4)
    stage, other_blocks = lax.optimization_barrier((stage, other_blocks))

    main, rest = stage[:, :, :MAIN], stage[:, :, MAIN:]
    zz = ("z", "z")
    main_ahead = send(main, around(zz, 1, True))
    main_far = send(main_ahead, around(zz, 1, True))
    main_behind = send_after(main, around(zz, -1, True), main_ahead)
    lists = lax.optimization_barrier((block_rows[0], block_cols[0], block_count[0], ahead))
    lists = jnp.concatenate([lists[0] % ROW_BLOCKS, lists[1], lists[2]])
    lists = jnp.pad(lists, (0, 256 - 2 * SLOTS - 1))[None]
    meta = jnp.concatenate([lists, send_after(lists, permutation(other_core), main_ahead)])
    rest, meta = lax.optimization_barrier((rest, meta))
    rest_ahead = send(rest, around(two, 1, False))
    rest_behind = send(rest, around(two, -1, False))
    rest_far = send(rest, around(two, 2, False))

    mains = [jnp.zeros((ZH, ZL, 4, MAIN, WIDE), bf16)] * 2
    for array, at in (
        (main, z),
        (main_ahead, (z - sign) % 4),
        (main_behind, (z + sign) % 4),
        (main_far, (z + 2) % 4),
    ):
        mains = [put(into, array[i][None, None], d0=at // ZL, d1=at % ZL) for i, into in enumerate(mains)]
    into = jnp.zeros((CORE, 4, 4, OWN - MAIN, WIDE), bf16)
    for array, at in (
        (rest, at_two),
        (rest_ahead, (at_two - 1) % 4),
        (rest_behind, (at_two + 1) % 4),
        (rest_far, (at_two + 2) % 4),
    ):
        into = put(into, array[:, :, None], d2=at)
    rest = into

    ahead, behind = around(two, 1, False), around(two, -1, False)
    mains, rest = lax.optimization_barrier((mains, rest))
    ahead_0 = send(mains[0], ahead)
    behind_1 = send(mains[1], behind)
    rest_ahead = send(rest, around(zz, 1, True))
    rest_behind = send(rest, around(zz, -1, True))
    ahead_1 = send_after(mains[1], ahead, ahead_0)
    behind_0 = send_after(mains[0], behind, behind_1)
    far_0 = send(ahead_0, ahead)
    far_1 = send_after(behind_1, behind, rest_ahead)
    rest_far = send_after(rest_ahead, around(zz, 1, True), rest_behind)
    near = [mains[0], mains[1], rest, ahead_0, ahead_1, rest_ahead, behind_0, behind_1, rest_behind]
    panels, slab = panels_and_slab(near, (far_0, far_1, rest_far))
    slab = slab.reshape(ROWS, WIDE)
    theirs = swap_cores(slab)
    second_half = multiply(1, meta, other_blocks, panels)

    def add(*arrays):
        return sum(a.astype(f32) for a in arrays)

    xx = ("x", "x")
    ahead, behind = around(xx, 1, True), around(xx, -1, True)
    opposite = around(xx, 2, True)
    half_mine, to_low = cross(chunks_low, 2, second_half, slab, theirs)
    from_low = swap_low(to_low)
    panels, half_mine = lax.optimization_barrier((panels, half_mine))
    first_half = multiply(0, meta, own_blocks, panels)
    mine, to_ahead, to_behind, to_far = cross(chunks_x, 4, first_half, slab, theirs)
    parts = (mine, send(to_ahead, ahead), send(to_behind, behind), send(to_far, opposite))
    own, *sent = sum_chunks(chunks_x, 4, half_mine, from_low)
    second = (own, send(sent[0], ahead), send(sent[1], behind), send(sent[2], opposite))
    parts, _ = lax.optimization_barrier((parts, sent))
    own, sent = sum_chunks(chunks_low, 2, *parts)
    first_shard = add(own, swap_low(sent))
    second_shard = add(*second)

    last = (x == X - 1) & (zl == ZL - 1)
    at = jnp.arange(SHARD, dtype=jnp.int32)[:, None] + (CROSS - SHARD)

    def weights_of(shard):
        own = jnp.where(last & (at == NOCC), shard, shard * (1.0 / NB)).astype(bf16)
        return jnp.where(last & (at == NOCC + 1), own[NOCC - (CROSS - SHARD)][None], swap_cores(own))

    def parts_x(array):
        return array, send(array, ahead), send(array, behind), send(array, opposite)

    def joined(parts, places):
        n = parts[0].shape[0]
        into = jnp.zeros((n * len(parts), WIDE), bf16)
        for part, k in zip(parts, places):
            into = lax.dynamic_update_slice(into, part, ((k % len(parts)) * n, 0))
        return into

    array = weights_of(first_shard)
    from_low = swap_low(array)
    by_x = joined((array, from_low), (zl, 1 - zl))
    by_low = joined(parts_x(weights_of(second_shard)), (x, x - sign, x + sign, x + 2))
    by_low, by_x = lax.optimization_barrier((by_low, by_x))
    keep, give = exchange((first_half, second_half), (by_low, swap_low(by_low)), parts_x(by_x))

    yy = ("y", "y")
    ahead, behind, opposite = around(yy, 1, True), around(yy, -1, True), around(yy, 2, True)
    own, *sent = sum_chunks(chunks_y, 4, keep, swap_cores(give))
    part = own + add(send(sent[0], ahead), send(sent[1], behind), send(sent[2], opposite))
    part = (part + swap_high(part)).astype(bf16)
    into = jnp.zeros((CROSS // 2, ROWS), bf16)
    for k, array in (
        (y, part),
        (y - sign, send(part, ahead)),
        (y + sign, send(part, behind)),
        (y + 2, send(part, opposite)),
    ):
        into = lax.dynamic_update_slice(into, array, ((k % Y) * SHARD, 0))
    return widen(into, swap_cores(into)).T


def solution(mesh):
    in_specs = (
        P("aux", "row", None, None),
        P("aux", "row"),
        P("aux", "row"),
        P("aux", "row"),
        P(("aux", "row"), None),
        P(("aux", "row"), None),
    )
    out_specs = P("row", None)
    return jax.shard_map(local, mesh=mesh, in_specs=in_specs, out_specs=out_specs, check_vma=False)
```

```python
import itertools

import jax
import jax.numpy as jnp
from jax import lax
from jax.experimental import pallas as pl
from jax.experimental.pallas import tpu as pltpu
from jax.sharding import PartitionSpec as P

Y, ZH, CORE, X, ZL = 4, 2, 2, 4, 2
AXES = ("aux", "row")
BLK = 128
ROW_BLOCKS = 6
ROWS = ROW_BLOCKS * BLK
SLOTS = 96
NB = 6144
NOCC = 800
WIDE = 896
CROSS = 832
SHARD = CROSS // 8
OWN = 48
STEP = 4
UNROLL = 3
FIELDS = 1 + 2 * STEP
MOST = SLOTS // STEP + ROW_BLOCKS + UNROLL
MAIN = 32
PARTS = 24
bf16, f32 = jnp.bfloat16, jnp.float32


def permutation(move):
    pairs = []
    for y, zh, c, x, zl in itertools.product(range(Y), range(ZH), range(CORE), range(X), range(ZL)):
        at = dict(y=y, z=zh * ZL + zl, c=c, x=x)
        to = move(dict(at))

        def flat(d):
            return (((d["y"] * ZH + d["z"] // ZL) * CORE + d["c"]) * X + d["x"]) * ZL + d["z"] % ZL

        pairs.append((flat(at), flat(to)))
    return pairs


def around(axes, by, mirror):
    def move(d):
        axis = axes[d["c"]]
        d[axis] = (d[axis] + (-by if mirror and d["c"] else by)) % 4
        return d

    return permutation(move)


def other_core(d):
    d["c"] = 1 - d["c"]
    return d


def other_low(d):
    d["z"] = d["z"] ^ 1
    return d


def other_high(d):
    d["z"] = d["z"] ^ 2
    return d


def send(array, pairs):
    return lax.ppermute(array, AXES, pairs)


def swap_cores(array):
    return send(array, permutation(other_core))


def swap_low(array):
    return send(array, permutation(other_low))


def swap_high(array):
    return send(array, permutation(other_high))


def here():
    aux, row = lax.axis_index("aux"), lax.axis_index("row")
    return aux % CORE, row, row // ZL, row % ZL


def place_parts(main0, main1, rest, at_two, at_z, held, sems):
    core = here()[0]
    copies = []
    for a in range(4):
        y, x = jnp.where(core == 0, at_two, a), jnp.where(core == 0, a, at_two)
        for c, main in enumerate((main0, main1)):
            copies.append((main.at[:, :, a], held.at[y, :, c, x, :, pl.ds(0, MAIN)]))
        for b in range(4):
            y, x = jnp.where(core == 0, b, a), jnp.where(core == 0, a, b)
            into = held.at[y, at_z // ZL, :, x, at_z % ZL, pl.ds(MAIN, OWN - MAIN)]
            copies.append((rest.at[:, a, b], into))
    return [pltpu.make_async_copy(*copy, sems.at[i]) for i, copy in enumerate(copies)]


def positions():
    aux = lax.axis_index("aux")
    core, _, x, zl = here()
    y, z = aux // (ZH * CORE), aux // CORE % ZH * ZL + zl
    return jnp.where(core == 0, y, x), z, 1 - 2 * core


def near_kernel(*refs):
    parts, held, sems = refs[:9], refs[9], refs[10]
    at_two, z, sign = positions()
    copies = []
    for k, (two, along) in enumerate(((0, 0), (3, 4 - sign), (1, 4 + sign))):
        where = ((at_two + two) % 4, (z + along) % 4)
        copies += place_parts(*parts[3 * k : 3 * k + 3], *where, held, sems.at[k])
    for copy in copies:
        copy.start()
    for copy in copies:
        copy.wait()


def far_kernel(main0, main1, rest, near, held, slab, sems):
    at_two, z, _ = positions()
    row = here()[1]
    copies = place_parts(main0, main1, rest, (at_two + 2) % 4, (z + 2) % 4, held, sems)
    for copy in copies:
        copy.start()
    for copy in copies:
        copy.wait()
    copy = pltpu.make_async_copy(held.at[row // ZL, row % ZL], slab, sems.at[PARTS])
    copy.start()
    copy.wait()


def panels_and_slab(near, far):
    anywhere = pl.BlockSpec(memory_space=pl.ANY)
    held = jax.ShapeDtypeStruct((Y, ZH, CORE, X, ZL, OWN, WIDE), bf16)
    panels = pl.pallas_call(
        near_kernel,
        out_shape=held,
        in_specs=[anywhere] * 9,
        out_specs=anywhere,
        scratch_shapes=[pltpu.SemaphoreType.DMA((3, PARTS))],
        compiler_params=pltpu.CompilerParams(vmem_limit_bytes=4 * 1024 * 1024),
        name="near",
    )(*near)
    return pl.pallas_call(
        far_kernel,
        out_shape=[held, jax.ShapeDtypeStruct((CORE, X, ZL, OWN, WIDE), bf16)],
        in_specs=[anywhere] * 4,
        out_specs=[anywhere] * 2,
        input_output_aliases={3: 0},
        scratch_shapes=[pltpu.SemaphoreType.DMA((PARTS + 1,))],
        compiler_params=pltpu.CompilerParams(vmem_limit_bytes=4 * 1024 * 1024),
        name="far",
    )(*far, panels)


def plan_kernel(meta, steps, order, counts):
    for q in range(2):

        def clear(i, carry):
            counts[i] = 0
            return carry

        lax.fori_loop(0, ROW_BLOCKS, clear, 0)

        def put(s, carry):
            group = meta[q, s]
            n = counts[group]
            order[group, n] = s
            counts[group] = n + 1
            return carry

        lax.fori_loop(0, meta[q, 2 * SLOTS], put, 0)

        def list_group(group, base):
            n = counts[group]
            for i in range(STEP):
                order[group, n + i] = SLOTS
            many = (n + STEP - 1) // STEP

            def list_step(i, carry):
                at = (base + i) * FIELDS
                steps[q, at] = group
                for k in range(STEP):
                    s = order[group, i * STEP + k]
                    steps[q, at + 1 + k] = s
                    steps[q, at + 1 + STEP + k] = jnp.where(s < SLOTS, meta[q, SLOTS + s], 0)
                return carry

            lax.fori_loop(0, many, list_step, 0)
            return base + many

        many = lax.fori_loop(0, ROW_BLOCKS, list_group, 0)
        for u in range(UNROLL - 1):
            at = (many + u) * FIELDS
            steps[q, at] = ROW_BLOCKS
            for k in range(STEP):
                steps[q, at + 1 + k] = SLOTS
                steps[q, at + 1 + STEP + k] = 0
        steps[q, MOST * FIELDS] = many


def plan(meta):
    smem = pl.BlockSpec(memory_space=pltpu.SMEM)
    return pl.pallas_call(
        plan_kernel,
        out_shape=jax.ShapeDtypeStruct((2, MOST * FIELDS + 1), jnp.int32),
        in_specs=[smem],
        out_specs=smem,
        scratch_shapes=[
            pltpu.SMEM((ROW_BLOCKS, SLOTS + 2 * STEP), jnp.int32),
            pltpu.SMEM((ROW_BLOCKS,), jnp.int32),
        ],
        compiler_params=pltpu.CompilerParams(vmem_limit_bytes=2**20),
        cost_estimate=pl.CostEstimate(flops=2**31, bytes_accessed=2**12, transcendentals=0),
        name="plan",
    )(meta)


def multiply_kernel(q, steps, factors, held, out, total):
    total[...] = jnp.zeros_like(total)
    many = steps[q, MOST * FIELDS]
    panels = held.reshape(NB, WIDE)

    def some(i, carry):
        products = []
        for u in range(UNROLL):
            left, right = [], []
            for k in range(STEP):
                slot = steps[q, (i * UNROLL + u) * FIELDS + 1 + k]
                block = factors[jnp.minimum(slot, SLOTS - 1)]
                left.append(jnp.where(slot < SLOTS, block, jnp.zeros_like(block)))
                column = steps[q, (i * UNROLL + u) * FIELDS + 1 + STEP + k]
                right.append(panels[pl.ds(pl.multiple_of(column * BLK, BLK), BLK), :])
            products.append(
                jnp.dot(jnp.concatenate(left, axis=1), jnp.concatenate(right, axis=0), preferred_element_type=f32)
            )
        for u in range(UNROLL):
            total[steps[q, (i * UNROLL + u) * FIELDS]] += products[u]
        return carry

    lax.fori_loop(0, (many + UNROLL - 1) // UNROLL, some, 0)
    for group in range(ROW_BLOCKS):
        out[group * BLK : (group + 1) * BLK, :] = total[group].astype(bf16)


def multiply(q, steps, factors, panels):
    vmem = pl.BlockSpec(memory_space=pltpu.VMEM)

    def kernel(*refs):
        multiply_kernel(q, *refs)

    return pl.pallas_call(
        kernel,
        out_shape=jax.ShapeDtypeStruct((ROWS, WIDE), bf16),
        in_specs=[pl.BlockSpec(memory_space=pltpu.SMEM), vmem, vmem],
        out_specs=vmem,
        scratch_shapes=[
            pltpu.VMEM((ROW_BLOCKS + 1, BLK, WIDE), f32),
        ],
        compiler_params=pltpu.CompilerParams(vmem_limit_bytes=24 * 1024 * 1024),
        cost_estimate=pl.CostEstimate(flops=96 * 2 * 128 * 128 * 896, bytes_accessed=2**23, transcendentals=0),
        name="multiply",
    )(steps, factors, panels)


def cross_kernel(starts, half, slab, theirs, *refs):
    outs, used, product = refs[:-2], refs[-2], refs[-1]
    core, row, _, _ = here()
    used[...] = jnp.where(core == 0, slab[...], theirs[...])
    product[...] = lax.dot_general(
        half[...], used[...], (((0,), (0,)), ((), ())), preferred_element_type=f32
    ).astype(bf16)
    value = jnp.sum(half[...].astype(f32) * theirs[...].astype(f32), keepdims=True)
    high = value.astype(bf16).astype(f32)
    middle = (value - high).astype(bf16).astype(f32)
    low = value - high - middle
    lane = lax.broadcasted_iota(jnp.int32, (16, WIDE), 1)
    line = lax.broadcasted_iota(jnp.int32, (16, WIDE), 0)
    coded = jnp.where(
        lane == 3 * row, high, jnp.where(lane == 3 * row + 1, middle, jnp.where(lane == 3 * row + 2, low, 0.0))
    )
    product[NOCC : NOCC + 16, :] = jnp.where(line == 0, coded, 0.0).astype(bf16)
    for out, start in zip(outs, starts()):
        n = out.shape[0]
        out[...] = product[pl.ds(pl.multiple_of(start * n, n), n), :]


def chunks_x():
    core, _, x, _ = here()
    return x, (x + 1 - 2 * core) % X, (x - 1 + 2 * core) % X, (x + 2) % X


def chunks_low():
    zl = here()[3]
    return zl, 1 - zl


def cross(starts, many, half, slab, theirs):
    def kernel(*refs):
        cross_kernel(starts, *refs)

    return pl.pallas_call(
        kernel,
        out_shape=[jax.ShapeDtypeStruct((CROSS // many, WIDE), bf16)] * many,
        in_specs=[pl.BlockSpec(memory_space=pltpu.VMEM)] * 3,
        out_specs=[pl.BlockSpec(memory_space=pltpu.VMEM)] * many,
        scratch_shapes=[pltpu.VMEM((ROWS, WIDE), bf16), pltpu.VMEM((WIDE, WIDE), bf16)],
        compiler_params=pltpu.CompilerParams(vmem_limit_bytes=30 * 1024 * 1024),
        cost_estimate=pl.CostEstimate(flops=2 * 768 * 896 * 896, bytes_accessed=2**23, transcendentals=0),
        name="cross",
    )(half, slab, theirs)


def sum_kernel(starts, many, *refs):
    arrays, outs, total = refs[:many], refs[many:-1], refs[-1]
    total[...] = sum(array[...].astype(f32) for array in arrays)
    for out, start in zip(outs, starts()):
        n = out.shape[0]
        out[...] = total[pl.ds(pl.multiple_of(start * n, n), n), :].astype(out.dtype)


def sum_chunks(starts, pieces, *arrays):
    n, width = arrays[0].shape
    own = jax.ShapeDtypeStruct((n // pieces, width), f32)
    sent = jax.ShapeDtypeStruct((n // pieces, width), bf16)

    def kernel(*refs):
        sum_kernel(starts, len(arrays), *refs)

    return pl.pallas_call(
        kernel,
        out_shape=[own] + [sent] * (pieces - 1),
        in_specs=[pl.BlockSpec(memory_space=pltpu.VMEM)] * len(arrays),
        out_specs=[pl.BlockSpec(memory_space=pltpu.VMEM)] * pieces,
        scratch_shapes=[pltpu.VMEM((n, width), f32)],
        compiler_params=pltpu.CompilerParams(vmem_limit_bytes=24 * 1024 * 1024),
        cost_estimate=pl.CostEstimate(flops=n * width, bytes_accessed=2**21, transcendentals=0),
        name="sum_chunks",
    )(*arrays)


def chunks_y():
    y, c = lax.axis_index("aux") // (ZH * CORE), here()[0]
    return y, (y + 1 - 2 * c) % Y, (y - 1 + 2 * c) % Y, (y + 2) % Y


def exchange_kernel(*refs):
    halves, parts, (keep, give, held, weights, turned, sems) = refs[:2], refs[2:8], refs[8:]
    core, _, _, _ = here()
    copies = [[pltpu.make_async_copy(halves[q], held.at[q], sems.at[6 + q])] for q in range(2)]
    for i, (q, at) in enumerate([(0, at) for at in chunks_low()] + [(1, at) for at in chunks_arrived()]):
        n = parts[i].shape[0]
        into = weights.at[q, pl.ds(pl.multiple_of(at * n, n), n), :]
        copies[q].append(pltpu.make_async_copy(parts[i], into, sems.at[i]))
    for copy in copies[0] + copies[1]:
        copy.start()
    exchanged = []
    for q in range(2):
        weights[q, CROSS:, :] = jnp.zeros((WIDE - CROSS, WIDE), bf16)
        for copy in copies[q]:
            copy.wait()
        exchanged.append(jnp.dot(held[q], weights[q], preferred_element_type=f32))
    line = lax.broadcasted_iota(jnp.int32, (16, WIDE), 0)
    total = None
    for q in range(2):
        codes = jnp.where(line == 0, weights[q, NOCC : NOCC + 16, :].astype(f32), 0.0)
        codes = codes + jnp.where(line == 1, weights[1 - q, NOCC : NOCC + 16, :].astype(f32), 0.0)
        coulomb = jnp.sum(codes, keepdims=True) * (1.0 / NB)
        factor = jnp.where(core == 0, 2.0 * coulomb, 0.0)
        term = factor * held[q].astype(f32) - exchanged[q]
        total = term if total is None else total + term
    turned[...] = total.T
    n = CROSS // 2
    keep[...] = turned[pl.ds(pl.multiple_of(core * n, n), n), :]
    give[...] = turned[pl.ds(pl.multiple_of((1 - core) * n, n), n), :]


def chunks_arrived():
    x, ahead, behind, far = chunks_x()
    return x, behind, ahead, far


def exchange(halves, low_parts, x_parts):
    return pl.pallas_call(
        exchange_kernel,
        out_shape=[jax.ShapeDtypeStruct((CROSS // 2, ROWS), f32)] * 2,
        in_specs=[pl.BlockSpec(memory_space=pl.ANY)] * 8,
        out_specs=[pl.BlockSpec(memory_space=pltpu.VMEM)] * 2,
        scratch_shapes=[
            pltpu.VMEM((2, ROWS, WIDE), bf16),
            pltpu.VMEM((2, WIDE, WIDE), bf16),
            pltpu.VMEM((WIDE, ROWS), f32),
            pltpu.SemaphoreType.DMA((8,)),
        ],
        compiler_params=pltpu.CompilerParams(vmem_limit_bytes=48 * 1024 * 1024),
        cost_estimate=pl.CostEstimate(flops=4 * 768 * 896 * 896, bytes_accessed=2**23, transcendentals=0),
        name="exchange",
    )(*halves, *low_parts, *x_parts)


def widen_kernel(own, others, out):
    core, n = here()[0], CROSS // 2
    out[:n, :] = jnp.where(core == 0, own[...], others[...]).astype(f32)
    out[n:, :] = jnp.where(core == 0, others[...], own[...])[: NOCC - n].astype(f32)


def widen(own, others):
    return pl.pallas_call(
        widen_kernel,
        out_shape=jax.ShapeDtypeStruct((NOCC, ROWS), f32),
        in_specs=[pl.BlockSpec(memory_space=pltpu.VMEM)] * 2,
        out_specs=pl.BlockSpec(memory_space=pltpu.VMEM),
        compiler_params=pltpu.CompilerParams(vmem_limit_bytes=16 * 1024 * 1024),
        name="widen",
    )(own, others)


def local(factors, block_rows, block_cols, block_count, orbitals, response):
    aux, row = lax.axis_index("aux"), lax.axis_index("row")
    y, zh, c = aux // (ZH * CORE), (aux // CORE) % ZH, aux % CORE
    x, zl = row // ZL, row % ZL
    z = zh * ZL + zl
    sign = 1 - 2 * c
    first = c == 0

    def choose(a, b):
        return jnp.where(first, a, b)

    def send_after(array, pairs, *earlier):
        return send(lax.optimization_barrier((array, *earlier))[0], pairs)

    def put(into, array, **at):
        index = [jnp.int32(0)] * into.ndim
        for dim, i in at.items():
            index[int(dim[1:])] = i
        return lax.dynamic_update_slice(into, array, index)

    got = send(choose(response, orbitals), permutation(other_core))
    own_blocks = factors[0]
    other_blocks = send_after(own_blocks, permutation(other_core), got)
    both = jnp.stack([choose(orbitals, got), choose(got, response)])
    both = jnp.pad(both, ((0, 0), (0, 0), (0, WIDE - NOCC)))

    one, two = ("x", "y"), ("y", "x")
    at_one, at_two = choose(x, y), choose(y, x)
    shape = (CORE, 4, OWN, WIDE)
    stage = put(jnp.zeros(shape, bf16), both[:, None], d1=at_one)
    ahead = send(both, around(one, 1, False))
    behind = send(both, around(one, -1, False))
    far = send(both, around(one, 2, False))
    stage = put(stage, ahead[:, None], d1=(at_one - 1) % 4)
    stage = put(stage, behind[:, None], d1=(at_one + 1) % 4)
    stage = put(stage, far[:, None], d1=(at_one + 2) % 4)
    stage, other_blocks = lax.optimization_barrier((stage, other_blocks))

    main, rest = stage[:, :, :MAIN], stage[:, :, MAIN:]
    zz = ("z", "z")
    main_ahead = send(main, around(zz, 1, True))
    main_far = send(main_ahead, around(zz, 1, True))
    main_behind = send_after(main, around(zz, -1, True), main_ahead)
    lists = lax.optimization_barrier((block_rows[0], block_cols[0], block_count[0], ahead))
    lists = jnp.concatenate([lists[0] % ROW_BLOCKS, lists[1], lists[2]])
    lists = jnp.pad(lists, (0, 256 - 2 * SLOTS - 1))[None]
    meta = jnp.concatenate([lists, send_after(lists, permutation(other_core), main_ahead)])
    rest, meta = lax.optimization_barrier((rest, meta))
    rest_ahead = send(rest, around(two, 1, False))
    rest_behind = send(rest, around(two, -1, False))
    rest_far = send(rest, around(two, 2, False))

    mains = [jnp.zeros((ZH, ZL, 4, MAIN, WIDE), bf16)] * 2
    for array, at in (
        (main, z),
        (main_ahead, (z - sign) % 4),
        (main_behind, (z + sign) % 4),
        (main_far, (z + 2) % 4),
    ):
        mains = [put(into, array[i][None, None], d0=at // ZL, d1=at % ZL) for i, into in enumerate(mains)]
    into = jnp.zeros((CORE, 4, 4, OWN - MAIN, WIDE), bf16)
    for array, at in (
        (rest, at_two),
        (rest_ahead, (at_two - 1) % 4),
        (rest_behind, (at_two + 1) % 4),
        (rest_far, (at_two + 2) % 4),
    ):
        into = put(into, array[:, :, None], d2=at)
    rest = into

    ahead, behind = around(two, 1, False), around(two, -1, False)
    mains, rest = lax.optimization_barrier((mains, rest))
    ahead_0 = send(mains[0], ahead)
    behind_1 = send(mains[1], behind)
    rest_ahead = send(rest, around(zz, 1, True))
    rest_behind = send(rest, around(zz, -1, True))
    steps = plan(meta)
    ahead_1 = send_after(mains[1], ahead, ahead_0, steps)
    behind_0 = send_after(mains[0], behind, behind_1, steps)
    far_0 = send(ahead_0, ahead)
    far_1 = send_after(behind_1, behind, rest_ahead)
    rest_far = send_after(rest_ahead, around(zz, 1, True), rest_behind)
    near = [mains[0], mains[1], rest, ahead_0, ahead_1, rest_ahead, behind_0, behind_1, rest_behind]
    panels, slab = panels_and_slab(near, (far_0, far_1, rest_far))
    slab = slab.reshape(ROWS, WIDE)
    theirs = swap_cores(slab)
    second_half = multiply(1, steps, other_blocks, panels)

    def add(*arrays):
        return sum(a.astype(f32) for a in arrays)

    xx = ("x", "x")
    ahead, behind = around(xx, 1, True), around(xx, -1, True)
    opposite = around(xx, 2, True)
    half_mine, to_low = cross(chunks_low, 2, second_half, slab, theirs)
    from_low = swap_low(to_low)
    panels, half_mine = lax.optimization_barrier((panels, half_mine))
    first_half = multiply(0, steps, own_blocks, panels)
    mine, to_ahead, to_behind, to_far = cross(chunks_x, 4, first_half, slab, theirs)
    parts = (mine, send(to_ahead, ahead), send(to_behind, behind), send(to_far, opposite))
    own, *sent = sum_chunks(chunks_x, 4, half_mine, from_low)
    second = (own, send(sent[0], ahead), send(sent[1], behind), send(sent[2], opposite))
    parts, _ = lax.optimization_barrier((parts, sent))
    own, sent = sum_chunks(chunks_low, 2, *parts)
    first_shard = add(own, swap_low(sent))
    second_shard = add(*second)

    last = (x == X - 1) & (zl == ZL - 1)
    at = jnp.arange(SHARD, dtype=jnp.int32)[:, None] + (CROSS - SHARD)

    def weights_of(shard):
        own = jnp.where(last & (at == NOCC), shard, shard * (1.0 / NB)).astype(bf16)
        return jnp.where(last & (at == NOCC + 1), own[NOCC - (CROSS - SHARD)][None], swap_cores(own))

    def parts_x(array):
        return array, send(array, ahead), send(array, behind), send(array, opposite)

    def joined(parts, places):
        n = parts[0].shape[0]
        into = jnp.zeros((n * len(parts), WIDE), bf16)
        for part, k in zip(parts, places):
            into = lax.dynamic_update_slice(into, part, ((k % len(parts)) * n, 0))
        return into

    array = weights_of(first_shard)
    from_low = swap_low(array)
    by_x = joined((array, from_low), (zl, 1 - zl))
    by_low = joined(parts_x(weights_of(second_shard)), (x, x - sign, x + sign, x + 2))
    by_low, by_x = lax.optimization_barrier((by_low, by_x))
    keep, give = exchange((first_half, second_half), (by_low, swap_low(by_low)), parts_x(by_x))

    yy = ("y", "y")
    ahead, behind, opposite = around(yy, 1, True), around(yy, -1, True), around(yy, 2, True)
    own, *sent = sum_chunks(chunks_y, 4, keep, swap_cores(give))
    part = own + add(send(sent[0], ahead), send(sent[1], behind), send(sent[2], opposite))
    part = (part + swap_high(part)).astype(bf16)
    into = jnp.zeros((CROSS // 2, ROWS), bf16)
    for k, array in (
        (y, part),
        (y - sign, send(part, ahead)),
        (y + sign, send(part, behind)),
        (y + 2, send(part, opposite)),
    ):
        into = lax.dynamic_update_slice(into, array, ((k % Y) * SHARD, 0))
    return widen(into, swap_cores(into)).T


def solution(mesh):
    in_specs = (
        P("aux", "row", None, None),
        P("aux", "row"),
        P("aux", "row"),
        P("aux", "row"),
        P(("aux", "row"), None),
        P(("aux", "row"), None),
    )
    out_specs = P("row", None)
    return jax.shard_map(local, mesh=mesh, in_specs=in_specs, out_specs=out_specs, check_vma=False)
```

```python
import itertools

import jax
import jax.numpy as jnp
from jax import lax
from jax.experimental import pallas as pl
from jax.experimental.pallas import tpu as pltpu
from jax.sharding import PartitionSpec as P

Y, ZH, CORE, X, ZL = 4, 2, 2, 4, 2
AXES = ("aux", "row")
BLK = 128
ROW_BLOCKS = 6
ROWS = ROW_BLOCKS * BLK
SLOTS = 96
NB = 6144
NOCC = 800
WIDE = 896
CROSS = 832
SHARD = CROSS // 8
OWN = 48
STEP = 4
UNROLL = 6
FIELDS = 1 + 2 * STEP
MOST = SLOTS // STEP + ROW_BLOCKS + UNROLL
MAIN = 32
PARTS = 24
bf16, f32 = jnp.bfloat16, jnp.float32


def permutation(move):
    pairs = []
    for y, zh, c, x, zl in itertools.product(range(Y), range(ZH), range(CORE), range(X), range(ZL)):
        at = dict(y=y, z=zh * ZL + zl, c=c, x=x)
        to = move(dict(at))

        def flat(d):
            return (((d["y"] * ZH + d["z"] // ZL) * CORE + d["c"]) * X + d["x"]) * ZL + d["z"] % ZL

        pairs.append((flat(at), flat(to)))
    return pairs


def around(axes, by, mirror):
    def move(d):
        axis = axes[d["c"]]
        d[axis] = (d[axis] + (-by if mirror and d["c"] else by)) % 4
        return d

    return permutation(move)


def other_core(d):
    d["c"] = 1 - d["c"]
    return d


def other_low(d):
    d["z"] = d["z"] ^ 1
    return d


def other_high(d):
    d["z"] = d["z"] ^ 2
    return d


def send(array, pairs):
    return lax.ppermute(array, AXES, pairs)


def swap_cores(array):
    return send(array, permutation(other_core))


def swap_low(array):
    return send(array, permutation(other_low))


def swap_high(array):
    return send(array, permutation(other_high))


def here():
    aux, row = lax.axis_index("aux"), lax.axis_index("row")
    return aux % CORE, row, row // ZL, row % ZL


def place_parts(main0, main1, rest, at_two, at_z, held, sems):
    core = here()[0]
    copies = []
    for a in range(4):
        y, x = jnp.where(core == 0, at_two, a), jnp.where(core == 0, a, at_two)
        for c, main in enumerate((main0, main1)):
            copies.append((main.at[:, :, a], held.at[y, :, c, x, :, pl.ds(0, MAIN)]))
        for b in range(4):
            y, x = jnp.where(core == 0, b, a), jnp.where(core == 0, a, b)
            into = held.at[y, at_z // ZL, :, x, at_z % ZL, pl.ds(MAIN, OWN - MAIN)]
            copies.append((rest.at[:, a, b], into))
    return [pltpu.make_async_copy(*copy, sems.at[i]) for i, copy in enumerate(copies)]


def positions():
    aux = lax.axis_index("aux")
    core, _, x, zl = here()
    y, z = aux // (ZH * CORE), aux // CORE % ZH * ZL + zl
    return jnp.where(core == 0, y, x), z, 1 - 2 * core


def near_kernel(*refs):
    parts, held, sems = refs[:9], refs[9], refs[10]
    at_two, z, sign = positions()
    copies = []
    for k, (two, along) in enumerate(((0, 0), (3, 4 - sign), (1, 4 + sign))):
        where = ((at_two + two) % 4, (z + along) % 4)
        copies += place_parts(*parts[3 * k : 3 * k + 3], *where, held, sems.at[k])
    for copy in copies:
        copy.start()
    for copy in copies:
        copy.wait()


def far_kernel(main0, main1, rest, near, held, slab, sems):
    at_two, z, _ = positions()
    row = here()[1]
    copies = place_parts(main0, main1, rest, (at_two + 2) % 4, (z + 2) % 4, held, sems)
    for copy in copies:
        copy.start()
    for copy in copies:
        copy.wait()
    copy = pltpu.make_async_copy(held.at[row // ZL, row % ZL], slab, sems.at[PARTS])
    copy.start()
    copy.wait()


def panels_and_slab(near, far):
    anywhere = pl.BlockSpec(memory_space=pl.ANY)
    held = jax.ShapeDtypeStruct((Y, ZH, CORE, X, ZL, OWN, WIDE), bf16)
    panels = pl.pallas_call(
        near_kernel,
        out_shape=held,
        in_specs=[anywhere] * 9,
        out_specs=anywhere,
        scratch_shapes=[pltpu.SemaphoreType.DMA((3, PARTS))],
        compiler_params=pltpu.CompilerParams(vmem_limit_bytes=4 * 1024 * 1024),
        name="near",
    )(*near)
    return pl.pallas_call(
        far_kernel,
        out_shape=[held, jax.ShapeDtypeStruct((CORE, X, ZL, OWN, WIDE), bf16)],
        in_specs=[anywhere] * 4,
        out_specs=[anywhere] * 2,
        input_output_aliases={3: 0},
        scratch_shapes=[pltpu.SemaphoreType.DMA((PARTS + 1,))],
        compiler_params=pltpu.CompilerParams(vmem_limit_bytes=4 * 1024 * 1024),
        name="far",
    )(*far, panels)


def plan_kernel(meta, steps, order, counts):
    for q in range(2):

        def clear(i, carry):
            counts[i] = 0
            return carry

        lax.fori_loop(0, ROW_BLOCKS, clear, 0)

        def put(s, carry):
            group = meta[q, s]
            n = counts[group]
            order[group, n] = s
            counts[group] = n + 1
            return carry

        lax.fori_loop(0, meta[q, 2 * SLOTS], put, 0)

        def list_group(group, base):
            n = counts[group]
            for i in range(STEP):
                order[group, n + i] = SLOTS
            many = (n + STEP - 1) // STEP

            def list_step(i, carry):
                at = (base + i) * FIELDS
                steps[q, at] = group
                for k in range(STEP):
                    s = order[group, i * STEP + k]
                    steps[q, at + 1 + k] = s
                    steps[q, at + 1 + STEP + k] = jnp.where(s < SLOTS, meta[q, SLOTS + s], 0)
                return carry

            lax.fori_loop(0, many, list_step, 0)
            return base + many

        many = lax.fori_loop(0, ROW_BLOCKS, list_group, 0)
        for u in range(UNROLL - 1):
            at = (many + u) * FIELDS
            steps[q, at] = ROW_BLOCKS
            for k in range(STEP):
                steps[q, at + 1 + k] = SLOTS
                steps[q, at + 1 + STEP + k] = 0
        steps[q, MOST * FIELDS] = many


def plan(meta):
    smem = pl.BlockSpec(memory_space=pltpu.SMEM)
    return pl.pallas_call(
        plan_kernel,
        out_shape=jax.ShapeDtypeStruct((2, MOST * FIELDS + 1), jnp.int32),
        in_specs=[smem],
        out_specs=smem,
        scratch_shapes=[
            pltpu.SMEM((ROW_BLOCKS, SLOTS + 2 * STEP), jnp.int32),
            pltpu.SMEM((ROW_BLOCKS,), jnp.int32),
        ],
        compiler_params=pltpu.CompilerParams(vmem_limit_bytes=2**20),
        cost_estimate=pl.CostEstimate(flops=2**31, bytes_accessed=2**12, transcendentals=0),
        name="plan",
    )(meta)


def multiply_kernel(q, steps, factors, held, out, total):
    total[...] = jnp.zeros_like(total)
    many = steps[q, MOST * FIELDS]
    panels = held.reshape(NB, WIDE)

    def some(i, carry):
        products = []
        for u in range(UNROLL):
            left, right = [], []
            for k in range(STEP):
                slot = steps[q, (i * UNROLL + u) * FIELDS + 1 + k]
                block = factors[jnp.minimum(slot, SLOTS - 1)]
                left.append(jnp.where(slot < SLOTS, block, jnp.zeros_like(block)))
                column = steps[q, (i * UNROLL + u) * FIELDS + 1 + STEP + k]
                right.append(panels[pl.ds(pl.multiple_of(column * BLK, BLK), BLK), :])
            products.append(
                jnp.dot(jnp.concatenate(left, axis=1), jnp.concatenate(right, axis=0), preferred_element_type=f32)
            )
        for u in range(UNROLL):
            total[steps[q, (i * UNROLL + u) * FIELDS]] += products[u]
        return carry

    lax.fori_loop(0, (many + UNROLL - 1) // UNROLL, some, 0)
    for group in range(ROW_BLOCKS):
        out[group * BLK : (group + 1) * BLK, :] = total[group].astype(bf16)


def multiply(q, steps, factors, panels):
    vmem = pl.BlockSpec(memory_space=pltpu.VMEM)

    def kernel(*refs):
        multiply_kernel(q, *refs)

    return pl.pallas_call(
        kernel,
        out_shape=jax.ShapeDtypeStruct((ROWS, WIDE), bf16),
        in_specs=[pl.BlockSpec(memory_space=pltpu.SMEM), vmem, vmem],
        out_specs=vmem,
        scratch_shapes=[
            pltpu.VMEM((ROW_BLOCKS + 1, BLK, WIDE), f32),
        ],
        compiler_params=pltpu.CompilerParams(vmem_limit_bytes=24 * 1024 * 1024),
        cost_estimate=pl.CostEstimate(flops=96 * 2 * 128 * 128 * 896, bytes_accessed=2**23, transcendentals=0),
        name="multiply",
    )(steps, factors, panels)


def cross_kernel(starts, half, slab, theirs, *refs):
    outs, used, product = refs[:-2], refs[-2], refs[-1]
    core, row, _, _ = here()
    used[...] = jnp.where(core == 0, slab[...], theirs[...])
    product[...] = lax.dot_general(
        half[...], used[...], (((0,), (0,)), ((), ())), preferred_element_type=f32
    ).astype(bf16)
    value = jnp.sum(half[...].astype(f32) * theirs[...].astype(f32), keepdims=True)
    high = value.astype(bf16).astype(f32)
    middle = (value - high).astype(bf16).astype(f32)
    low = value - high - middle
    lane = lax.broadcasted_iota(jnp.int32, (16, WIDE), 1)
    line = lax.broadcasted_iota(jnp.int32, (16, WIDE), 0)
    coded = jnp.where(
        lane == 3 * row, high, jnp.where(lane == 3 * row + 1, middle, jnp.where(lane == 3 * row + 2, low, 0.0))
    )
    product[NOCC : NOCC + 16, :] = jnp.where(line == 0, coded, 0.0).astype(bf16)
    for out, start in zip(outs, starts()):
        n = out.shape[0]
        out[...] = product[pl.ds(pl.multiple_of(start * n, n), n), :]


def chunks_x():
    core, _, x, _ = here()
    return x, (x + 1 - 2 * core) % X, (x - 1 + 2 * core) % X, (x + 2) % X


def chunks_low():
    zl = here()[3]
    return zl, 1 - zl


def cross(starts, many, half, slab, theirs):
    def kernel(*refs):
        cross_kernel(starts, *refs)

    return pl.pallas_call(
        kernel,
        out_shape=[jax.ShapeDtypeStruct((CROSS // many, WIDE), bf16)] * many,
        in_specs=[pl.BlockSpec(memory_space=pltpu.VMEM)] * 3,
        out_specs=[pl.BlockSpec(memory_space=pltpu.VMEM)] * many,
        scratch_shapes=[pltpu.VMEM((ROWS, WIDE), bf16), pltpu.VMEM((WIDE, WIDE), bf16)],
        compiler_params=pltpu.CompilerParams(vmem_limit_bytes=30 * 1024 * 1024),
        cost_estimate=pl.CostEstimate(flops=2 * 768 * 896 * 896, bytes_accessed=2**23, transcendentals=0),
        name="cross",
    )(half, slab, theirs)


def sum_kernel(starts, many, *refs):
    arrays, outs, total = refs[:many], refs[many:-1], refs[-1]
    total[...] = sum(array[...].astype(f32) for array in arrays)
    for out, start in zip(outs, starts()):
        n = out.shape[0]
        out[...] = total[pl.ds(pl.multiple_of(start * n, n), n), :].astype(out.dtype)


def sum_chunks(starts, pieces, *arrays):
    n, width = arrays[0].shape
    own = jax.ShapeDtypeStruct((n // pieces, width), f32)
    sent = jax.ShapeDtypeStruct((n // pieces, width), bf16)

    def kernel(*refs):
        sum_kernel(starts, len(arrays), *refs)

    return pl.pallas_call(
        kernel,
        out_shape=[own] + [sent] * (pieces - 1),
        in_specs=[pl.BlockSpec(memory_space=pltpu.VMEM)] * len(arrays),
        out_specs=[pl.BlockSpec(memory_space=pltpu.VMEM)] * pieces,
        scratch_shapes=[pltpu.VMEM((n, width), f32)],
        compiler_params=pltpu.CompilerParams(vmem_limit_bytes=24 * 1024 * 1024),
        cost_estimate=pl.CostEstimate(flops=n * width, bytes_accessed=2**21, transcendentals=0),
        name="sum_chunks",
    )(*arrays)


def chunks_y():
    y, c = lax.axis_index("aux") // (ZH * CORE), here()[0]
    return y, (y + 1 - 2 * c) % Y, (y - 1 + 2 * c) % Y, (y + 2) % Y


def exchange_kernel(*refs):
    halves, parts, (keep, give, held, weights, turned, sems) = refs[:2], refs[2:8], refs[8:]
    core, _, _, _ = here()
    copies = [[pltpu.make_async_copy(halves[q], held.at[q], sems.at[6 + q])] for q in range(2)]
    for i, (q, at) in enumerate([(0, at) for at in chunks_low()] + [(1, at) for at in chunks_arrived()]):
        n = parts[i].shape[0]
        into = weights.at[q, pl.ds(pl.multiple_of(at * n, n), n), :]
        copies[q].append(pltpu.make_async_copy(parts[i], into, sems.at[i]))
    for copy in copies[0] + copies[1]:
        copy.start()
    exchanged = []
    for q in range(2):
        weights[q, CROSS:, :] = jnp.zeros((WIDE - CROSS, WIDE), bf16)
        for copy in copies[q]:
            copy.wait()
        exchanged.append(jnp.dot(held[q], weights[q], preferred_element_type=f32))
    line = lax.broadcasted_iota(jnp.int32, (16, WIDE), 0)
    total = None
    for q in range(2):
        codes = jnp.where(line == 0, weights[q, NOCC : NOCC + 16, :].astype(f32), 0.0)
        codes = codes + jnp.where(line == 1, weights[1 - q, NOCC : NOCC + 16, :].astype(f32), 0.0)
        coulomb = jnp.sum(codes, keepdims=True) * (1.0 / NB)
        factor = jnp.where(core == 0, 2.0 * coulomb, 0.0)
        term = factor * held[q].astype(f32) - exchanged[q]
        total = term if total is None else total + term
    turned[...] = total.T
    n = CROSS // 2
    keep[...] = turned[pl.ds(pl.multiple_of(core * n, n), n), :]
    give[...] = turned[pl.ds(pl.multiple_of((1 - core) * n, n), n), :]


def chunks_arrived():
    x, ahead, behind, far = chunks_x()
    return x, behind, ahead, far


def exchange(halves, low_parts, x_parts):
    return pl.pallas_call(
        exchange_kernel,
        out_shape=[jax.ShapeDtypeStruct((CROSS // 2, ROWS), f32)] * 2,
        in_specs=[pl.BlockSpec(memory_space=pl.ANY)] * 8,
        out_specs=[pl.BlockSpec(memory_space=pltpu.VMEM)] * 2,
        scratch_shapes=[
            pltpu.VMEM((2, ROWS, WIDE), bf16),
            pltpu.VMEM((2, WIDE, WIDE), bf16),
            pltpu.VMEM((WIDE, ROWS), f32),
            pltpu.SemaphoreType.DMA((8,)),
        ],
        compiler_params=pltpu.CompilerParams(vmem_limit_bytes=48 * 1024 * 1024),
        cost_estimate=pl.CostEstimate(flops=4 * 768 * 896 * 896, bytes_accessed=2**23, transcendentals=0),
        name="exchange",
    )(*halves, *low_parts, *x_parts)


def widen_kernel(own, others, out):
    core, n = here()[0], CROSS // 2
    out[:n, :] = jnp.where(core == 0, own[...], others[...]).astype(f32)
    out[n:, :] = jnp.where(core == 0, others[...], own[...])[: NOCC - n].astype(f32)


def widen(own, others):
    part = ROWS // 3
    return pl.pallas_call(
        widen_kernel,
        grid=(3,),
        out_shape=jax.ShapeDtypeStruct((NOCC, ROWS), f32),
        in_specs=[pl.BlockSpec((CROSS // 2, part), lambda i: (0, i))] * 2,
        out_specs=pl.BlockSpec((NOCC, part), lambda i: (0, i)),
        compiler_params=pltpu.CompilerParams(vmem_limit_bytes=16 * 1024 * 1024),
        name="widen",
    )(own, others)


def local(factors, block_rows, block_cols, block_count, orbitals, response):
    aux, row = lax.axis_index("aux"), lax.axis_index("row")
    y, zh, c = aux // (ZH * CORE), (aux // CORE) % ZH, aux % CORE
    x, zl = row // ZL, row % ZL
    z = zh * ZL + zl
    sign = 1 - 2 * c
    first = c == 0

    def choose(a, b):
        return jnp.where(first, a, b)

    def send_after(array, pairs, *earlier):
        return send(lax.optimization_barrier((array, *earlier))[0], pairs)

    def put(into, array, **at):
        index = [jnp.int32(0)] * into.ndim
        for dim, i in at.items():
            index[int(dim[1:])] = i
        return lax.dynamic_update_slice(into, array, index)

    got = send(choose(response, orbitals), permutation(other_core))
    own_blocks = factors[0]
    other_blocks = send_after(own_blocks, permutation(other_core), got)
    both = jnp.stack([choose(orbitals, got), choose(got, response)])
    both = jnp.pad(both, ((0, 0), (0, 0), (0, WIDE - NOCC)))

    one, two = ("x", "y"), ("y", "x")
    at_one, at_two = choose(x, y), choose(y, x)
    shape = (CORE, 4, OWN, WIDE)
    stage = put(jnp.zeros(shape, bf16), both[:, None], d1=at_one)
    ahead = send(both, around(one, 1, False))
    behind = send(both, around(one, -1, False))
    far = send(both, around(one, 2, False))
    stage = put(stage, ahead[:, None], d1=(at_one - 1) % 4)
    stage = put(stage, behind[:, None], d1=(at_one + 1) % 4)
    stage = put(stage, far[:, None], d1=(at_one + 2) % 4)
    stage, other_blocks = lax.optimization_barrier((stage, other_blocks))

    main, rest = stage[:, :, :MAIN], stage[:, :, MAIN:]
    zz = ("z", "z")
    main_ahead = send(main, around(zz, 1, True))
    main_far = send(main_ahead, around(zz, 1, True))
    main_behind = send_after(main, around(zz, -1, True), main_ahead)
    lists = lax.optimization_barrier((block_rows[0], block_cols[0], block_count[0], ahead))
    lists = jnp.concatenate([lists[0] % ROW_BLOCKS, lists[1], lists[2]])
    lists = jnp.pad(lists, (0, 256 - 2 * SLOTS - 1))[None]
    meta = jnp.concatenate([lists, send_after(lists, permutation(other_core), main_ahead)])
    rest, meta = lax.optimization_barrier((rest, meta))
    rest_ahead = send(rest, around(two, 1, False))
    rest_behind = send(rest, around(two, -1, False))
    rest_far = send(rest, around(two, 2, False))

    mains = [jnp.zeros((ZH, ZL, 4, MAIN, WIDE), bf16)] * 2
    for array, at in (
        (main, z),
        (main_ahead, (z - sign) % 4),
        (main_behind, (z + sign) % 4),
        (main_far, (z + 2) % 4),
    ):
        mains = [put(into, array[i][None, None], d0=at // ZL, d1=at % ZL) for i, into in enumerate(mains)]
    into = jnp.zeros((CORE, 4, 4, OWN - MAIN, WIDE), bf16)
    for array, at in (
        (rest, at_two),
        (rest_ahead, (at_two - 1) % 4),
        (rest_behind, (at_two + 1) % 4),
        (rest_far, (at_two + 2) % 4),
    ):
        into = put(into, array[:, :, None], d2=at)
    rest = into

    ahead, behind = around(two, 1, False), around(two, -1, False)
    mains, rest = lax.optimization_barrier((mains, rest))
    ahead_0 = send(mains[0], ahead)
    behind_1 = send(mains[1], behind)
    rest_ahead = send(rest, around(zz, 1, True))
    rest_behind = send(rest, around(zz, -1, True))
    steps = plan(meta)
    ahead_1 = send_after(mains[1], ahead, ahead_0, steps)
    behind_0 = send_after(mains[0], behind, behind_1, steps)
    far_0 = send(ahead_0, ahead)
    far_1 = send_after(behind_1, behind, rest_ahead)
    rest_far = send_after(rest_ahead, around(zz, 1, True), rest_behind)
    near = [mains[0], mains[1], rest, ahead_0, ahead_1, rest_ahead, behind_0, behind_1, rest_behind]
    panels, slab = panels_and_slab(near, (far_0, far_1, rest_far))
    slab = slab.reshape(ROWS, WIDE)
    theirs = swap_cores(slab)
    second_half = multiply(1, steps, other_blocks, panels)

    def add(*arrays):
        return sum(a.astype(f32) for a in arrays)

    xx = ("x", "x")
    ahead, behind = around(xx, 1, True), around(xx, -1, True)
    opposite = around(xx, 2, True)
    half_mine, to_low = cross(chunks_low, 2, second_half, slab, theirs)
    from_low = swap_low(to_low)
    panels, half_mine = lax.optimization_barrier((panels, half_mine))
    first_half = multiply(0, steps, own_blocks, panels)
    mine, to_ahead, to_behind, to_far = cross(chunks_x, 4, first_half, slab, theirs)
    parts = (mine, send(to_ahead, ahead), send(to_behind, behind), send(to_far, opposite))
    own, *sent = sum_chunks(chunks_x, 4, half_mine, from_low)
    second = (own, send(sent[0], ahead), send(sent[1], behind), send(sent[2], opposite))
    parts, _ = lax.optimization_barrier((parts, sent))
    own, sent = sum_chunks(chunks_low, 2, *parts)
    first_shard = add(own, swap_low(sent))
    second_shard = add(*second)

    last = (x == X - 1) & (zl == ZL - 1)
    at = jnp.arange(SHARD, dtype=jnp.int32)[:, None] + (CROSS - SHARD)

    def weights_of(shard):
        own = jnp.where(last & (at == NOCC), shard, shard * (1.0 / NB)).astype(bf16)
        return jnp.where(last & (at == NOCC + 1), own[NOCC - (CROSS - SHARD)][None], swap_cores(own))

    def parts_x(array):
        return array, send(array, ahead), send(array, behind), send(array, opposite)

    def joined(parts, places):
        n = parts[0].shape[0]
        into = jnp.zeros((n * len(parts), WIDE), bf16)
        for part, k in zip(parts, places):
            into = lax.dynamic_update_slice(into, part, ((k % len(parts)) * n, 0))
        return into

    array = weights_of(first_shard)
    from_low = swap_low(array)
    by_x = joined((array, from_low), (zl, 1 - zl))
    by_low = joined(parts_x(weights_of(second_shard)), (x, x - sign, x + sign, x + 2))
    by_low, by_x = lax.optimization_barrier((by_low, by_x))
    keep, give = exchange((first_half, second_half), (by_low, swap_low(by_low)), parts_x(by_x))

    yy = ("y", "y")
    ahead, behind, opposite = around(yy, 1, True), around(yy, -1, True), around(yy, 2, True)
    own, *sent = sum_chunks(chunks_y, 4, keep, swap_cores(give))
    part = own + add(send(sent[0], ahead), send(sent[1], behind), send(sent[2], opposite))
    part = (part + swap_high(part)).astype(bf16)
    into = jnp.zeros((CROSS // 2, ROWS), bf16)
    for k, array in (
        (y, part),
        (y - sign, send(part, ahead)),
        (y + sign, send(part, behind)),
        (y + 2, send(part, opposite)),
    ):
        into = lax.dynamic_update_slice(into, array, ((k % Y) * SHARD, 0))
    return widen(into, swap_cores(into)).T


def solution(mesh):
    in_specs = (
        P("aux", "row", None, None),
        P("aux", "row"),
        P("aux", "row"),
        P("aux", "row"),
        P(("aux", "row"), None),
        P(("aux", "row"), None),
    )
    out_specs = P("row", None)
    return jax.shard_map(local, mesh=mesh, in_specs=in_specs, out_specs=out_specs, check_vma=False)
```

```python
import itertools

import jax
import jax.numpy as jnp
from jax import lax
from jax.experimental import pallas as pl
from jax.experimental.pallas import tpu as pltpu
from jax.sharding import PartitionSpec as P

Y, ZH, CORE, X, ZL = 4, 2, 2, 4, 2
AXES = ("aux", "row")
BLK = 128
ROW_BLOCKS = 6
ROWS = ROW_BLOCKS * BLK
SLOTS = 96
NB = 6144
NOCC = 800
WIDE = 896
CROSS = 832
SHARD = CROSS // 8
OWN = 48
STEP = 4
UNROLL = 6
FIELDS = 1 + 2 * STEP
MOST = SLOTS // STEP + ROW_BLOCKS + UNROLL
MAIN = 32
PARTS = 24
bf16, f32 = jnp.bfloat16, jnp.float32


def permutation(move):
    pairs = []
    for y, zh, c, x, zl in itertools.product(range(Y), range(ZH), range(CORE), range(X), range(ZL)):
        at = dict(y=y, z=zh * ZL + zl, c=c, x=x)
        to = move(dict(at))

        def flat(d):
            return (((d["y"] * ZH + d["z"] // ZL) * CORE + d["c"]) * X + d["x"]) * ZL + d["z"] % ZL

        pairs.append((flat(at), flat(to)))
    return pairs


def around(axes, by, mirror):
    def move(d):
        axis = axes[d["c"]]
        d[axis] = (d[axis] + (-by if mirror and d["c"] else by)) % 4
        return d

    return permutation(move)


def other_core(d):
    d["c"] = 1 - d["c"]
    return d


def other_low(d):
    d["z"] = d["z"] ^ 1
    return d


def other_high(d):
    d["z"] = d["z"] ^ 2
    return d


def send(array, pairs):
    return lax.ppermute(array, AXES, pairs)


def swap_cores(array):
    return send(array, permutation(other_core))


def swap_low(array):
    return send(array, permutation(other_low))


def swap_high(array):
    return send(array, permutation(other_high))


def here():
    aux, row = lax.axis_index("aux"), lax.axis_index("row")
    return aux % CORE, row, row // ZL, row % ZL


def place_parts(main0, main1, rest, at_two, at_z, held, sems):
    core = here()[0]
    copies = []
    for a in range(4):
        y, x = jnp.where(core == 0, at_two, a), jnp.where(core == 0, a, at_two)
        for c, main in enumerate((main0, main1)):
            copies.append((main.at[:, :, a], held.at[y, :, c, x, :, pl.ds(0, MAIN)]))
        for b in range(4):
            y, x = jnp.where(core == 0, b, a), jnp.where(core == 0, a, b)
            into = held.at[y, at_z // ZL, :, x, at_z % ZL, pl.ds(MAIN, OWN - MAIN)]
            copies.append((rest.at[:, a, b], into))
    return [pltpu.make_async_copy(*copy, sems.at[i]) for i, copy in enumerate(copies)]


def positions():
    aux = lax.axis_index("aux")
    core, _, x, zl = here()
    y, z = aux // (ZH * CORE), aux // CORE % ZH * ZL + zl
    return jnp.where(core == 0, y, x), z, 1 - 2 * core


def near_kernel(*refs):
    parts, held, sems = refs[:9], refs[9], refs[10]
    at_two, z, sign = positions()
    copies = []
    for k, (two, along) in enumerate(((0, 0), (3, 4 - sign), (1, 4 + sign))):
        where = ((at_two + two) % 4, (z + along) % 4)
        copies += place_parts(*parts[3 * k : 3 * k + 3], *where, held, sems.at[k])
    for copy in copies:
        copy.start()
    for copy in copies:
        copy.wait()


def far_kernel(main0, main1, rest, near, held, slab, sems):
    at_two, z, _ = positions()
    row = here()[1]
    copies = place_parts(main0, main1, rest, (at_two + 2) % 4, (z + 2) % 4, held, sems)
    for copy in copies:
        copy.start()
    for copy in copies:
        copy.wait()
    copy = pltpu.make_async_copy(held.at[row // ZL, row % ZL], slab, sems.at[PARTS])
    copy.start()
    copy.wait()


def panels_and_slab(near, far):
    anywhere = pl.BlockSpec(memory_space=pl.ANY)
    held = jax.ShapeDtypeStruct((Y, ZH, CORE, X, ZL, OWN, WIDE), bf16)
    panels = pl.pallas_call(
        near_kernel,
        out_shape=held,
        in_specs=[anywhere] * 9,
        out_specs=anywhere,
        scratch_shapes=[pltpu.SemaphoreType.DMA((3, PARTS))],
        compiler_params=pltpu.CompilerParams(vmem_limit_bytes=4 * 1024 * 1024),
        name="near",
    )(*near)
    return pl.pallas_call(
        far_kernel,
        out_shape=[held, jax.ShapeDtypeStruct((CORE, X, ZL, OWN, WIDE), bf16)],
        in_specs=[anywhere] * 4,
        out_specs=[anywhere] * 2,
        input_output_aliases={3: 0},
        scratch_shapes=[pltpu.SemaphoreType.DMA((PARTS + 1,))],
        compiler_params=pltpu.CompilerParams(vmem_limit_bytes=4 * 1024 * 1024),
        name="far",
    )(*far, panels)


def plan_kernel(meta, steps, order, counts):
    for q in range(2):

        def clear(i, carry):
            counts[i] = 0
            return carry

        lax.fori_loop(0, ROW_BLOCKS, clear, 0)

        def put(s, carry):
            group = meta[q, s]
            n = counts[group]
            order[group, n] = s
            counts[group] = n + 1
            return carry

        lax.fori_loop(0, meta[q, 2 * SLOTS], put, 0)

        def list_group(group, base):
            n = counts[group]
            for i in range(STEP):
                order[group, n + i] = SLOTS
            many = (n + STEP - 1) // STEP

            def list_step(i, carry):
                at = (base + i) * FIELDS
                steps[q, at] = group
                for k in range(STEP):
                    s = order[group, i * STEP + k]
                    steps[q, at + 1 + k] = s
                    steps[q, at + 1 + STEP + k] = jnp.where(s < SLOTS, meta[q, SLOTS + s], 0)
                return carry

            lax.fori_loop(0, many, list_step, 0)
            return base + many

        many = lax.fori_loop(0, ROW_BLOCKS, list_group, 0)
        for u in range(UNROLL - 1):
            at = (many + u) * FIELDS
            steps[q, at] = ROW_BLOCKS
            for k in range(STEP):
                steps[q, at + 1 + k] = SLOTS
                steps[q, at + 1 + STEP + k] = 0
        steps[q, MOST * FIELDS] = many


def plan(meta):
    smem = pl.BlockSpec(memory_space=pltpu.SMEM)
    return pl.pallas_call(
        plan_kernel,
        out_shape=jax.ShapeDtypeStruct((2, MOST * FIELDS + 1), jnp.int32),
        in_specs=[smem],
        out_specs=smem,
        scratch_shapes=[
            pltpu.SMEM((ROW_BLOCKS, SLOTS + 2 * STEP), jnp.int32),
            pltpu.SMEM((ROW_BLOCKS,), jnp.int32),
        ],
        compiler_params=pltpu.CompilerParams(vmem_limit_bytes=2**20),
        cost_estimate=pl.CostEstimate(flops=2**31, bytes_accessed=2**12, transcendentals=0),
        name="plan",
    )(meta)


def multiply_kernel(q, steps, factors, held, out, total):
    total[...] = jnp.zeros_like(total)
    many = steps[q, MOST * FIELDS]
    panels = held.reshape(NB, WIDE)

    def some(i, carry):
        products = []
        for u in range(UNROLL):
            left, right = [], []
            for k in range(STEP):
                slot = steps[q, (i * UNROLL + u) * FIELDS + 1 + k]
                block = factors[jnp.minimum(slot, SLOTS - 1)]
                left.append(jnp.where(slot < SLOTS, block, jnp.zeros_like(block)))
                column = steps[q, (i * UNROLL + u) * FIELDS + 1 + STEP + k]
                right.append(panels[pl.ds(pl.multiple_of(column * BLK, BLK), BLK), :])
            products.append(
                jnp.dot(jnp.concatenate(left, axis=1), jnp.concatenate(right, axis=0), preferred_element_type=f32)
            )
        for u in range(UNROLL):
            total[steps[q, (i * UNROLL + u) * FIELDS]] += products[u]
        return carry

    lax.fori_loop(0, (many + UNROLL - 1) // UNROLL, some, 0)
    for group in range(ROW_BLOCKS):
        out[group * BLK : (group + 1) * BLK, :] = total[group].astype(bf16)


def multiply(q, steps, factors, panels):
    vmem = pl.BlockSpec(memory_space=pltpu.VMEM)

    def kernel(*refs):
        multiply_kernel(q, *refs)

    return pl.pallas_call(
        kernel,
        out_shape=jax.ShapeDtypeStruct((ROWS, WIDE), bf16),
        in_specs=[pl.BlockSpec(memory_space=pltpu.SMEM), vmem, vmem],
        out_specs=vmem,
        scratch_shapes=[
            pltpu.VMEM((ROW_BLOCKS + 1, BLK, WIDE), f32),
        ],
        compiler_params=pltpu.CompilerParams(vmem_limit_bytes=24 * 1024 * 1024),
        cost_estimate=pl.CostEstimate(flops=96 * 2 * 128 * 128 * 896, bytes_accessed=2**23, transcendentals=0),
        name="multiply",
    )(steps, factors, panels)


def cross_kernel(starts, half, slab, theirs, *refs):
    outs, used, product = refs[:-2], refs[-2], refs[-1]
    core, row, _, _ = here()
    used[...] = jnp.where(core == 0, slab[...], theirs[...])
    product[...] = lax.dot_general(
        half[...], used[...], (((0,), (0,)), ((), ())), preferred_element_type=f32
    ).astype(bf16)
    value = jnp.sum(half[...].astype(f32) * theirs[...].astype(f32), keepdims=True)
    high = value.astype(bf16).astype(f32)
    middle = (value - high).astype(bf16).astype(f32)
    low = value - high - middle
    lane = lax.broadcasted_iota(jnp.int32, (16, WIDE), 1)
    line = lax.broadcasted_iota(jnp.int32, (16, WIDE), 0)
    coded = jnp.where(
        lane == 3 * row, high, jnp.where(lane == 3 * row + 1, middle, jnp.where(lane == 3 * row + 2, low, 0.0))
    )
    product[NOCC : NOCC + 16, :] = jnp.where(line == 0, coded, 0.0).astype(bf16)
    for out, start in zip(outs, starts()):
        n = out.shape[0]
        out[...] = product[pl.ds(pl.multiple_of(start * n, n), n), :]


def chunks_x():
    core, _, x, _ = here()
    return x, (x + 1 - 2 * core) % X, (x - 1 + 2 * core) % X, (x + 2) % X


def chunks_low():
    zl = here()[3]
    return zl, 1 - zl


def cross(starts, many, half, slab, theirs):
    def kernel(*refs):
        cross_kernel(starts, *refs)

    return pl.pallas_call(
        kernel,
        out_shape=[jax.ShapeDtypeStruct((CROSS // many, WIDE), bf16)] * many,
        in_specs=[pl.BlockSpec(memory_space=pltpu.VMEM)] * 3,
        out_specs=[pl.BlockSpec(memory_space=pltpu.VMEM)] * many,
        scratch_shapes=[pltpu.VMEM((ROWS, WIDE), bf16), pltpu.VMEM((WIDE, WIDE), bf16)],
        compiler_params=pltpu.CompilerParams(vmem_limit_bytes=30 * 1024 * 1024),
        cost_estimate=pl.CostEstimate(flops=2 * 768 * 896 * 896, bytes_accessed=2**23, transcendentals=0),
        name="cross",
    )(half, slab, theirs)


def sum_kernel(starts, many, *refs):
    arrays, outs, total = refs[:many], refs[many:-1], refs[-1]
    total[...] = sum(array[...].astype(f32) for array in arrays)
    for out, start in zip(outs, starts()):
        n = out.shape[0]
        out[...] = total[pl.ds(pl.multiple_of(start * n, n), n), :].astype(out.dtype)


def sum_chunks(starts, pieces, *arrays):
    n, width = arrays[0].shape
    own = jax.ShapeDtypeStruct((n // pieces, width), f32)
    sent = jax.ShapeDtypeStruct((n // pieces, width), bf16)

    def kernel(*refs):
        sum_kernel(starts, len(arrays), *refs)

    return pl.pallas_call(
        kernel,
        out_shape=[own] + [sent] * (pieces - 1),
        in_specs=[pl.BlockSpec(memory_space=pltpu.VMEM)] * len(arrays),
        out_specs=[pl.BlockSpec(memory_space=pltpu.VMEM)] * pieces,
        scratch_shapes=[pltpu.VMEM((n, width), f32)],
        compiler_params=pltpu.CompilerParams(vmem_limit_bytes=24 * 1024 * 1024),
        cost_estimate=pl.CostEstimate(flops=n * width, bytes_accessed=2**21, transcendentals=0),
        name="sum_chunks",
    )(*arrays)


def chunks_y():
    y, c = lax.axis_index("aux") // (ZH * CORE), here()[0]
    return y, (y + 1 - 2 * c) % Y, (y - 1 + 2 * c) % Y, (y + 2) % Y


def exchange_kernel(*refs):
    halves, parts, (keep, give, held, weights, turned, sems) = refs[:2], refs[2:8], refs[8:]
    core, _, _, _ = here()
    copies = [[pltpu.make_async_copy(halves[q], held.at[q], sems.at[6 + q])] for q in range(2)]
    for i, (q, at) in enumerate([(0, at) for at in chunks_low()] + [(1, at) for at in chunks_arrived()]):
        n = parts[i].shape[0]
        into = weights.at[q, pl.ds(pl.multiple_of(at * n, n), n), :]
        copies[q].append(pltpu.make_async_copy(parts[i], into, sems.at[i]))
    for copy in copies[0] + copies[1]:
        copy.start()
    exchanged = []
    for q in range(2):
        weights[q, CROSS:, :] = jnp.zeros((WIDE - CROSS, WIDE), bf16)
        for copy in copies[q]:
            copy.wait()
        exchanged.append(jnp.dot(held[q], weights[q], preferred_element_type=f32))
    line = lax.broadcasted_iota(jnp.int32, (16, WIDE), 0)
    total = None
    for q in range(2):
        codes = jnp.where(line == 0, weights[q, NOCC : NOCC + 16, :].astype(f32), 0.0)
        codes = codes + jnp.where(line == 1, weights[1 - q, NOCC : NOCC + 16, :].astype(f32), 0.0)
        coulomb = jnp.sum(codes, keepdims=True) * (1.0 / NB)
        factor = jnp.where(core == 0, 2.0 * coulomb, 0.0)
        term = factor * held[q].astype(f32) - exchanged[q]
        total = term if total is None else total + term
    turned[...] = total.T
    n = CROSS // 2
    keep[...] = turned[pl.ds(pl.multiple_of(core * n, n), n), :]
    give[...] = turned[pl.ds(pl.multiple_of((1 - core) * n, n), n), :]


def chunks_arrived():
    x, ahead, behind, far = chunks_x()
    return x, behind, ahead, far


def exchange(halves, low_parts, x_parts):
    return pl.pallas_call(
        exchange_kernel,
        out_shape=[jax.ShapeDtypeStruct((CROSS // 2, ROWS), f32)] * 2,
        in_specs=[pl.BlockSpec(memory_space=pl.ANY)] * 8,
        out_specs=[pl.BlockSpec(memory_space=pltpu.VMEM)] * 2,
        scratch_shapes=[
            pltpu.VMEM((2, ROWS, WIDE), bf16),
            pltpu.VMEM((2, WIDE, WIDE), bf16),
            pltpu.VMEM((WIDE, ROWS), f32),
            pltpu.SemaphoreType.DMA((8,)),
        ],
        compiler_params=pltpu.CompilerParams(vmem_limit_bytes=48 * 1024 * 1024),
        cost_estimate=pl.CostEstimate(flops=4 * 768 * 896 * 896, bytes_accessed=2**23, transcendentals=0),
        name="exchange",
    )(*halves, *low_parts, *x_parts)


def widen_kernel(own, others, out):
    core, n = here()[0], CROSS // 2
    out[:n, :] = jnp.where(core == 0, own[...], others[...]).astype(f32)
    out[n:, :] = jnp.where(core == 0, others[...], own[...])[: NOCC - n].astype(f32)


def widen(own, others):
    return pl.pallas_call(
        widen_kernel,
        out_shape=jax.ShapeDtypeStruct((NOCC, ROWS), f32),
        in_specs=[pl.BlockSpec(memory_space=pltpu.VMEM)] * 2,
        out_specs=pl.BlockSpec(memory_space=pltpu.VMEM),
        compiler_params=pltpu.CompilerParams(vmem_limit_bytes=16 * 1024 * 1024),
        name="widen",
    )(own, others)


def local(factors, block_rows, block_cols, block_count, orbitals, response):
    aux, row = lax.axis_index("aux"), lax.axis_index("row")
    y, zh, c = aux // (ZH * CORE), (aux // CORE) % ZH, aux % CORE
    x, zl = row // ZL, row % ZL
    z = zh * ZL + zl
    sign = 1 - 2 * c
    first = c == 0

    def choose(a, b):
        return jnp.where(first, a, b)

    def send_after(array, pairs, *earlier):
        return send(lax.optimization_barrier((array, *earlier))[0], pairs)

    def put(into, array, **at):
        index = [jnp.int32(0)] * into.ndim
        for dim, i in at.items():
            index[int(dim[1:])] = i
        return lax.dynamic_update_slice(into, array, index)

    got = send(choose(response, orbitals), permutation(other_core))
    own_blocks = factors[0]
    other_blocks = send_after(own_blocks, permutation(other_core), got)
    both = jnp.stack([choose(orbitals, got), choose(got, response)])
    both = jnp.pad(both, ((0, 0), (0, 0), (0, WIDE - NOCC)))

    one, two = ("x", "y"), ("y", "x")
    at_one, at_two = choose(x, y), choose(y, x)
    shape = (CORE, 4, OWN, WIDE)
    stage = put(jnp.zeros(shape, bf16), both[:, None], d1=at_one)
    ahead = send(both, around(one, 1, False))
    behind = send(both, around(one, -1, False))
    far = send(both, around(one, 2, False))
    stage = put(stage, ahead[:, None], d1=(at_one - 1) % 4)
    stage = put(stage, behind[:, None], d1=(at_one + 1) % 4)
    stage = put(stage, far[:, None], d1=(at_one + 2) % 4)
    stage, other_blocks = lax.optimization_barrier((stage, other_blocks))

    main, rest = stage[:, :, :MAIN], stage[:, :, MAIN:]
    zz = ("z", "z")
    main_ahead = send(main, around(zz, 1, True))
    main_far = send(main_ahead, around(zz, 1, True))
    main_behind = send_after(main, around(zz, -1, True), main_ahead)
    lists = lax.optimization_barrier((block_rows[0], block_cols[0], block_count[0], ahead))
    lists = jnp.concatenate([lists[0] % ROW_BLOCKS, lists[1], lists[2]])
    lists = jnp.pad(lists, (0, 256 - 2 * SLOTS - 1))[None]
    meta = jnp.concatenate([lists, send_after(lists, permutation(other_core), main_ahead)])
    rest, meta = lax.optimization_barrier((rest, meta))
    rest_ahead = send(rest, around(two, 1, False))
    rest_behind = send(rest, around(two, -1, False))
    rest_far = send(rest, around(two, 2, False))

    mains = [jnp.zeros((ZH, ZL, 4, MAIN, WIDE), bf16)] * 2
    for array, at in (
        (main, z),
        (main_ahead, (z - sign) % 4),
        (main_behind, (z + sign) % 4),
        (main_far, (z + 2) % 4),
    ):
        mains = [put(into, array[i][None, None], d0=at // ZL, d1=at % ZL) for i, into in enumerate(mains)]
    into = jnp.zeros((CORE, 4, 4, OWN - MAIN, WIDE), bf16)
    for array, at in (
        (rest, at_two),
        (rest_ahead, (at_two - 1) % 4),
        (rest_behind, (at_two + 1) % 4),
        (rest_far, (at_two + 2) % 4),
    ):
        into = put(into, array[:, :, None], d2=at)
    rest = into

    ahead, behind = around(two, 1, False), around(two, -1, False)
    mains, rest = lax.optimization_barrier((mains, rest))
    ahead_0 = send(mains[0], ahead)
    behind_1 = send(mains[1], behind)
    rest_ahead = send(rest, around(zz, 1, True))
    rest_behind = send(rest, around(zz, -1, True))
    steps = plan(meta)
    ahead_1 = send_after(mains[1], ahead, ahead_0, steps)
    behind_0 = send_after(mains[0], behind, behind_1, steps)
    far_0 = send(ahead_0, ahead)
    far_1 = send_after(behind_1, behind, rest_ahead)
    rest_far = send_after(rest_ahead, around(zz, 1, True), rest_behind)
    near = [mains[0], mains[1], rest, ahead_0, ahead_1, rest_ahead, behind_0, behind_1, rest_behind]
    panels, slab = panels_and_slab(near, (far_0, far_1, rest_far))
    slab = slab.reshape(ROWS, WIDE)
    theirs = swap_cores(slab)
    second_half = multiply(1, steps, other_blocks, panels)

    def add(*arrays):
        return sum(a.astype(f32) for a in arrays)

    xx = ("x", "x")
    ahead, behind = around(xx, 1, True), around(xx, -1, True)
    opposite = around(xx, 2, True)
    half_mine, to_low = cross(chunks_low, 2, second_half, slab, theirs)
    from_low = swap_low(to_low)
    panels, half_mine = lax.optimization_barrier((panels, half_mine))
    first_half = multiply(0, steps, own_blocks, panels)
    mine, to_ahead, to_behind, to_far = cross(chunks_x, 4, first_half, slab, theirs)
    parts = (mine, send(to_ahead, ahead), send(to_behind, behind), send(to_far, opposite))
    own, *sent = sum_chunks(chunks_x, 4, half_mine, from_low)
    second = (own, send(sent[0], ahead), send(sent[1], behind), send(sent[2], opposite))
    parts, _ = lax.optimization_barrier((parts, second[1]))
    own, sent = sum_chunks(chunks_low, 2, *parts)
    first_shard = add(own, swap_low(sent))
    second_shard = add(*second)

    last = (x == X - 1) & (zl == ZL - 1)
    at = jnp.arange(SHARD, dtype=jnp.int32)[:, None] + (CROSS - SHARD)

    def weights_of(shard):
        own = jnp.where(last & (at == NOCC), shard, shard * (1.0 / NB)).astype(bf16)
        return jnp.where(last & (at == NOCC + 1), own[NOCC - (CROSS - SHARD)][None], swap_cores(own))

    def parts_x(array):
        return array, send(array, ahead), send(array, behind), send(array, opposite)

    def joined(parts, places):
        n = parts[0].shape[0]
        into = jnp.zeros((n * len(parts), WIDE), bf16)
        for part, k in zip(parts, places):
            into = lax.dynamic_update_slice(into, part, ((k % len(parts)) * n, 0))
        return into

    array = weights_of(first_shard)
    from_low = swap_low(array)
    by_x = joined((array, from_low), (zl, 1 - zl))
    by_low = joined(parts_x(weights_of(second_shard)), (x, x - sign, x + sign, x + 2))
    by_low, by_x = lax.optimization_barrier((by_low, by_x))
    keep, give = exchange((first_half, second_half), (by_low, swap_low(by_low)), parts_x(by_x))

    yy = ("y", "y")
    ahead, behind, opposite = around(yy, 1, True), around(yy, -1, True), around(yy, 2, True)
    own, *sent = sum_chunks(chunks_y, 4, keep, swap_cores(give))
    part = own + add(send(sent[0], ahead), send(sent[1], behind), send(sent[2], opposite))
    part = (part + swap_high(part)).astype(bf16)
    into = jnp.zeros((CROSS // 2, ROWS), bf16)
    for k, array in (
        (y, part),
        (y - sign, send(part, ahead)),
        (y + sign, send(part, behind)),
        (y + 2, send(part, opposite)),
    ):
        into = lax.dynamic_update_slice(into, array, ((k % Y) * SHARD, 0))
    return widen(into, swap_cores(into)).T


def solution(mesh):
    in_specs = (
        P("aux", "row", None, None),
        P("aux", "row"),
        P("aux", "row"),
        P("aux", "row"),
        P(("aux", "row"), None),
        P(("aux", "row"), None),
    )
    out_specs = P("row", None)
    return jax.shard_map(local, mesh=mesh, in_specs=in_specs, out_specs=out_specs, check_vma=False)
```

```python
import itertools

import jax
import jax.numpy as jnp
from jax import lax
from jax.experimental import pallas as pl
from jax.experimental.pallas import tpu as pltpu
from jax.sharding import PartitionSpec as P

Y, ZH, CORE, X, ZL = 4, 2, 2, 4, 2
AXES = ("aux", "row")
BLK = 128
ROW_BLOCKS = 6
ROWS = ROW_BLOCKS * BLK
SLOTS = 96
NB = 6144
NOCC = 800
WIDE = 896
CROSS = 832
SHARD = CROSS // 8
OWN = 48
STEP = 4
UNROLL = 6
FIELDS = 1 + 2 * STEP
MOST = SLOTS // STEP + ROW_BLOCKS + UNROLL
MAIN = 32
PARTS = 24
bf16, f32 = jnp.bfloat16, jnp.float32


def permutation(move):
    pairs = []
    for y, zh, c, x, zl in itertools.product(range(Y), range(ZH), range(CORE), range(X), range(ZL)):
        at = dict(y=y, z=zh * ZL + zl, c=c, x=x)
        to = move(dict(at))

        def flat(d):
            return (((d["y"] * ZH + d["z"] // ZL) * CORE + d["c"]) * X + d["x"]) * ZL + d["z"] % ZL

        pairs.append((flat(at), flat(to)))
    return pairs


def around(axes, by, mirror):
    def move(d):
        axis = axes[d["c"]]
        d[axis] = (d[axis] + (-by if mirror and d["c"] else by)) % 4
        return d

    return permutation(move)


def other_core(d):
    d["c"] = 1 - d["c"]
    return d


def other_low(d):
    d["z"] = d["z"] ^ 1
    return d


def other_high(d):
    d["z"] = d["z"] ^ 2
    return d


def send(array, pairs):
    return lax.ppermute(array, AXES, pairs)


def swap_cores(array):
    return send(array, permutation(other_core))


def swap_low(array):
    return send(array, permutation(other_low))


def swap_high(array):
    return send(array, permutation(other_high))


def here():
    aux, row = lax.axis_index("aux"), lax.axis_index("row")
    return aux % CORE, row, row // ZL, row % ZL


def place_parts(main0, main1, rest, at_two, at_z, held, sems):
    core = here()[0]
    copies = []
    for a in range(4):
        y, x = jnp.where(core == 0, at_two, a), jnp.where(core == 0, a, at_two)
        for c, main in enumerate((main0, main1)):
            copies.append((main.at[:, :, a], held.at[y, :, c, x, :, pl.ds(0, MAIN)]))
        for b in range(4):
            y, x = jnp.where(core == 0, b, a), jnp.where(core == 0, a, b)
            into = held.at[y, at_z // ZL, :, x, at_z % ZL, pl.ds(MAIN, OWN - MAIN)]
            copies.append((rest.at[:, a, b], into))
    return [pltpu.make_async_copy(*copy, sems.at[i]) for i, copy in enumerate(copies)]


def positions():
    aux = lax.axis_index("aux")
    core, _, x, zl = here()
    y, z = aux // (ZH * CORE), aux // CORE % ZH * ZL + zl
    return jnp.where(core == 0, y, x), z, 1 - 2 * core


def near_kernel(*refs):
    parts, held, sems = refs[:9], refs[9], refs[10]
    at_two, z, sign = positions()
    copies = []
    for k, (two, along) in enumerate(((0, 0), (3, 4 - sign), (1, 4 + sign))):
        where = ((at_two + two) % 4, (z + along) % 4)
        copies += place_parts(*parts[3 * k : 3 * k + 3], *where, held, sems.at[k])
    for copy in copies:
        copy.start()
    for copy in copies:
        copy.wait()


def far_kernel(main0, main1, rest, near, held, slab, sems):
    at_two, z, _ = positions()
    row = here()[1]
    copies = place_parts(main0, main1, rest, (at_two + 2) % 4, (z + 2) % 4, held, sems)
    for copy in copies:
        copy.start()
    for copy in copies:
        copy.wait()
    copy = pltpu.make_async_copy(held.at[row // ZL, row % ZL], slab, sems.at[PARTS])
    copy.start()
    copy.wait()


def panels_and_slab(near, far):
    anywhere = pl.BlockSpec(memory_space=pl.ANY)
    held = jax.ShapeDtypeStruct((Y, ZH, CORE, X, ZL, OWN, WIDE), bf16)
    panels = pl.pallas_call(
        near_kernel,
        out_shape=held,
        in_specs=[anywhere] * 9,
        out_specs=anywhere,
        scratch_shapes=[pltpu.SemaphoreType.DMA((3, PARTS))],
        compiler_params=pltpu.CompilerParams(vmem_limit_bytes=4 * 1024 * 1024),
        name="near",
    )(*near)
    return pl.pallas_call(
        far_kernel,
        out_shape=[held, jax.ShapeDtypeStruct((CORE, X, ZL, OWN, WIDE), bf16)],
        in_specs=[anywhere] * 4,
        out_specs=[anywhere] * 2,
        input_output_aliases={3: 0},
        scratch_shapes=[pltpu.SemaphoreType.DMA((PARTS + 1,))],
        compiler_params=pltpu.CompilerParams(vmem_limit_bytes=4 * 1024 * 1024),
        name="far",
    )(*far, panels)


def plan_kernel(meta, steps, order, counts):
    for q in range(2):

        def clear(i, carry):
            counts[i] = 0
            return carry

        lax.fori_loop(0, ROW_BLOCKS, clear, 0)

        def put(s, carry):
            group = meta[q, s]
            n = counts[group]
            order[group, n] = s
            counts[group] = n + 1
            return carry

        lax.fori_loop(0, meta[q, 2 * SLOTS], put, 0)

        def list_group(group, base):
            n = counts[group]
            for i in range(STEP):
                order[group, n + i] = SLOTS
            many = (n + STEP - 1) // STEP

            def list_step(i, carry):
                at = (base + i) * FIELDS
                steps[q, at] = group
                for k in range(STEP):
                    s = order[group, i * STEP + k]
                    steps[q, at + 1 + k] = s
                    steps[q, at + 1 + STEP + k] = jnp.where(s < SLOTS, meta[q, SLOTS + s], 0)
                return carry

            lax.fori_loop(0, many, list_step, 0)
            return base + many

        many = lax.fori_loop(0, ROW_BLOCKS, list_group, 0)
        for u in range(UNROLL - 1):
            at = (many + u) * FIELDS
            steps[q, at] = ROW_BLOCKS
            for k in range(STEP):
                steps[q, at + 1 + k] = SLOTS
                steps[q, at + 1 + STEP + k] = 0
        steps[q, MOST * FIELDS] = many


def plan(meta):
    smem = pl.BlockSpec(memory_space=pltpu.SMEM)
    return pl.pallas_call(
        plan_kernel,
        out_shape=jax.ShapeDtypeStruct((2, MOST * FIELDS + 1), jnp.int32),
        in_specs=[smem],
        out_specs=smem,
        scratch_shapes=[
            pltpu.SMEM((ROW_BLOCKS, SLOTS + 2 * STEP), jnp.int32),
            pltpu.SMEM((ROW_BLOCKS,), jnp.int32),
        ],
        compiler_params=pltpu.CompilerParams(vmem_limit_bytes=2**20),
        cost_estimate=pl.CostEstimate(flops=2**31, bytes_accessed=2**12, transcendentals=0),
        name="plan",
    )(meta)


def multiply_kernel(q, steps, factors, held, out, total):
    total[...] = jnp.zeros_like(total)
    many = steps[q, MOST * FIELDS]
    panels = held.reshape(NB, WIDE)

    def some(i, carry):
        products = []
        for u in range(UNROLL):
            left, right = [], []
            for k in range(STEP):
                slot = steps[q, (i * UNROLL + u) * FIELDS + 1 + k]
                block = factors[jnp.minimum(slot, SLOTS - 1)]
                left.append(jnp.where(slot < SLOTS, block, jnp.zeros_like(block)))
                column = steps[q, (i * UNROLL + u) * FIELDS + 1 + STEP + k]
                right.append(panels[pl.ds(pl.multiple_of(column * BLK, BLK), BLK), :])
            products.append(
                jnp.dot(jnp.concatenate(left, axis=1), jnp.concatenate(right, axis=0), preferred_element_type=f32)
            )
        for u in range(UNROLL):
            total[steps[q, (i * UNROLL + u) * FIELDS]] += products[u]
        return carry

    lax.fori_loop(0, (many + UNROLL - 1) // UNROLL, some, 0)
    for group in range(ROW_BLOCKS):
        out[group * BLK : (group + 1) * BLK, :] = total[group].astype(bf16)


def multiply(q, steps, factors, panels):
    vmem = pl.BlockSpec(memory_space=pltpu.VMEM)

    def kernel(*refs):
        multiply_kernel(q, *refs)

    return pl.pallas_call(
        kernel,
        out_shape=jax.ShapeDtypeStruct((ROWS, WIDE), bf16),
        in_specs=[pl.BlockSpec(memory_space=pltpu.SMEM), vmem, vmem],
        out_specs=vmem,
        scratch_shapes=[
            pltpu.VMEM((ROW_BLOCKS + 1, BLK, WIDE), f32),
        ],
        compiler_params=pltpu.CompilerParams(vmem_limit_bytes=24 * 1024 * 1024),
        cost_estimate=pl.CostEstimate(flops=96 * 2 * 128 * 128 * 896, bytes_accessed=2**23, transcendentals=0),
        name="multiply",
    )(steps, factors, panels)


def cross_kernel(starts, half, slab, theirs, *refs):
    outs, used, product = refs[:-2], refs[-2], refs[-1]
    core, row, _, _ = here()
    used[...] = jnp.where(core == 0, slab[...], theirs[...])
    product[...] = lax.dot_general(
        half[...], used[...], (((0,), (0,)), ((), ())), preferred_element_type=f32
    ).astype(bf16)
    value = jnp.sum(half[...].astype(f32) * theirs[...].astype(f32), keepdims=True)
    high = value.astype(bf16).astype(f32)
    middle = (value - high).astype(bf16).astype(f32)
    low = value - high - middle
    lane = lax.broadcasted_iota(jnp.int32, (16, WIDE), 1)
    line = lax.broadcasted_iota(jnp.int32, (16, WIDE), 0)
    coded = jnp.where(
        lane == 3 * row, high, jnp.where(lane == 3 * row + 1, middle, jnp.where(lane == 3 * row + 2, low, 0.0))
    )
    product[NOCC : NOCC + 16, :] = jnp.where(line == 0, coded, 0.0).astype(bf16)
    for out, start in zip(outs, starts()):
        n = out.shape[0]
        out[...] = product[pl.ds(pl.multiple_of(start * n, n), n), :]


def chunks_x():
    core, _, x, _ = here()
    return x, (x + 1 - 2 * core) % X, (x - 1 + 2 * core) % X, (x + 2) % X


def chunks_low():
    zl = here()[3]
    return zl, 1 - zl


def cross(starts, many, half, slab, theirs):
    def kernel(*refs):
        cross_kernel(starts, *refs)

    return pl.pallas_call(
        kernel,
        out_shape=[jax.ShapeDtypeStruct((CROSS // many, WIDE), bf16)] * many,
        in_specs=[pl.BlockSpec(memory_space=pltpu.VMEM)] * 3,
        out_specs=[pl.BlockSpec(memory_space=pltpu.VMEM)] * many,
        scratch_shapes=[pltpu.VMEM((ROWS, WIDE), bf16), pltpu.VMEM((WIDE, WIDE), bf16)],
        compiler_params=pltpu.CompilerParams(vmem_limit_bytes=30 * 1024 * 1024),
        cost_estimate=pl.CostEstimate(flops=2 * 768 * 896 * 896, bytes_accessed=2**23, transcendentals=0),
        name="cross",
    )(half, slab, theirs)


def sum_kernel(starts, many, *refs):
    arrays, outs, total = refs[:many], refs[many:-1], refs[-1]
    total[...] = sum(array[...].astype(f32) for array in arrays)
    for out, start in zip(outs, starts()):
        n = out.shape[0]
        out[...] = total[pl.ds(pl.multiple_of(start * n, n), n), :].astype(out.dtype)


def sum_chunks(starts, pieces, *arrays):
    n, width = arrays[0].shape
    own = jax.ShapeDtypeStruct((n // pieces, width), f32)
    sent = jax.ShapeDtypeStruct((n // pieces, width), bf16)

    def kernel(*refs):
        sum_kernel(starts, len(arrays), *refs)

    return pl.pallas_call(
        kernel,
        out_shape=[own] + [sent] * (pieces - 1),
        in_specs=[pl.BlockSpec(memory_space=pltpu.VMEM)] * len(arrays),
        out_specs=[pl.BlockSpec(memory_space=pltpu.VMEM)] * pieces,
        scratch_shapes=[pltpu.VMEM((n, width), f32)],
        compiler_params=pltpu.CompilerParams(vmem_limit_bytes=24 * 1024 * 1024),
        cost_estimate=pl.CostEstimate(flops=n * width, bytes_accessed=2**21, transcendentals=0),
        name="sum_chunks",
    )(*arrays)


def chunks_y():
    y, c = lax.axis_index("aux") // (ZH * CORE), here()[0]
    return y, (y + 1 - 2 * c) % Y, (y - 1 + 2 * c) % Y, (y + 2) % Y


def exchange_kernel(*refs):
    halves, parts, (keep, give, held, weights, turned, sems) = refs[:2], refs[2:8], refs[8:]
    core, _, _, _ = here()
    copies = [[pltpu.make_async_copy(halves[q], held.at[q], sems.at[6 + q])] for q in range(2)]
    for i, (q, at) in enumerate([(0, at) for at in chunks_low()] + [(1, at) for at in chunks_arrived()]):
        n = parts[i].shape[0]
        into = weights.at[q, pl.ds(pl.multiple_of(at * n, n), n), :]
        copies[q].append(pltpu.make_async_copy(parts[i], into, sems.at[i]))
    for copy in copies[0] + copies[1]:
        copy.start()
    exchanged = []
    for q in range(2):
        weights[q, CROSS:, :] = jnp.zeros((WIDE - CROSS, WIDE), bf16)
        for copy in copies[q]:
            copy.wait()
        exchanged.append(jnp.dot(held[q], weights[q], preferred_element_type=f32))
    line = lax.broadcasted_iota(jnp.int32, (16, WIDE), 0)
    total = None
    for q in range(2):
        codes = jnp.where(line == 0, weights[q, NOCC : NOCC + 16, :].astype(f32), 0.0)
        codes = codes + jnp.where(line == 1, weights[1 - q, NOCC : NOCC + 16, :].astype(f32), 0.0)
        coulomb = jnp.sum(codes, keepdims=True) * (1.0 / NB)
        factor = jnp.where(core == 0, 2.0 * coulomb, 0.0)
        term = factor * held[q].astype(f32) - exchanged[q]
        total = term if total is None else total + term
    turned[...] = total.T
    n = CROSS // 2
    keep[...] = turned[pl.ds(pl.multiple_of(core * n, n), n), :]
    give[...] = turned[pl.ds(pl.multiple_of((1 - core) * n, n), n), :]


def chunks_arrived():
    x, ahead, behind, far = chunks_x()
    return x, behind, ahead, far


def exchange(halves, low_parts, x_parts):
    return pl.pallas_call(
        exchange_kernel,
        out_shape=[jax.ShapeDtypeStruct((CROSS // 2, ROWS), f32)] * 2,
        in_specs=[pl.BlockSpec(memory_space=pl.ANY)] * 8,
        out_specs=[pl.BlockSpec(memory_space=pltpu.VMEM)] * 2,
        scratch_shapes=[
            pltpu.VMEM((2, ROWS, WIDE), bf16),
            pltpu.VMEM((2, WIDE, WIDE), bf16),
            pltpu.VMEM((WIDE, ROWS), f32),
            pltpu.SemaphoreType.DMA((8,)),
        ],
        compiler_params=pltpu.CompilerParams(vmem_limit_bytes=48 * 1024 * 1024),
        cost_estimate=pl.CostEstimate(flops=4 * 768 * 896 * 896, bytes_accessed=2**23, transcendentals=0),
        name="exchange",
    )(*halves, *low_parts, *x_parts)


def widen_kernel(own, others, out, wide, sems):
    core, n = here()[0], CROSS // 4
    copies = []
    for i in range(4):
        low, high = i * n, min((i + 1) * n, NOCC)
        rows = slice(low % (2 * n), low % (2 * n) + high - low)
        mine, its = (own, others) if i < 2 else (others, own)
        wide[low:high, :] = jnp.where(core == 0, mine[rows, :], its[rows, :]).astype(f32)
        at = pl.ds(low, high - low)
        copies.append(pltpu.make_async_copy(wide.at[at], out.at[at], sems.at[i]))
        copies[-1].start()
    for copy in copies:
        copy.wait()


def widen(own, others):
    return pl.pallas_call(
        widen_kernel,
        out_shape=jax.ShapeDtypeStruct((NOCC, ROWS), f32),
        in_specs=[pl.BlockSpec(memory_space=pltpu.VMEM)] * 2,
        out_specs=pl.BlockSpec(memory_space=pl.ANY),
        scratch_shapes=[pltpu.VMEM((NOCC, ROWS), f32), pltpu.SemaphoreType.DMA((4,))],
        compiler_params=pltpu.CompilerParams(vmem_limit_bytes=16 * 1024 * 1024),
        name="widen",
    )(own, others)


def local(factors, block_rows, block_cols, block_count, orbitals, response):
    aux, row = lax.axis_index("aux"), lax.axis_index("row")
    y, zh, c = aux // (ZH * CORE), (aux // CORE) % ZH, aux % CORE
    x, zl = row // ZL, row % ZL
    z = zh * ZL + zl
    sign = 1 - 2 * c
    first = c == 0

    def choose(a, b):
        return jnp.where(first, a, b)

    def send_after(array, pairs, *earlier):
        return send(lax.optimization_barrier((array, *earlier))[0], pairs)

    def put(into, array, **at):
        index = [jnp.int32(0)] * into.ndim
        for dim, i in at.items():
            index[int(dim[1:])] = i
        return lax.dynamic_update_slice(into, array, index)

    got = send(choose(response, orbitals), permutation(other_core))
    own_blocks = factors[0]
    other_blocks = send_after(own_blocks, permutation(other_core), got)
    both = jnp.stack([choose(orbitals, got), choose(got, response)])
    both = jnp.pad(both, ((0, 0), (0, 0), (0, WIDE - NOCC)))

    one, two = ("x", "y"), ("y", "x")
    at_one, at_two = choose(x, y), choose(y, x)
    shape = (CORE, 4, OWN, WIDE)
    stage = put(jnp.zeros(shape, bf16), both[:, None], d1=at_one)
    ahead = send(both, around(one, 1, False))
    behind = send(both, around(one, -1, False))
    far = send(both, around(one, 2, False))
    stage = put(stage, ahead[:, None], d1=(at_one - 1) % 4)
    stage = put(stage, behind[:, None], d1=(at_one + 1) % 4)
    stage = put(stage, far[:, None], d1=(at_one + 2) % 4)
    stage, other_blocks = lax.optimization_barrier((stage, other_blocks))

    main, rest = stage[:, :, :MAIN], stage[:, :, MAIN:]
    zz = ("z", "z")
    main_ahead = send(main, around(zz, 1, True))
    main_far = send(main_ahead, around(zz, 1, True))
    main_behind = send_after(main, around(zz, -1, True), main_ahead)
    lists = lax.optimization_barrier((block_rows[0], block_cols[0], block_count[0], ahead))
    lists = jnp.concatenate([lists[0] % ROW_BLOCKS, lists[1], lists[2]])
    lists = jnp.pad(lists, (0, 256 - 2 * SLOTS - 1))[None]
    meta = jnp.concatenate([lists, send_after(lists, permutation(other_core), main_ahead)])
    rest, meta = lax.optimization_barrier((rest, meta))
    rest_ahead = send(rest, around(two, 1, False))
    rest_behind = send(rest, around(two, -1, False))
    rest_far = send(rest, around(two, 2, False))

    mains = [jnp.zeros((ZH, ZL, 4, MAIN, WIDE), bf16)] * 2
    for array, at in (
        (main, z),
        (main_ahead, (z - sign) % 4),
        (main_behind, (z + sign) % 4),
        (main_far, (z + 2) % 4),
    ):
        mains = [put(into, array[i][None, None], d0=at // ZL, d1=at % ZL) for i, into in enumerate(mains)]
    into = jnp.zeros((CORE, 4, 4, OWN - MAIN, WIDE), bf16)
    for array, at in (
        (rest, at_two),
        (rest_ahead, (at_two - 1) % 4),
        (rest_behind, (at_two + 1) % 4),
        (rest_far, (at_two + 2) % 4),
    ):
        into = put(into, array[:, :, None], d2=at)
    rest = into

    ahead, behind = around(two, 1, False), around(two, -1, False)
    mains, rest = lax.optimization_barrier((mains, rest))
    ahead_0 = send(mains[0], ahead)
    behind_1 = send(mains[1], behind)
    rest_ahead = send(rest, around(zz, 1, True))
    rest_behind = send(rest, around(zz, -1, True))
    steps = plan(meta)
    ahead_1 = send_after(mains[1], ahead, ahead_0, steps)
    behind_0 = send_after(mains[0], behind, behind_1, steps)
    far_0 = send(ahead_0, ahead)
    far_1 = send_after(behind_1, behind, rest_ahead)
    rest_far = send_after(rest_ahead, around(zz, 1, True), rest_behind)
    near = [mains[0], mains[1], rest, ahead_0, ahead_1, rest_ahead, behind_0, behind_1, rest_behind]
    panels, slab = panels_and_slab(near, (far_0, far_1, rest_far))
    slab = slab.reshape(ROWS, WIDE)
    theirs = swap_cores(slab)
    second_half = multiply(1, steps, other_blocks, panels)

    def add(*arrays):
        return sum(a.astype(f32) for a in arrays)

    xx = ("x", "x")
    ahead, behind = around(xx, 1, True), around(xx, -1, True)
    opposite = around(xx, 2, True)
    half_mine, to_low = cross(chunks_low, 2, second_half, slab, theirs)
    from_low = swap_low(to_low)
    panels, half_mine = lax.optimization_barrier((panels, half_mine))
    first_half = multiply(0, steps, own_blocks, panels)
    mine, to_ahead, to_behind, to_far = cross(chunks_x, 4, first_half, slab, theirs)
    parts = (mine, send(to_ahead, ahead), send(to_behind, behind), send(to_far, opposite))
    own, *sent = sum_chunks(chunks_x, 4, half_mine, from_low)
    second = (own, send(sent[0], ahead), send(sent[1], behind), send(sent[2], opposite))
    parts, _ = lax.optimization_barrier((parts, second[1]))
    own, sent = sum_chunks(chunks_low, 2, *parts)
    first_shard = add(own, swap_low(sent))
    second_shard = add(*second)

    last = (x == X - 1) & (zl == ZL - 1)
    at = jnp.arange(SHARD, dtype=jnp.int32)[:, None] + (CROSS - SHARD)

    def weights_of(shard):
        own = jnp.where(last & (at == NOCC), shard, shard * (1.0 / NB)).astype(bf16)
        return jnp.where(last & (at == NOCC + 1), own[NOCC - (CROSS - SHARD)][None], swap_cores(own))

    def parts_x(array):
        return array, send(array, ahead), send(array, behind), send(array, opposite)

    def joined(parts, places):
        n = parts[0].shape[0]
        into = jnp.zeros((n * len(parts), WIDE), bf16)
        for part, k in zip(parts, places):
            into = lax.dynamic_update_slice(into, part, ((k % len(parts)) * n, 0))
        return into

    array = weights_of(first_shard)
    from_low = swap_low(array)
    by_x = joined((array, from_low), (zl, 1 - zl))
    by_low = joined(parts_x(weights_of(second_shard)), (x, x - sign, x + sign, x + 2))
    by_low, by_x = lax.optimization_barrier((by_low, by_x))
    keep, give = exchange((first_half, second_half), (by_low, swap_low(by_low)), parts_x(by_x))

    yy = ("y", "y")
    ahead, behind, opposite = around(yy, 1, True), around(yy, -1, True), around(yy, 2, True)
    own, *sent = sum_chunks(chunks_y, 4, keep, swap_cores(give))
    part = own + add(send(sent[0], ahead), send(sent[1], behind), send(sent[2], opposite))
    part = (part + swap_high(part)).astype(bf16)
    into = jnp.zeros((CROSS // 2, ROWS), bf16)
    for k, array in (
        (y, part),
        (y - sign, send(part, ahead)),
        (y + sign, send(part, behind)),
        (y + 2, send(part, opposite)),
    ):
        into = lax.dynamic_update_slice(into, array, ((k % Y) * SHARD, 0))
    return widen(into, swap_cores(into)).T


def solution(mesh):
    in_specs = (
        P("aux", "row", None, None),
        P("aux", "row"),
        P("aux", "row"),
        P("aux", "row"),
        P(("aux", "row"), None),
        P(("aux", "row"), None),
    )
    out_specs = P("row", None)
    return jax.shard_map(local, mesh=mesh, in_specs=in_specs, out_specs=out_specs, check_vma=False)
```
